512 devices in a mesh: gx: 32 (over y_hi, z), gy: 4 (over x), gz: 4 (over y_lo, core).
Axes of the slice: x: 4, y: 4 (y_hi: 2, y_lo: 2; y = y_hi * 2 + y_lo), z: 16, core: 2. Of those that a mesh axis runs over, the one named last changes fastest.
Arguments:
- fields: float32 [12, 256, 32, 512], P(None, 'gx', 'gy', 'gz'), as said below
- reacting: int32 [256, 32, 512], P('gx', 'gy', 'gz'), may hold values from 0 to 1, as said below
- panel_map: int32 [2, 256, 512], P(None, 'gx', 'gz'), may hold values from 0 to 4095, as said below
- layer_one: bfloat16 [1600, 12], replicated, may hold values from -4 to 4
- layer_two: bfloat16 [800, 1600], replicated, may hold values from -0.21875 to 0.21875
- layer_three: bfloat16 [400, 800], replicated, may hold values from -0.3125 to 0.3125
- layer_four: bfloat16 [12, 400], replicated, may hold values from -0.3125 to 0.3125
Outputs:
- new_fields: float32 [12, 256, 32, 512], P(None, 'gx', 'gy', 'gz')
- impulse: float32 [4096], P(('gx', 'gy', 'gz'))
The draws below stay inside these ranges and needn't reach their ends.
Inputs may be any that keep to these rules, and one draw needn't show every extreme that they name: `fields`: component 0 (density) lies between 0.3 and 3.3; the velocities (components 1 to 3 over component 0) between -1.2 and 1.2; the pressure 0.4 (component 4 - |momentum|^2 / (2 density)) between 0.3 and 5; components 5 to 11 are 0.01 to 0.14 times component 0. Each device's aligned block of 8 x 8 x 128 cells holds at most 256 reacting cells. The blocks that share their ranges along the second and third dimensions hold exactly 64 reacting cells each on average, and one in eight of them, and at least one, hold exactly 256. `panel_map`: every panel is a patch of 8 x 8 cells of one wall, shifted by 4 cells along the first dimension and closed around it; panels are numbered in a random order and each number is used once.
All inputs are finite; a program needn't handle non-finite values.
Results may differ from the reference program's by a relative error of at most 0.0014.
Values may be sent and summed in bfloat16 or wider, within the bound.
A program may use at most 64 MiB of HBM per device.

```python
import math
import jax
import jax.numpy as jnp
from jax import lax

CX = 8
CY = 8
CZ = 128
BAL = 64
COMPS = 12
H1 = 1600
H2 = 800
H3 = 400
PATCH = 8
NX = 256
NY = 32
NZ = 512
REACTING = 32768
PANELS = 4096


HEAT_RATIO = 1.4


def draw_fields(key, part):
    sub_keys = jax.random.split(key, 4)
    shape_grid = (NX, NY, NZ)
    log_density = jax.random.uniform(sub_keys[0], shape_grid, jnp.float32, math.log(0.5), math.log(2.0))
    log_pressure = jax.random.uniform(sub_keys[1], shape_grid, jnp.float32, math.log(0.5), math.log(3.0))
    fractions = jax.random.uniform(sub_keys[3], (COMPS - 5,) + shape_grid, jnp.float32, 0.01, 0.14)
    velocity = jnp.clip(0.4 * jax.random.normal(sub_keys[2], (3,) + shape_grid, jnp.float32), -1.2, 1.2)
    density = jnp.exp(log_density)
    pressure = jnp.exp(log_pressure)
    energy = pressure / (HEAT_RATIO - 1.0) + 0.5 * density * jnp.sum(velocity * velocity, axis=0)
    return jnp.concatenate([density[None], density[None] * velocity, energy[None], density[None] * fractions], axis=0).astype(jnp.float32)


def draw_reacting(key, part):
    gx_count = NX // CX
    gy_count = NY // CY
    gz_count = NZ // CZ
    capacity = BAL * min(4, gx_count)
    hot_count = max(gx_count // 8, 1)
    cold_count = gx_count - hot_count
    rest_rows = gx_count * BAL - hot_count * capacity
    base_rows = rest_rows // cold_count
    extra_rows = rest_rows % cold_count
    groups = gy_count * gz_count
    sub_keys = jax.random.split(key, 3)
    ranks = jnp.arange(gx_count, dtype=jnp.int32)
    cold_rank = ranks - hot_count
    pair_index = jnp.maximum(cold_rank, 0) // 2
    sign_pair = jnp.where(cold_rank % 2 == 0, 1, -1) * jnp.where((cold_rank == cold_count - 1) & (cold_count % 2 == 1), 0, 1)
    pair_shift = jax.random.randint(sub_keys[0], (groups, gx_count // 2 + 1), 0, base_rows // 2 + 1, dtype=jnp.int32)
    cold_rows = base_rows + (cold_rank < extra_rows).astype(jnp.int32)[None, :] + sign_pair[None, :] * pair_shift[:, pair_index]
    by_rank = jnp.where(ranks[None, :] < hot_count, capacity, cold_rows).astype(jnp.int32)
    orders = jax.vmap(lambda sub_key: jax.random.permutation(sub_key, gx_count))(jax.random.split(sub_keys[1], groups))
    by_device = jnp.zeros((groups, gx_count), jnp.int32).at[jnp.arange(groups)[:, None], orders].set(by_rank)
    cell_count = CX * CY * CZ
    cell_order = jax.vmap(lambda sub_key: jax.random.permutation(sub_key, cell_count))(jax.random.split(sub_keys[2], groups * gx_count))
    cell_order = cell_order.reshape(groups, gx_count, cell_count)
    react_flags = (cell_order < by_device[:, :, None]).astype(jnp.int32)
    blocks = react_flags.reshape(gy_count, gz_count, gx_count, CX, CY, CZ)
    return blocks.transpose(2, 3, 0, 4, 1, 5).reshape(NX, NY, NZ)


def draw_panel_map(key, part):
    across = NX // PATCH
    along = NZ // PATCH
    panel_total = 2 * across * along
    shuffle = jax.random.permutation(key, panel_total)
    wall_side = jnp.arange(2, dtype=jnp.int32)[:, None, None]
    x_cells = jnp.arange(NX, dtype=jnp.int32)[None, :, None]
    z_cells = jnp.arange(NZ, dtype=jnp.int32)[None, None, :]
    patch_index = wall_side * across * along + (x_cells + PATCH // 2) // PATCH % across * along + z_cells // PATCH
    return shuffle[patch_index].astype(jnp.int32)


def bell_draw(key, dims, width, bound, held_as=jnp.bfloat16):
    array = width * jax.random.normal(key, dims, jnp.float32)
    return jnp.clip(array, min=-bound, max=bound).astype(held_as)


def setup_inputs(seed: int = 0) -> dict:
    arg_keys = jax.random.split(jax.random.key(seed), 8)
    fields = draw_fields(jax.random.fold_in(arg_keys[7], 71), 0)
    reacting = draw_reacting(jax.random.fold_in(arg_keys[7], 71), 0)
    panel_map = draw_panel_map(jax.random.fold_in(arg_keys[7], 71), 0)
    layer_one = bell_draw(arg_keys[3], (H1, COMPS), 1.0, 4.0)
    layer_two = bell_draw(arg_keys[4], (H2, H1), (H1 // 2) ** -0.5, 0.21875)
    layer_three = bell_draw(arg_keys[5], (H3, H2), (H2 // 2) ** -0.5, 0.3125)
    layer_four = bell_draw(arg_keys[6], (COMPS, H3), H3 ** -0.5, 0.3125)
    return dict(fields=fields, reacting=reacting, panel_map=panel_map, layer_one=layer_one, layer_two=layer_two, layer_three=layer_three, layer_four=layer_four)


HEAT_RATIO = 1.4
TIME_STEP = 0.1
CHEM_STEP = 0.25
WENO_EPS = 1e-06

def take_slab(array_in, begin_at, length_of, flux_axis):
    return lax.slice_in_dim(array_in, begin_at, begin_at + length_of, axis=flux_axis)

def weno_face(upwind_two, upwind_one, center, downwind_one, downwind_two):
    cand_zero = (2.0 * upwind_two - 7.0 * upwind_one + 11.0 * center) / 6.0
    cand_one = (-upwind_one + 5.0 * center + 2.0 * downwind_one) / 6.0
    cand_two = (2.0 * center + 5.0 * downwind_one - downwind_two) / 6.0
    smooth_zero = 13.0 / 12.0 * (upwind_two - 2.0 * upwind_one + center) ** 2 + 0.25 * (upwind_two - 4.0 * upwind_one + 3.0 * center) ** 2
    smooth_one = 13.0 / 12.0 * (upwind_one - 2.0 * center + downwind_one) ** 2 + 0.25 * (upwind_one - downwind_one) ** 2
    smooth_two = 13.0 / 12.0 * (center - 2.0 * downwind_one + downwind_two) ** 2 + 0.25 * (3.0 * center - 4.0 * downwind_one + downwind_two) ** 2
    weight_zero = 0.1 / (WENO_EPS + smooth_zero) ** 2
    weight_one = 0.6 / (WENO_EPS + smooth_one) ** 2
    weight_two = 0.3 / (WENO_EPS + smooth_two) ** 2
    weight_sum = weight_zero + weight_one + weight_two
    return (weight_zero * cand_zero + weight_one * cand_one + weight_two * cand_two) / weight_sum

def to_recon(fields):
    density = fields[0]
    velocity = fields[1:4] / density[None]
    pressure = (HEAT_RATIO - 1.0) * (fields[4] - 0.5 * density * lax.optimization_barrier(jnp.sum(velocity * velocity, axis=0)))
    fractions = fields[5:] / density[None]
    return jnp.concatenate([jnp.log(density)[None], velocity, jnp.log(pressure)[None], fractions], axis=0)

def normal_of(normal, ndims):
    return (jnp.arange(3) == normal).reshape((3,) + (1,) * (ndims - 1))

def side_terms(recon, normal):
    density = jnp.exp(recon[0])
    velocity = recon[1:4]
    pressure = jnp.exp(recon[4])
    fractions = recon[5:]
    speed_n = velocity[normal]
    energy = pressure / (HEAT_RATIO - 1.0) + 0.5 * density * lax.optimization_barrier(jnp.sum(velocity * velocity, axis=0))
    conserved = jnp.concatenate([density[None], density[None] * velocity, energy[None], density[None] * fractions], axis=0)
    mass_flux = density * speed_n
    normal_mask = normal_of(normal, recon.ndim)
    momentum_flux = mass_flux[None] * velocity + jnp.where(normal_mask, pressure[None], 0.0)
    flux_terms = jnp.concatenate([mass_flux[None], momentum_flux, ((energy + pressure) * speed_n)[None], mass_flux[None] * fractions], axis=0)
    sound_speed = jnp.sqrt(HEAT_RATIO * pressure / density)
    return (density, velocity, pressure, fractions, energy, conserved, flux_terms, speed_n, sound_speed)

def star_state(density, velocity, pressure, fractions, energy, speed_n, wave_speed, contact, normal_mask):
    relative = wave_speed - speed_n
    factor = density * relative / (wave_speed - contact)
    star_velocity = jnp.where(normal_mask, contact[None], velocity)
    star_energy = energy / density + (contact - speed_n) * (contact + pressure / (density * relative))
    return jnp.concatenate([factor[None], factor[None] * star_velocity, (factor * star_energy)[None], factor[None] * fractions], axis=0)

def hllc_flux(left_recon, right_recon, normal):
    left_density, left_velocity, left_pressure, left_fractions, left_energy, left_cons, left_flux, left_speed, left_sound = side_terms(left_recon, normal)
    right_density, right_velocity, right_pressure, right_fractions, right_energy, right_cons, right_flux, right_speed, right_sound = side_terms(right_recon, normal)
    wave_left = jnp.minimum(left_speed - left_sound, right_speed - right_sound)
    wave_right = jnp.maximum(left_speed + left_sound, right_speed + right_sound)
    left_rel = wave_left - left_speed
    right_rel = wave_right - right_speed
    contact = (right_pressure - left_pressure + left_density * left_speed * left_rel - right_density * right_speed * right_rel) / (left_density * left_rel - right_density * right_rel)
    normal_mask = normal_of(normal, left_recon.ndim)
    star_left = star_state(left_density, left_velocity, left_pressure, left_fractions, left_energy, left_speed, wave_left, contact, normal_mask)
    star_right = star_state(right_density, right_velocity, right_pressure, right_fractions, right_energy, right_speed, wave_right, contact, normal_mask)
    left_star_flux = left_flux + wave_left[None] * (star_left - left_cons)
    right_star_flux = right_flux + wave_right[None] * (star_right - right_cons)
    return jnp.where(wave_left[None] >= 0, left_flux, jnp.where(contact[None] >= 0, left_star_flux, jnp.where(wave_right[None] > 0, right_star_flux, right_flux)))

def face_flux(padded, normal):
    flux_axis = normal + 1
    face_count = padded.shape[flux_axis] - 5
    stencil = [take_slab(padded, offset, face_count, flux_axis) for offset in range(6)]
    left_state = weno_face(stencil[0], stencil[1], stencil[2], stencil[3], stencil[4])
    right_state = weno_face(stencil[5], stencil[4], stencil[3], stencil[2], stencil[1])
    return hllc_flux(left_state, right_state, normal)

def mirror_walls(padded, normal, at_first, at_last):
    flux_axis = normal + 1
    cell_count = padded.shape[flux_axis] - 6
    flip_sign = jnp.where(jnp.arange(padded.shape[0]) == 1 + normal, -1.0, 1.0).astype(padded.dtype).reshape((-1, 1, 1, 1))
    ghost_low = jnp.flip(take_slab(padded, 3, 3, flux_axis), flux_axis) * flip_sign
    ghost_high = jnp.flip(take_slab(padded, cell_count, 3, flux_axis), flux_axis) * flip_sign
    low_side = jnp.where(at_first, ghost_low, take_slab(padded, 0, 3, flux_axis))
    high_side = jnp.where(at_last, ghost_high, take_slab(padded, cell_count + 3, 3, flux_axis))
    return jnp.concatenate([low_side, take_slab(padded, 3, cell_count, flux_axis), high_side], axis=flux_axis)

def chem_rates(features, layer_one, layer_two, layer_three, layer_four):
    hidden_one = jax.nn.gelu(jnp.dot(layer_one, features, preferred_element_type=jnp.float32)).astype(jnp.bfloat16)
    hidden_two = jax.nn.gelu(jnp.dot(layer_two, hidden_one, preferred_element_type=jnp.float32)).astype(jnp.bfloat16)
    hidden_three = jax.nn.gelu(jnp.dot(layer_three, hidden_two, preferred_element_type=jnp.float32)).astype(jnp.bfloat16)
    return jnp.dot(layer_four, hidden_three, preferred_element_type=jnp.float32).astype(jnp.bfloat16)

def reference(fields, reacting, panel_map, layer_one, layer_two, layer_three, layer_four):
    recon_fields = to_recon(fields)
    update = jnp.zeros_like(fields)
    wall_faces = None
    for normal in range(3):
        widths = [(0, 0)] * 4
        widths[normal + 1] = (3, 3)
        padded = mirror_walls(jnp.pad(recon_fields, widths), normal, True, True)
        split_axis = 3 if normal == 0 else 1
        extent = padded.shape[split_axis]
        pieces = math.gcd(extent, 64)
        blocked = jnp.moveaxis(padded, split_axis, 0)
        blocked = blocked.reshape((pieces, extent // pieces) + blocked.shape[1:])

        def one_block(one_piece):
            local_block = jnp.moveaxis(one_piece, 0, split_axis)
            face_fluxes = face_flux(local_block, normal)
            cell_count = face_fluxes.shape[normal + 1] - 1
            change = take_slab(face_fluxes, 1, cell_count, normal + 1) - take_slab(face_fluxes, 0, cell_count, normal + 1)
            edge_faces = jnp.concatenate([take_slab(face_fluxes, 0, 1, normal + 1), take_slab(face_fluxes, cell_count, 1, normal + 1)], axis=normal + 1)
            return (jnp.moveaxis(change, split_axis, 0), jnp.moveaxis(edge_faces, split_axis, 0))
        changes, edges_all = lax.map(one_block, blocked)
        change = jnp.moveaxis(changes.reshape((extent,) + changes.shape[2:]), 0, split_axis)
        update = update + change
        if normal == 1:
            wall_faces = jnp.moveaxis(edges_all.reshape((extent,) + edges_all.shape[2:]), 0, split_axis)
    cell_total = reacting.size
    flat_recon = recon_fields.reshape(COMPS, cell_total)
    where_rows = jnp.nonzero(reacting.reshape(cell_total), size=REACTING)[0].astype(jnp.int32)
    features = flat_recon[:, where_rows].astype(jnp.bfloat16)
    block_rows = math.gcd(REACTING, 4096)
    block_count = REACTING // block_rows
    feature_blocks = jnp.moveaxis(features.reshape(COMPS, block_count, block_rows), 1, 0)
    rate_blocks = lax.map(lambda row_block: chem_rates(row_block, layer_one, layer_two, layer_three, layer_four), feature_blocks)
    rate_rows = jnp.moveaxis(rate_blocks, 0, 1).reshape(COMPS, REACTING)
    source = jnp.zeros((COMPS, cell_total), jnp.float32).at[:, where_rows].add(rate_rows.astype(jnp.float32))
    new_fields = fields - TIME_STEP * update + CHEM_STEP * source.reshape(fields.shape)
    wall_push = jnp.moveaxis(wall_faces[2], 1, 0)
    impulse = jax.ops.segment_sum(wall_push.reshape(-1), panel_map.reshape(-1), num_segments=PANELS) / float(PATCH * PATCH)
    return (new_fields, impulse)
```

```python
import functools
import math

import jax
import jax.numpy as jnp
from jax import lax
from jax.experimental import pallas as pl
from jax.experimental.pallas import tpu as pltpu
from jax.sharding import PartitionSpec as P

COMPS = 12
CX = 8
CY = 8
CZ = 128
ROWS = CX * CY
HALF = CZ // 2
CAP = 256
H1 = 1600
H2 = 800
H3 = 400
PATCH = 8
LANES = 128

TIME_STEP = 0.1
CHEM_STEP = 0.25
WENO_EPS = 1e-06
ALPHA = math.sqrt(12.0 / 13.0)
EPS_SCALED = WENO_EPS * 12.0 / 13.0
LOG_HEAT_HALF = 0.5 * math.log(1.4)

MESH = pl.DeviceIdType.MESH
F32 = jnp.float32
BF16 = jnp.bfloat16


def recip(x):
    r = pl.reciprocal(x, approx=True)
    return r * (2.0 - x * r)


def weno_pair(v):
    count = v.shape[0]
    d = v[1:] - v[:-1]
    q = d[1:] - d[:-1]
    g = (q[1:] - q[:-1]) * (1.0 / 3.0)
    da = d * ALPHA
    ha = q * (0.5 * ALPHA)
    qq = q * q + EPS_SCALED
    m = count - 4
    f0 = da[1 : 1 + m] + ha[0:m]
    f1 = da[1 : 1 + m] + ha[1 : 1 + m]
    f2 = da[2 : 2 + m] - ha[2 : 2 + m]
    t0 = f0 * f0 + qq[0:m]
    t1 = f1 * f1 + qq[1 : 1 + m]
    t2 = f2 * f2 + qq[2 : 2 + m]
    a = t1 * t2
    b = t0 * t2
    c = t0 * t1
    a = a * a
    b = b * b * 6.0
    c = c * c
    u = a + c + b
    x = a * g[0:m]
    y = c * g[1 : 1 + m]
    center = v[2 : 2 + m] + q[1 : 1 + m] * (1.0 / 3.0)
    hd = d * 0.5
    n = m - 1
    low = slice(0, n)
    high = slice(1, m)
    left = (
        center[low]
        + hd[1 : 1 + n]
        - (x[low] + 1.5 * y[low]) * pl.reciprocal(u[low] + 2.0 * c[low], approx=True)
    )
    right = (
        center[high]
        - hd[3 : 3 + n]
        + (y[high] + 1.5 * x[high]) * pl.reciprocal(u[high] + 2.0 * a[high], approx=True)
    )
    return left, right


def hllc(left, right, normal, only_push=False):
    rl = jnp.exp(left[0])
    rr = jnp.exp(right[0])
    p_l = jnp.exp(left[4])
    p_r = jnp.exp(right[4])
    cl = jnp.exp(0.5 * (left[4] - left[0]) + LOG_HEAT_HALF)
    cr = jnp.exp(0.5 * (right[4] - right[0]) + LOG_HEAT_HALF)
    ul = left[1 + normal]
    ur = right[1 + normal]
    sl = jnp.minimum(ul - cl, ur - cr)
    sr = jnp.maximum(ul + cl, ur + cr)
    al = rl * (sl - ul)
    ar = rr * (sr - ur)
    s = (p_r - p_l + al * ul - ar * ur) * recip(al - ar)
    take_left = jnp.maximum(s, sl) >= 0.0

    def pick(i, j):
        return jnp.where(take_left, i, j)

    rho = pick(rl, rr)
    p = pick(p_l, p_r)
    sk = pick(sl, sr)
    a = pick(al, ar)
    beyond = pick(sl, -sr) >= 0.0
    un = pick(ul, ur)
    inv = recip(sk - s)
    pstar = p + a * (s - un)
    u_face = jnp.where(beyond, un, s)
    p_face = jnp.where(beyond, p, pstar)
    mass = jnp.where(beyond, rho, a * inv) * u_face
    push = mass * u_face + p_face
    if only_push:
        return push
    vel = [un if i == normal else pick(left[1 + i], right[1 + i]) for i in range(3)]
    energy = 2.5 * p + 0.5 * rho * (vel[0] * vel[0] + vel[1] * vel[1] + vel[2] * vel[2])
    estar = ((sk - un) * energy + pstar * s - p * un) * inv
    e_face = jnp.where(beyond, energy, estar)
    flux = [mass]
    for i in range(3):
        flux.append(push if i == normal else mass * vel[i])
    flux.append(u_face * (e_face + p_face))
    for i in range(5, COMPS):
        flux.append(mass * pick(left[i], right[i]))
    return flux


def gelu(x):
    k = math.sqrt(2.0 / math.pi)
    y = x * (x * x * (0.044715 * k) + k)
    h = 0.5 * x
    return h * jnp.tanh(y) + h


def dot_nt(a, b):
    return lax.dot_general(a, b, (((1,), (1,)), ((), ())), preferred_element_type=F32)


def dot_tn(a, b):
    return lax.dot_general(a, b, (((0,), (0,)), ((), ())), preferred_element_type=F32)


def iota(shape, dim):
    return lax.broadcasted_iota(jnp.int32, shape, dim)


def one_where(mask):
    return jnp.where(mask, 1.0, 0.0)


def kernel(
    sizes,
    fields_hbm,
    react_hbm,
    pmap_hbm,
    w1_hbm,
    w2_hbm,
    w3_hbm,
    w4_hbm,
    out_ref,
    imp_ref,
    fields,
    react,
    pmap,
    w1,
    w2,
    w3,
    w4,
    rec,
    ybuf,
    zbuf,
    xlo,
    xhi,
    ylo,
    yhi,
    zlo,
    zhi,
    st_l,
    st_r,
    flux_x,
    flux_y,
    flux_z,
    turn_y,
    turn_z,
    hid1,
    hid2,
    source,
    contrib,
    rows1,
    parts,
    own,
    load_sem,
    send_sem,
    recv_sem,
    s1_send,
    s1_recv,
    s2_send,
    s2_recv,
):
    nx, ny, nz = sizes
    gx = lax.axis_index("gx")
    gy = lax.axis_index("gy")
    gz = lax.axis_index("gz")
    is_wall = (gy == 0) | (gy == ny - 1)
    group = ny * nz
    me = gy * nz + gz
    walls = 2 * nz

    loads = []
    for i, (src, dst) in enumerate(
        (
            (fields_hbm, fields),
            (react_hbm, react),
            (pmap_hbm, pmap),
            (w1_hbm, w1),
            (w2_hbm, w2),
            (w3_hbm, w3),
            (w4_hbm, w4),
        )
    ):
        copy = pltpu.make_async_copy(src, dst, load_sem.at[i])
        copy.start()
        loads.append(copy)

    barrier = pltpu.get_barrier_semaphore()
    around = {
        "xlo": {"gx": lax.rem(gx + nx - 1, nx)},
        "xhi": {"gx": lax.rem(gx + 1, nx)},
        "ylo": {"gy": lax.rem(gy + ny - 1, ny)},
        "yhi": {"gy": lax.rem(gy + 1, ny)},
        "zlo": {"gz": lax.rem(gz + nz - 1, nz)},
        "zhi": {"gz": lax.rem(gz + 1, nz)},
    }
    for where in around.values():
        pl.semaphore_signal(barrier, inc=1, device_id=where, device_id_type=MESH)

    def greet_wall(w, carry):
        to_y = (w // nz) * (ny - 1)
        to_z = lax.rem(w, nz)

        @pl.when(to_y * nz + to_z != me)
        def _():
            pl.semaphore_signal(
                barrier, inc=1, device_id={"gy": to_y, "gz": to_z}, device_id_type=MESH
            )

        return carry

    lax.fori_loop(0, walls, greet_wall, 0)

    @pl.when(is_wall)
    def _():
        def greet_row(j, carry):
            pl.semaphore_signal(
                barrier, inc=1, device_id={"gx": lax.rem(gx + j, nx)}, device_id_type=MESH
            )
            return carry

        lax.fori_loop(1, nx, greet_row, 0)

    loads[0].wait()

    def recon_step(i, carry):
        span = pl.ds(pl.multiple_of(i * 16, 16), 16)
        rho = fields[0, span, :]
        inv = recip(rho)
        inv = inv * (2.0 - rho * inv)
        vel = [fields[k, span, :] * inv for k in (1, 2, 3)]
        speed = vel[0] * vel[0] + vel[1] * vel[1] + vel[2] * vel[2]
        pressure = 0.4 * (fields[4, span, :] - 0.5 * rho * speed)
        rec[0, span, :] = jnp.log(rho)
        for k in range(3):
            rec[1 + k, span, :] = vel[k]
        rec[4, span, :] = jnp.log(pressure)
        for k in range(5, COMPS):
            rec[k, span, :] = fields[k, span, :] * inv
        return carry

    lax.fori_loop(0, ROWS // 16, recon_step, 0)

    @pl.when(is_wall)
    def _():
        pl.semaphore_wait(barrier, 6 + nx - 1 + group - 1)

    @pl.when(jnp.logical_not(is_wall))
    def _():
        pl.semaphore_wait(barrier, 6)

    sends = []

    def send(i, src, dst, where):
        copy = pltpu.make_async_remote_copy(
            src_ref=src,
            dst_ref=dst,
            send_sem=send_sem.at[i],
            recv_sem=recv_sem.at[i],
            device_id=around[where],
            device_id_type=MESH,
        )
        copy.start()
        sends.append(copy)

    send(0, rec.at[:, pl.ds(0, 24), :], xhi, "xlo")
    send(1, rec.at[:, pl.ds(ROWS - 24, 24), :], xlo, "xhi")

    def turn_to_y(k, carry):
        for y in range(CY):
            ybuf[k, pl.ds(8 * y, 8), :] = rec[k, pl.ds(y, CX, stride=CY), :]
        return carry

    lax.fori_loop(0, COMPS, turn_to_y, 0)
    send(2, ybuf.at[:, pl.ds(0, 24), :], yhi, "ylo")
    send(3, ybuf.at[:, pl.ds(ROWS - 24, 24), :], ylo, "yhi")

    first_half = iota((HALF, LANES), 1) < HALF

    def turn_to_z(i, carry):
        both = rec[pl.ds(2 * i, 2), :, :].reshape(2 * ROWS, CZ).T
        top = both[:HALF]
        bottom = both[HALF:]
        zbuf[2 * i, pl.ds(8, HALF), :] = jnp.where(first_half, top, pltpu.roll(bottom, HALF, 1))
        zbuf[2 * i + 1, pl.ds(8, HALF), :] = jnp.where(first_half, pltpu.roll(top, HALF, 1), bottom)
        return carry

    lax.fori_loop(0, COMPS // 2, turn_to_z, 0)
    send(4, zbuf.at[:, pl.ds(8, 8), :], zhi, "zlo")
    send(5, zbuf.at[:, pl.ds(HALF, 8), :], zlo, "zhi")

    loads[2].wait()

    @pl.when(is_wall)
    def _():
        low = gy == 0

        def line(k, sign):
            near = [
                jnp.where(low, ybuf[k, pl.ds(8 * j, 8), :], ybuf[k, pl.ds(ROWS - 8 - 8 * j, 8), :])
                for j in range(3)
            ]
            ghost = [sign * x for x in near]
            below = ghost[::-1] + near
            above = near[::-1] + ghost
            return jnp.stack([jnp.where(low, i, j) for i, j in zip(below, above)])

        left, right = {}, {}
        for k in (0, 2, 4):
            left[k], right[k] = weno_pair(line(k, -1.0 if k == 2 else 1.0))
        push = hllc(left, right, 1, only_push=True)[0] * (1.0 / (PATCH * PATCH))
        ids = jnp.where(low, pmap[0], pmap[1])
        total = jnp.zeros((nx, LANES), F32)
        for h in range(2):
            value = jnp.sum(push[4 * h : 4 * h + 4], axis=0, keepdims=True)
            panel = ids[4 * h : 4 * h + 1]
            spread = jnp.where(iota((nx, LANES), 0) == panel // LANES, value, 0.0)
            lane = one_where(iota((LANES, LANES), 0) == panel % LANES).astype(BF16)
            big = spread.astype(BF16)
            small = (spread - big.astype(F32)).astype(BF16)
            total = total + dot_nt(big, lane) + dot_nt(small, lane)
        contrib[...] = total.reshape(nx, 1, LANES)
        rows1[0] = contrib[gx]

        def send_row(j, carry):
            to = lax.rem(gx + j, nx)
            pltpu.make_async_remote_copy(
                src_ref=contrib.at[to],
                dst_ref=rows1.at[j],
                send_sem=s1_send,
                recv_sem=s1_recv,
                device_id={"gx": to},
                device_id_type=MESH,
            ).start()
            return carry

        lax.fori_loop(1, nx, send_row, 0)

    loads[1].wait()
    hot = react[...] > 0
    flags = one_where(hot).astype(BF16)
    upto = one_where(iota((CZ, CZ), 0) <= iota((CZ, CZ), 1)).astype(BF16)
    within = jnp.dot(flags, upto, preferred_element_type=F32)
    sums = jnp.dot(flags, jnp.ones((CZ, CAP), BF16), preferred_element_type=F32)
    above = one_where(iota((ROWS, ROWS), 1) < iota((ROWS, ROWS), 0)).astype(BF16)
    start = jnp.dot(above, sums.astype(BF16), preferred_element_type=F32)
    slot = iota((ROWS, CAP), 1).astype(F32)
    row_hot = one_where((start <= slot) & (slot < start + sums))
    rank = jnp.where(hot, start[:, :CZ] + within, 0.0).astype(BF16)
    sums_t = dot_nt(jnp.ones((CAP, CZ), BF16), flags)
    before = one_where(iota((ROWS, ROWS), 0) < iota((ROWS, ROWS), 1)).astype(BF16)
    start_t = jnp.dot(sums_t.astype(BF16), before, preferred_element_type=F32)
    slot_t = iota((CAP, ROWS), 0).astype(F32)
    row_hot_t = one_where((start_t <= slot_t) & (slot_t < start_t + sums_t)).astype(BF16)
    line_rank = jnp.dot(row_hot_t, rank, preferred_element_type=F32)
    lane_hot = one_where(line_rank == iota((CAP, CZ), 0).astype(F32) + 1.0).astype(BF16)

    cells = rec[...].reshape(COMPS * ROWS, CZ).astype(BF16)
    spread_cells = dot_nt(cells, lane_hot).reshape(COMPS, ROWS, CAP)
    features = jnp.sum(spread_cells * row_hot[None], axis=1).astype(BF16)

    loads[3].wait()
    hid1[...] = gelu(dot_tn(w1[...], features)).astype(BF16)
    loads[4].wait()
    hid2[...] = gelu(jnp.dot(w2[...], hid1[...], preferred_element_type=F32)).astype(BF16)
    loads[5].wait()
    loads[6].wait()
    hid3 = gelu(jnp.dot(w3[...], hid2[...], preferred_element_type=F32)).astype(BF16)
    rates = jnp.dot(w4[...], hid3, preferred_element_type=F32).astype(BF16).astype(F32)
    spread_rates = (rates[:, None, :] * row_hot[None]).reshape(COMPS * ROWS, CAP).astype(BF16)
    source[...] = jnp.dot(spread_rates, lane_hot, preferred_element_type=F32).reshape(
        COMPS, ROWS, CZ
    )

    slot_of = (gy // jnp.int32(max(ny - 1, 1))) * nz + gz

    @pl.when(is_wall)
    def _():
        pltpu.make_async_copy(rows1.at[pl.ds(1, nx - 1)], rows1.at[pl.ds(1, nx - 1)], s1_recv).wait()
        own[...] = jnp.sum(rows1[...], axis=0)
        parts[slot_of] = own[...]

        def send_part(j, carry):
            to = lax.rem(me + j, group)
            pltpu.make_async_remote_copy(
                src_ref=own,
                dst_ref=parts.at[slot_of],
                send_sem=s2_send,
                recv_sem=s2_recv,
                device_id={"gy": to // nz, "gz": lax.rem(to, nz)},
                device_id_type=MESH,
            ).start()
            return carry

        lax.fori_loop(1, group, send_part, 0)

    def faces(load, normal, flux):
        def weno_step(k, carry):
            left, right = weno_pair(load(k))
            st_l[k] = left
            st_r[k] = right
            return carry

        lax.fori_loop(0, COMPS, weno_step, 0)

        def flux_step(i, carry):
            span = pl.ds(i * 3, 3)
            left = [st_l[k, span] for k in range(COMPS)]
            right = [st_r[k, span] for k in range(COMPS)]
            for k, x in enumerate(hllc(left, right, normal)):
                flux[k, span] = x
            return carry

        lax.fori_loop(0, 3, flux_step, 0)

    def sign_of(k, normal):
        return jnp.where(k == 1 + normal, -1.0, 1.0).astype(F32)

    sends[4].wait_recv()
    sends[5].wait_recv()
    first_lanes = iota((8, LANES), 1) < HALF

    def ghosts_z(k, carry):
        zbuf[k, pl.ds(0, 8), :] = pltpu.roll(
            jnp.where(first_lanes, zbuf[k, pl.ds(HALF, 8), :], zlo[k]), HALF, 1
        )
        zbuf[k, pl.ds(HALF + 8, 8), :] = pltpu.roll(
            jnp.where(first_lanes, zhi[k], zbuf[k, pl.ds(8, 8), :]), HALF, 1
        )
        return carry

    lax.fori_loop(0, COMPS, ghosts_z, 0)
    lane_low = iota((1, LANES), 1) < HALF

    @pl.when(gz == 0)
    def _():
        def mirror(k, carry):
            for j in range(3):
                here = zbuf[k, pl.ds(7 - j, 1), :]
                inside = zbuf[k, pl.ds(8 + j, 1), :] * sign_of(k, 2)
                zbuf[k, pl.ds(7 - j, 1), :] = jnp.where(lane_low, inside, here)
            return carry

        lax.fori_loop(0, COMPS, mirror, 0)

    @pl.when(gz == nz - 1)
    def _():
        def mirror(k, carry):
            for j in range(3):
                here = zbuf[k, pl.ds(HALF + 8 + j, 1), :]
                inside = zbuf[k, pl.ds(HALF + 7 - j, 1), :] * sign_of(k, 2)
                zbuf[k, pl.ds(HALF + 8 + j, 1), :] = jnp.where(lane_low, here, inside)
            return carry

        lax.fori_loop(0, COMPS, mirror, 0)

    faces(
        lambda k: jnp.stack([zbuf[k, pl.ds(5 + j, 8, stride=8), :] for j in range(14)]), 2, flux_z
    )

    def mirror_planes(inner, low, high, normal, place, count):
        @pl.when(place == 0)
        def _():
            def mirror(k, carry):
                for j in range(3):
                    low[k, pl.ds(16 - 8 * j, 8), :] = inner[k, pl.ds(8 * j, 8), :] * sign_of(k, normal)
                return carry

            lax.fori_loop(0, COMPS, mirror, 0)

        @pl.when(place == count - 1)
        def _():
            def mirror(k, carry):
                for j in range(3):
                    high[k, pl.ds(8 * j, 8), :] = inner[k, pl.ds(ROWS - 8 - 8 * j, 8), :] * sign_of(
                        k, normal
                    )
                return carry

            lax.fori_loop(0, COMPS, mirror, 0)

    def planes(low, inner, high):
        def load(k):
            return jnp.concatenate(
                [low[k].reshape(3, 8, CZ), inner[k].reshape(8, 8, CZ), high[k].reshape(3, 8, CZ)]
            )

        return load

    sends[2].wait_recv()
    sends[3].wait_recv()
    mirror_planes(ybuf, ylo, yhi, 1, gy, ny)
    faces(planes(ylo, ybuf, yhi), 1, flux_y)
    sends[0].wait_recv()
    sends[1].wait_recv()
    mirror_planes(rec, xlo, xhi, 0, gx, nx)
    faces(planes(xlo, rec, xhi), 0, flux_x)

    def finish(i, carry):
        change = []
        for h in range(2):
            k = 2 * i + h
            along_z = flux_z[k, pl.ds(1, 8)] - flux_z[k, pl.ds(0, 8)]
            along_y = flux_y[k, pl.ds(1, 8)] - flux_y[k, pl.ds(0, 8)]
            for j in range(8):
                turn_z[h, pl.ds(j, 8, stride=8), :] = along_z[j]
                turn_y[h, pl.ds(j, 8, stride=8), :] = along_y[j]
            change.append((flux_x[k, pl.ds(1, 8)] - flux_x[k, pl.ds(0, 8)]).reshape(ROWS, CZ))
        one = turn_z[0]
        two = turn_z[1]
        top = jnp.where(first_half, one, pltpu.roll(two, HALF, 1))
        bottom = jnp.where(first_half, pltpu.roll(one, HALF, 1), two)
        back = jnp.concatenate([top, bottom], axis=0).T
        for h in range(2):
            k = 2 * i + h
            whole = change[h] + turn_y[h] + back[ROWS * h : ROWS * h + ROWS]
            out_ref[k] = fields[k] - TIME_STEP * whole + CHEM_STEP * source[k]
        return carry

    lax.fori_loop(0, COMPS // 2, finish, 0)

    @pl.when(is_wall)
    def _():
        few = pl.ds(0, walls - 1)
        pltpu.make_async_copy(parts.at[few], parts.at[few], s2_recv).wait()
        many = pl.ds(1, nx - 1)
        pltpu.make_async_copy(contrib.at[many], contrib.at[many], s1_send).wait()

        def sent(j, carry):
            pltpu.make_async_copy(own, own, s2_send).wait()
            return carry

        lax.fori_loop(1, group, sent, 0)

    @pl.when(jnp.logical_not(is_wall))
    def _():
        pltpu.make_async_copy(parts, parts, s2_recv).wait()

    total = jnp.sum(parts[...], axis=0)
    mine = LANES // group
    wide = jnp.broadcast_to(total, (8, LANES))
    imp_ref[...] = pltpu.roll(wide, lax.rem(LANES - me * mine, LANES), 1)
    for copy in sends:
        copy.wait_send()


def body(fields, reacting, panel_map, layer_one, layer_two, layer_three, layer_four):
    sizes = (lax.axis_size("gx"), lax.axis_size("gy"), lax.axis_size("gz"))
    nx, ny, nz = sizes
    any_spec = pl.BlockSpec(memory_space=pl.ANY)
    vmem_spec = pl.BlockSpec(memory_space=pltpu.VMEM)
    plane = (COMPS, ROWS, CZ)
    ghost = (COMPS, 24, CZ)
    state = (COMPS, 9, 8, CZ)
    dma = pltpu.SemaphoreType.DMA
    new_fields, impulse = pl.pallas_call(
        functools.partial(kernel, sizes),
        out_shape=(
            jax.ShapeDtypeStruct(plane, F32),
            jax.ShapeDtypeStruct((8, LANES), F32),
        ),
        in_specs=[any_spec] * 7,
        out_specs=(vmem_spec, vmem_spec),
        scratch_shapes=[
            pltpu.VMEM(plane, F32),
            pltpu.VMEM((ROWS, CZ), jnp.int32),
            pltpu.VMEM((2, CX, CZ), jnp.int32),
            pltpu.VMEM((COMPS, H1), BF16),
            pltpu.VMEM((H2, H1), BF16),
            pltpu.VMEM((H3, H2), BF16),
            pltpu.VMEM((COMPS, H3), BF16),
            pltpu.VMEM(plane, F32),
            pltpu.VMEM(plane, F32),
            pltpu.VMEM((COMPS, HALF + 16, LANES), F32),
            pltpu.VMEM(ghost, F32),
            pltpu.VMEM(ghost, F32),
            pltpu.VMEM(ghost, F32),
            pltpu.VMEM(ghost, F32),
            pltpu.VMEM((COMPS, 8, LANES), F32),
            pltpu.VMEM((COMPS, 8, LANES), F32),
            pltpu.VMEM(state, F32),
            pltpu.VMEM(state, F32),
            pltpu.VMEM(state, F32),
            pltpu.VMEM(state, F32),
            pltpu.VMEM(state, F32),
            pltpu.VMEM((2, ROWS, CZ), F32),
            pltpu.VMEM((2, ROWS, CZ), F32),
            pltpu.VMEM((H1, CAP), BF16),
            pltpu.VMEM((H2, CAP), BF16),
            pltpu.VMEM(plane, F32),
            pltpu.VMEM((nx, 1, LANES), F32),
            pltpu.VMEM((nx, 1, LANES), F32),
            pltpu.VMEM((2 * nz, 1, LANES), F32),
            pltpu.VMEM((1, LANES), F32),
            dma((7,)),
            dma((6,)),
            dma((6,)),
            dma(()),
            dma(()),
            dma(()),
            dma(()),
        ],
        compiler_params=pltpu.CompilerParams(
            collective_id=0, has_side_effects=True, vmem_limit_bytes=48 * 2**20
        ),
    )(
        fields.reshape(plane),
        reacting.reshape(ROWS, CZ),
        panel_map,
        layer_one.T,
        layer_two,
        layer_three,
        layer_four,
    )
    own_panels = 2 * nx * nz * (CZ // PATCH) // (nx * ny * nz)
    return new_fields.reshape(fields.shape), impulse[0, :own_panels]


def solution(mesh):
    return jax.shard_map(
        body,
        mesh=mesh,
        in_specs=(
            P(None, "gx", "gy", "gz"),
            P("gx", "gy", "gz"),
            P(None, "gx", "gz"),
            P(),
            P(),
            P(),
            P(),
        ),
        out_specs=(P(None, "gx", "gy", "gz"), P(("gx", "gy", "gz"))),
        check_vma=False,
    )
```

```python
import functools
import math

import jax
import jax.numpy as jnp
from jax import lax
from jax.experimental import pallas as pl
from jax.experimental.pallas import tpu as pltpu
from jax.sharding import PartitionSpec as P

COMPS = 12
CX = 8
CY = 8
CZ = 128
ROWS = CX * CY
HALF = CZ // 2
CAP = 256
H1 = 1600
H2 = 800
H3 = 400
PATCH = 8
LANES = 128

TIME_STEP = 0.1
CHEM_STEP = 0.25
WENO_EPS = 1e-06
ALPHA = math.sqrt(12.0 / 13.0)
EPS_SCALED = WENO_EPS * 12.0 / 13.0
LOG_HEAT_HALF = 0.5 * math.log(1.4)

MESH = pl.DeviceIdType.MESH
F32 = jnp.float32
BF16 = jnp.bfloat16


def recip(x):
    r = pl.reciprocal(x, approx=True)
    return r * (2.0 - x * r)


def weno_pair(v):
    count = v.shape[0]
    d = v[1:] - v[:-1]
    q = d[1:] - d[:-1]
    g = (q[1:] - q[:-1]) * (1.0 / 3.0)
    da = d * ALPHA
    ha = q * (0.5 * ALPHA)
    qq = q * q + EPS_SCALED
    m = count - 4
    f0 = da[1 : 1 + m] + ha[0:m]
    f1 = da[1 : 1 + m] + ha[1 : 1 + m]
    f2 = da[2 : 2 + m] - ha[2 : 2 + m]
    t0 = f0 * f0 + qq[0:m]
    t1 = f1 * f1 + qq[1 : 1 + m]
    t2 = f2 * f2 + qq[2 : 2 + m]
    a = t1 * t2
    b = t0 * t2
    c = t0 * t1
    a = a * a
    b = b * b * 6.0
    c = c * c
    u = a + c + b
    x = a * g[0:m]
    y = c * g[1 : 1 + m]
    center = v[2 : 2 + m] + q[1 : 1 + m] * (1.0 / 3.0)
    hd = d * 0.5
    n = m - 1
    low = slice(0, n)
    high = slice(1, m)
    left = (
        center[low]
        + hd[1 : 1 + n]
        - (x[low] + 1.5 * y[low]) * pl.reciprocal(u[low] + 2.0 * c[low], approx=True)
    )
    right = (
        center[high]
        - hd[3 : 3 + n]
        + (y[high] + 1.5 * x[high]) * pl.reciprocal(u[high] + 2.0 * a[high], approx=True)
    )
    return left, right


def hllc(left, right, normal, only_push=False):
    rl = jnp.exp(left[0])
    rr = jnp.exp(right[0])
    p_l = jnp.exp(left[4])
    p_r = jnp.exp(right[4])
    cl = jnp.exp(0.5 * (left[4] - left[0]) + LOG_HEAT_HALF)
    cr = jnp.exp(0.5 * (right[4] - right[0]) + LOG_HEAT_HALF)
    ul = left[1 + normal]
    ur = right[1 + normal]
    sl = jnp.minimum(ul - cl, ur - cr)
    sr = jnp.maximum(ul + cl, ur + cr)
    al = rl * (sl - ul)
    ar = rr * (sr - ur)
    s = (p_r - p_l + al * ul - ar * ur) * recip(al - ar)
    take_left = jnp.maximum(s, sl) >= 0.0

    def pick(i, j):
        return jnp.where(take_left, i, j)

    rho = pick(rl, rr)
    p = pick(p_l, p_r)
    sk = pick(sl, sr)
    a = pick(al, ar)
    beyond = pick(sl, -sr) >= 0.0
    un = pick(ul, ur)
    inv = recip(sk - s)
    pstar = p + a * (s - un)
    u_face = jnp.where(beyond, un, s)
    p_face = jnp.where(beyond, p, pstar)
    mass = jnp.where(beyond, rho, a * inv) * u_face
    push = mass * u_face + p_face
    if only_push:
        return push
    vel = [un if i == normal else pick(left[1 + i], right[1 + i]) for i in range(3)]
    energy = 2.5 * p + 0.5 * rho * (vel[0] * vel[0] + vel[1] * vel[1] + vel[2] * vel[2])
    estar = ((sk - un) * energy + pstar * s - p * un) * inv
    e_face = jnp.where(beyond, energy, estar)
    flux = [mass]
    for i in range(3):
        flux.append(push if i == normal else mass * vel[i])
    flux.append(u_face * (e_face + p_face))
    for i in range(5, COMPS):
        flux.append(mass * pick(left[i], right[i]))
    return flux


def gelu(x):
    k = math.sqrt(2.0 / math.pi)
    y = x * (x * x * (0.044715 * k) + k)
    h = 0.5 * x
    return h * jnp.tanh(y) + h


def dot_nt(a, b):
    return lax.dot_general(a, b, (((1,), (1,)), ((), ())), preferred_element_type=F32)


def dot_tn(a, b):
    return lax.dot_general(a, b, (((0,), (0,)), ((), ())), preferred_element_type=F32)


def iota(shape, dim):
    return lax.broadcasted_iota(jnp.int32, shape, dim)


def one_where(mask):
    return jnp.where(mask, 1.0, 0.0)


def kernel(
    sizes,
    fields_hbm,
    react_hbm,
    pmap_hbm,
    w1_hbm,
    w2_hbm,
    w3_hbm,
    w4_hbm,
    out_ref,
    imp_ref,
    fields,
    react,
    pmap,
    w1,
    w2,
    w3,
    w4,
    rec,
    ybuf,
    zbuf,
    xlo,
    xhi,
    ylo,
    yhi,
    zlo,
    zhi,
    st_l,
    st_r,
    flux_x,
    flux_y,
    flux_z,
    turn_y,
    turn_z,
    hid1,
    hid2,
    source,
    contrib,
    rows1,
    parts,
    own,
    load_sem,
    send_sem,
    recv_sem,
    s1_send,
    s1_recv,
    s2_send,
    s2_recv,
    ready,
):
    nx, ny, nz = sizes
    gx = lax.axis_index("gx")
    gy = lax.axis_index("gy")
    gz = lax.axis_index("gz")
    is_wall = (gy == 0) | (gy == ny - 1)
    group = ny * nz
    me = gy * nz + gz
    walls = 2 * nz

    loads = []
    for i, (src, dst) in enumerate(
        (
            (fields_hbm, fields),
            (react_hbm, react),
            (pmap_hbm, pmap),
            (w1_hbm, w1),
            (w2_hbm, w2),
            (w3_hbm, w3),
            (w4_hbm, w4),
        )
    ):
        copy = pltpu.make_async_copy(src, dst, load_sem.at[i])
        copy.start()
        loads.append(copy)

    barrier = pltpu.get_barrier_semaphore()
    around = {
        "xlo": {"gx": lax.rem(gx + nx - 1, nx)},
        "xhi": {"gx": lax.rem(gx + 1, nx)},
        "ylo": {"gy": lax.rem(gy + ny - 1, ny)},
        "yhi": {"gy": lax.rem(gy + 1, ny)},
        "zlo": {"gz": lax.rem(gz + nz - 1, nz)},
        "zhi": {"gz": lax.rem(gz + 1, nz)},
    }
    for where in around.values():
        pl.semaphore_signal(barrier, inc=1, device_id=where, device_id_type=MESH)

    def greet_wall(w, carry):
        to_y = (w // nz) * (ny - 1)
        to_z = lax.rem(w, nz)

        @pl.when(to_y * nz + to_z != me)
        def _():
            pl.semaphore_signal(
                barrier, inc=1, device_id={"gy": to_y, "gz": to_z}, device_id_type=MESH
            )

        return carry

    lax.fori_loop(0, walls, greet_wall, 0)

    half = nx // 2
    rank = lax.rem(gx, half) * 2 + gx // half

    def ranked(r):
        return lax.rem(r, 2) * half + r // 2

    @pl.when(is_wall)
    def _():
        def greet_row(r, carry):
            pl.semaphore_signal(barrier, inc=1, device_id={"gx": ranked(r)}, device_id_type=MESH)
            return carry

        lax.fori_loop(rank + 1, nx, greet_row, 0)

    loads[0].wait()

    def recon_step(i, carry):
        span = pl.ds(pl.multiple_of(i * 16, 16), 16)
        rho = fields[0, span, :]
        inv = recip(rho)
        inv = inv * (2.0 - rho * inv)
        vel = [fields[k, span, :] * inv for k in (1, 2, 3)]
        speed = vel[0] * vel[0] + vel[1] * vel[1] + vel[2] * vel[2]
        pressure = 0.4 * (fields[4, span, :] - 0.5 * rho * speed)
        rec[0, span, :] = jnp.log(rho)
        for k in range(3):
            rec[1 + k, span, :] = vel[k]
        rec[4, span, :] = jnp.log(pressure)
        for k in range(5, COMPS):
            rec[k, span, :] = fields[k, span, :] * inv
        return carry

    lax.fori_loop(0, ROWS // 16, recon_step, 0)

    @pl.when(is_wall)
    def _():
        pl.semaphore_wait(barrier, 6 + rank + group - 1)

    @pl.when(jnp.logical_not(is_wall))
    def _():
        pl.semaphore_wait(barrier, 6)

    sends = []

    def send(i, src, dst, where):
        copy = pltpu.make_async_remote_copy(
            src_ref=src,
            dst_ref=dst,
            send_sem=send_sem.at[i],
            recv_sem=recv_sem.at[i],
            device_id=around[where],
            device_id_type=MESH,
        )
        copy.start()
        sends.append(copy)

    send(0, rec.at[:, pl.ds(0, 24), :], xhi, "xlo")
    send(1, rec.at[:, pl.ds(ROWS - 24, 24), :], xlo, "xhi")

    def send_row(r, slot):
        to = ranked(r)
        pltpu.make_async_remote_copy(
            src_ref=contrib.at[to],
            dst_ref=rows1.at[slot],
            send_sem=s1_send,
            recv_sem=s1_recv,
            device_id={"gx": to},
            device_id_type=MESH,
        ).start()
        return 0

    loads[2].wait()

    @pl.when(is_wall)
    def _():
        low = gy == 0

        def line(k, sign):
            near = [
                jnp.where(
                    low,
                    rec[k, pl.ds(j, CX, stride=CY), :],
                    rec[k, pl.ds(CY - 1 - j, CX, stride=CY), :],
                )
                for j in range(3)
            ]
            ghost = [sign * x for x in near]
            below = ghost[::-1] + near
            above = near[::-1] + ghost
            return jnp.stack([jnp.where(low, i, j) for i, j in zip(below, above)])

        left, right = {}, {}
        for k in (0, 2, 4):
            left[k], right[k] = weno_pair(line(k, -1.0 if k == 2 else 1.0))
        push = hllc(left, right, 1, only_push=True)[0] * (1.0 / (PATCH * PATCH))
        ids = jnp.where(low, pmap[0], pmap[1])
        total = jnp.zeros((nx, LANES), F32)
        for h in range(2):
            value = jnp.sum(push[4 * h : 4 * h + 4], axis=0, keepdims=True)
            panel = ids[4 * h : 4 * h + 1]
            spread = jnp.where(iota((nx, LANES), 0) == panel // LANES, value, 0.0)
            lane = one_where(iota((LANES, LANES), 0) == panel % LANES).astype(BF16)
            big = spread.astype(BF16)
            small = (spread - big.astype(F32)).astype(BF16)
            total = total + dot_nt(big, lane) + dot_nt(small, lane)
        contrib[...] = total.reshape(nx, 1, LANES)
        rows1[0] = contrib[gx]

        lax.fori_loop(0, rank, lambda r, carry: send_row(r, r - rank + nx), 0)

        def signal_row(r, carry):
            pl.semaphore_signal(ready, inc=1, device_id={"gx": ranked(r)}, device_id_type=MESH)
            return carry

        lax.fori_loop(0, rank, signal_row, 0)

    def turn_to_y(k, carry):
        for y in range(CY):
            ybuf[k, pl.ds(8 * y, 8), :] = rec[k, pl.ds(y, CX, stride=CY), :]
        return carry

    lax.fori_loop(0, COMPS, turn_to_y, 0)
    send(2, ybuf.at[:, pl.ds(0, 24), :], yhi, "ylo")
    send(3, ybuf.at[:, pl.ds(ROWS - 24, 24), :], ylo, "yhi")

    first_half = iota((HALF, LANES), 1) < HALF

    def turn_to_z(i, carry):
        both = rec[pl.ds(2 * i, 2), :, :].reshape(2 * ROWS, CZ).T
        top = both[:HALF]
        bottom = both[HALF:]
        zbuf[2 * i, pl.ds(8, HALF), :] = jnp.where(first_half, top, pltpu.roll(bottom, HALF, 1))
        zbuf[2 * i + 1, pl.ds(8, HALF), :] = jnp.where(first_half, pltpu.roll(top, HALF, 1), bottom)
        return carry

    lax.fori_loop(0, COMPS // 2, turn_to_z, 0)
    send(4, zbuf.at[:, pl.ds(8, 8), :], zhi, "zlo")
    send(5, zbuf.at[:, pl.ds(HALF, 8), :], zlo, "zhi")

    loads[1].wait()
    hot = react[...] > 0
    flags = one_where(hot).astype(BF16)
    upto = one_where(iota((CZ, CZ), 0) <= iota((CZ, CZ), 1)).astype(BF16)
    within = jnp.dot(flags, upto, preferred_element_type=F32)
    sums = jnp.dot(flags, jnp.ones((CZ, CAP), BF16), preferred_element_type=F32)
    above = one_where(iota((ROWS, ROWS), 1) < iota((ROWS, ROWS), 0)).astype(BF16)
    start = jnp.dot(above, sums.astype(BF16), preferred_element_type=F32)
    slot = iota((ROWS, CAP), 1).astype(F32)
    row_hot = one_where((start <= slot) & (slot < start + sums))
    order = jnp.where(hot, start[:, :CZ] + within, 0.0).astype(BF16)
    sums_t = dot_nt(jnp.ones((CAP, CZ), BF16), flags)
    before = one_where(iota((ROWS, ROWS), 0) < iota((ROWS, ROWS), 1)).astype(BF16)
    start_t = jnp.dot(sums_t.astype(BF16), before, preferred_element_type=F32)
    slot_t = iota((CAP, ROWS), 0).astype(F32)
    row_hot_t = one_where((start_t <= slot_t) & (slot_t < start_t + sums_t)).astype(BF16)
    line_rank = jnp.dot(row_hot_t, order, preferred_element_type=F32)
    lane_hot = one_where(line_rank == iota((CAP, CZ), 0).astype(F32) + 1.0).astype(BF16)

    cells = rec[...].reshape(COMPS * ROWS, CZ).astype(BF16)
    spread_cells = dot_nt(cells, lane_hot).reshape(COMPS, ROWS, CAP)
    features = jnp.sum(spread_cells * row_hot[None], axis=1).astype(BF16)

    loads[3].wait()
    hid1[...] = gelu(dot_tn(w1[...], features)).astype(BF16)
    loads[4].wait()
    hid2[...] = gelu(jnp.dot(w2[...], hid1[...], preferred_element_type=F32)).astype(BF16)
    loads[5].wait()
    loads[6].wait()
    hid3 = gelu(jnp.dot(w3[...], hid2[...], preferred_element_type=F32)).astype(BF16)
    rates = jnp.dot(w4[...], hid3, preferred_element_type=F32).astype(BF16).astype(F32)
    spread_rates = (rates[:, None, :] * row_hot[None]).reshape(COMPS * ROWS, CAP).astype(BF16)
    source[...] = jnp.dot(spread_rates, lane_hot, preferred_element_type=F32).reshape(
        COMPS, ROWS, CZ
    )

    def faces(load, normal, flux):
        def weno_step(k, carry):
            left, right = weno_pair(load(k))
            st_l[k] = left
            st_r[k] = right
            return carry

        lax.fori_loop(0, COMPS, weno_step, 0)

        def flux_step(i, carry):
            span = pl.ds(i * 3, 3)
            left = [st_l[k, span] for k in range(COMPS)]
            right = [st_r[k, span] for k in range(COMPS)]
            for k, x in enumerate(hllc(left, right, normal)):
                flux[k, span] = x
            return carry

        lax.fori_loop(0, 3, flux_step, 0)

    def sign_of(k, normal):
        return jnp.where(k == 1 + normal, -1.0, 1.0).astype(F32)

    sends[4].wait_recv()
    sends[5].wait_recv()
    first_lanes = iota((8, LANES), 1) < HALF

    def ghosts_z(k, carry):
        zbuf[k, pl.ds(0, 8), :] = pltpu.roll(
            jnp.where(first_lanes, zbuf[k, pl.ds(HALF, 8), :], zlo[k]), HALF, 1
        )
        zbuf[k, pl.ds(HALF + 8, 8), :] = pltpu.roll(
            jnp.where(first_lanes, zhi[k], zbuf[k, pl.ds(8, 8), :]), HALF, 1
        )
        return carry

    lax.fori_loop(0, COMPS, ghosts_z, 0)
    lane_low = iota((1, LANES), 1) < HALF

    @pl.when(gz == 0)
    def _():
        def mirror(k, carry):
            for j in range(3):
                here = zbuf[k, pl.ds(7 - j, 1), :]
                inside = zbuf[k, pl.ds(8 + j, 1), :] * sign_of(k, 2)
                zbuf[k, pl.ds(7 - j, 1), :] = jnp.where(lane_low, inside, here)
            return carry

        lax.fori_loop(0, COMPS, mirror, 0)

    @pl.when(gz == nz - 1)
    def _():
        def mirror(k, carry):
            for j in range(3):
                here = zbuf[k, pl.ds(HALF + 8 + j, 1), :]
                inside = zbuf[k, pl.ds(HALF + 7 - j, 1), :] * sign_of(k, 2)
                zbuf[k, pl.ds(HALF + 8 + j, 1), :] = jnp.where(lane_low, here, inside)
            return carry

        lax.fori_loop(0, COMPS, mirror, 0)

    faces(
        lambda k: jnp.stack([zbuf[k, pl.ds(5 + j, 8, stride=8), :] for j in range(14)]), 2, flux_z
    )

    def mirror_planes(inner, low, high, normal, place, count):
        @pl.when(place == 0)
        def _():
            def mirror(k, carry):
                for j in range(3):
                    low[k, pl.ds(16 - 8 * j, 8), :] = inner[k, pl.ds(8 * j, 8), :] * sign_of(k, normal)
                return carry

            lax.fori_loop(0, COMPS, mirror, 0)

        @pl.when(place == count - 1)
        def _():
            def mirror(k, carry):
                for j in range(3):
                    high[k, pl.ds(8 * j, 8), :] = inner[k, pl.ds(ROWS - 8 - 8 * j, 8), :] * sign_of(
                        k, normal
                    )
                return carry

            lax.fori_loop(0, COMPS, mirror, 0)

    def planes(low, inner, high):
        def load(k):
            return jnp.concatenate(
                [low[k].reshape(3, 8, CZ), inner[k].reshape(8, 8, CZ), high[k].reshape(3, 8, CZ)]
            )

        return load

    sends[2].wait_recv()
    sends[3].wait_recv()
    mirror_planes(ybuf, ylo, yhi, 1, gy, ny)
    faces(planes(ylo, ybuf, yhi), 1, flux_y)
    slot_of = (gy // jnp.int32(max(ny - 1, 1))) * nz + gz

    @pl.when(is_wall)
    def _():
        @pl.when(rank < nx - 1)
        def _():
            pl.semaphore_wait(ready, nx - 1 - rank)
            lax.fori_loop(rank + 1, nx, lambda r, carry: send_row(r, r - rank), 0)

        pltpu.make_async_copy(rows1.at[pl.ds(1, nx - 1)], rows1.at[pl.ds(1, nx - 1)], s1_recv).wait()
        own[...] = jnp.sum(rows1[...], axis=0)
        parts[slot_of] = own[...]

        def send_part(j, carry):
            to = lax.rem(me + j, group)
            pltpu.make_async_remote_copy(
                src_ref=own,
                dst_ref=parts.at[slot_of],
                send_sem=s2_send,
                recv_sem=s2_recv,
                device_id={"gy": to // nz, "gz": lax.rem(to, nz)},
                device_id_type=MESH,
            ).start()
            return carry

        lax.fori_loop(1, group, send_part, 0)

    sends[0].wait_recv()
    sends[1].wait_recv()
    mirror_planes(rec, xlo, xhi, 0, gx, nx)
    faces(planes(xlo, rec, xhi), 0, flux_x)

    def finish(i, carry):
        change = []
        for h in range(2):
            k = 2 * i + h
            along_z = flux_z[k, pl.ds(1, 8)] - flux_z[k, pl.ds(0, 8)]
            along_y = flux_y[k, pl.ds(1, 8)] - flux_y[k, pl.ds(0, 8)]
            for j in range(8):
                turn_z[h, pl.ds(j, 8, stride=8), :] = along_z[j]
                turn_y[h, pl.ds(j, 8, stride=8), :] = along_y[j]
            change.append((flux_x[k, pl.ds(1, 8)] - flux_x[k, pl.ds(0, 8)]).reshape(ROWS, CZ))
        one = turn_z[0]
        two = turn_z[1]
        top = jnp.where(first_half, one, pltpu.roll(two, HALF, 1))
        bottom = jnp.where(first_half, pltpu.roll(one, HALF, 1), two)
        back = jnp.concatenate([top, bottom], axis=0).T
        for h in range(2):
            k = 2 * i + h
            whole = change[h] + turn_y[h] + back[ROWS * h : ROWS * h + ROWS]
            out_ref[k] = fields[k] - TIME_STEP * whole + CHEM_STEP * source[k]
        return carry

    lax.fori_loop(0, COMPS // 2, finish, 0)

    @pl.when(is_wall)
    def _():
        few = pl.ds(0, walls - 1)
        pltpu.make_async_copy(parts.at[few], parts.at[few], s2_recv).wait()
        many = pl.ds(1, nx - 1)
        pltpu.make_async_copy(contrib.at[many], contrib.at[many], s1_send).wait()

        def sent(j, carry):
            pltpu.make_async_copy(own, own, s2_send).wait()
            return carry

        lax.fori_loop(1, group, sent, 0)

    @pl.when(jnp.logical_not(is_wall))
    def _():
        pltpu.make_async_copy(parts, parts, s2_recv).wait()

    total = jnp.sum(parts[...], axis=0)
    mine = LANES // group
    wide = jnp.broadcast_to(total, (8, LANES))
    imp_ref[...] = pltpu.roll(wide, lax.rem(LANES - me * mine, LANES), 1)
    for copy in sends:
        copy.wait_send()


def body(fields, reacting, panel_map, layer_one, layer_two, layer_three, layer_four):
    sizes = (lax.axis_size("gx"), lax.axis_size("gy"), lax.axis_size("gz"))
    nx, ny, nz = sizes
    any_spec = pl.BlockSpec(memory_space=pltpu.HBM)
    vmem_spec = pl.BlockSpec(memory_space=pltpu.VMEM)
    plane = (COMPS, ROWS, CZ)
    ghost = (COMPS, 24, CZ)
    state = (COMPS, 9, 8, CZ)
    dma = pltpu.SemaphoreType.DMA
    held = pltpu.with_memory_space_constraint
    new_fields, impulse = pl.pallas_call(
        functools.partial(kernel, sizes),
        out_shape=(
            pltpu.VMEM(plane, F32),
            pltpu.VMEM((8, LANES), F32),
        ),
        in_specs=[any_spec] * 7,
        out_specs=(vmem_spec, vmem_spec),
        scratch_shapes=[
            pltpu.VMEM(plane, F32),
            pltpu.VMEM((ROWS, CZ), jnp.int32),
            pltpu.VMEM((2, CX, CZ), jnp.int32),
            pltpu.VMEM((COMPS, H1), BF16),
            pltpu.VMEM((H2, H1), BF16),
            pltpu.VMEM((H3, H2), BF16),
            pltpu.VMEM((COMPS, H3), BF16),
            pltpu.VMEM(plane, F32),
            pltpu.VMEM(plane, F32),
            pltpu.VMEM((COMPS, HALF + 16, LANES), F32),
            pltpu.VMEM(ghost, F32),
            pltpu.VMEM(ghost, F32),
            pltpu.VMEM(ghost, F32),
            pltpu.VMEM(ghost, F32),
            pltpu.VMEM((COMPS, 8, LANES), F32),
            pltpu.VMEM((COMPS, 8, LANES), F32),
            pltpu.VMEM(state, F32),
            pltpu.VMEM(state, F32),
            pltpu.VMEM(state, F32),
            pltpu.VMEM(state, F32),
            pltpu.VMEM(state, F32),
            pltpu.VMEM((2, ROWS, CZ), F32),
            pltpu.VMEM((2, ROWS, CZ), F32),
            pltpu.VMEM((H1, CAP), BF16),
            pltpu.VMEM((H2, CAP), BF16),
            pltpu.VMEM(plane, F32),
            pltpu.VMEM((nx, 1, LANES), F32),
            pltpu.VMEM((nx, 1, LANES), F32),
            pltpu.VMEM((2 * nz, 1, LANES), F32),
            pltpu.VMEM((1, LANES), F32),
            dma((7,)),
            dma((6,)),
            dma((6,)),
            dma(()),
            dma(()),
            dma(()),
            dma(()),
            pltpu.SemaphoreType.REGULAR,
        ],
        compiler_params=pltpu.CompilerParams(
            collective_id=0, has_side_effects=True, vmem_limit_bytes=48 * 2**20
        ),
    )(
        held(fields.reshape(plane), pltpu.HBM),
        held(reacting.reshape(ROWS, CZ), pltpu.HBM),
        held(panel_map, pltpu.HBM),
        held(layer_one.T, pltpu.HBM),
        held(layer_two, pltpu.HBM),
        held(layer_three, pltpu.HBM),
        held(layer_four, pltpu.HBM),
    )
    own_panels = 2 * nx * nz * (CZ // PATCH) // (nx * ny * nz)
    return new_fields.reshape(fields.shape), impulse[0, :own_panels]


def solution(mesh):
    return jax.shard_map(
        body,
        mesh=mesh,
        in_specs=(
            P(None, "gx", "gy", "gz"),
            P("gx", "gy", "gz"),
            P(None, "gx", "gz"),
            P(),
            P(),
            P(),
            P(),
        ),
        out_specs=(P(None, "gx", "gy", "gz"), P(("gx", "gy", "gz"))),
        check_vma=False,
    )
```

```python
import functools
import math

import jax
import jax.numpy as jnp
from jax import lax
from jax.experimental import pallas as pl
from jax.experimental.pallas import tpu as pltpu
from jax.sharding import PartitionSpec as P

COMPS = 12
CX = 8
CY = 8
CZ = 128
ROWS = CX * CY
HALF = CZ // 2
CAP = 256
H1 = 1600
H2 = 800
H3 = 400
PATCH = 8
LANES = 128

TIME_STEP = 0.1
CHEM_STEP = 0.25
WENO_EPS = 1e-06
ALPHA = math.sqrt(12.0 / 13.0)
EPS_SCALED = WENO_EPS * 12.0 / 13.0
LOG_HEAT_HALF = 0.5 * math.log(1.4)

MESH = pl.DeviceIdType.MESH
F32 = jnp.float32
BF16 = jnp.bfloat16


def recip(x):
    r = pl.reciprocal(x, approx=True)
    return r * (2.0 - x * r)


def primitive(rho, momentum, energy):
    inv = recip(rho)
    inv = inv * (2.0 - rho * inv)
    vel = [x * inv for x in momentum]
    speed = vel[0] * vel[0] + vel[1] * vel[1] + vel[2] * vel[2]
    return jnp.log(rho), vel, jnp.log(0.4 * (energy - 0.5 * rho * speed)), inv


def weno_pair(v):
    count = v.shape[0]
    d = v[1:] - v[:-1]
    q = d[1:] - d[:-1]
    g = (q[1:] - q[:-1]) * (1.0 / 3.0)
    da = d * ALPHA
    ha = q * (0.5 * ALPHA)
    qq = q * q + EPS_SCALED
    m = count - 4
    f0 = da[1 : 1 + m] + ha[0:m]
    f1 = da[1 : 1 + m] + ha[1 : 1 + m]
    f2 = da[2 : 2 + m] - ha[2 : 2 + m]
    t0 = f0 * f0 + qq[0:m]
    t1 = f1 * f1 + qq[1 : 1 + m]
    t2 = f2 * f2 + qq[2 : 2 + m]
    a = t1 * t2
    b = t0 * t2
    c = t0 * t1
    a = a * a
    b = b * b * 6.0
    c = c * c
    u = a + c + b
    x = a * g[0:m]
    y = c * g[1 : 1 + m]
    center = v[2 : 2 + m] + q[1 : 1 + m] * (1.0 / 3.0)
    hd = d * 0.5
    n = m - 1
    low = slice(0, n)
    high = slice(1, m)
    left = (
        center[low]
        + hd[1 : 1 + n]
        - (x[low] + 1.5 * y[low]) * pl.reciprocal(u[low] + 2.0 * c[low], approx=True)
    )
    right = (
        center[high]
        - hd[3 : 3 + n]
        + (y[high] + 1.5 * x[high]) * pl.reciprocal(u[high] + 2.0 * a[high], approx=True)
    )
    return left, right


def hllc(left, right, normal, only_push=False):
    rl = jnp.exp(left[0])
    rr = jnp.exp(right[0])
    p_l = jnp.exp(left[4])
    p_r = jnp.exp(right[4])
    cl = jnp.exp(0.5 * (left[4] - left[0]) + LOG_HEAT_HALF)
    cr = jnp.exp(0.5 * (right[4] - right[0]) + LOG_HEAT_HALF)
    ul = left[1 + normal]
    ur = right[1 + normal]
    sl = jnp.minimum(ul - cl, ur - cr)
    sr = jnp.maximum(ul + cl, ur + cr)
    al = rl * (sl - ul)
    ar = rr * (sr - ur)
    s = (p_r - p_l + al * ul - ar * ur) * recip(al - ar)
    take_left = jnp.maximum(s, sl) >= 0.0

    def pick(i, j):
        return jnp.where(take_left, i, j)

    rho = pick(rl, rr)
    p = pick(p_l, p_r)
    sk = pick(sl, sr)
    a = pick(al, ar)
    beyond = pick(sl, -sr) >= 0.0
    un = pick(ul, ur)
    inv = recip(sk - s)
    pstar = p + a * (s - un)
    u_face = jnp.where(beyond, un, s)
    p_face = jnp.where(beyond, p, pstar)
    mass = jnp.where(beyond, rho, a * inv) * u_face
    push = mass * u_face + p_face
    if only_push:
        return push
    vel = [un if i == normal else pick(left[1 + i], right[1 + i]) for i in range(3)]
    energy = 2.5 * p + 0.5 * rho * (vel[0] * vel[0] + vel[1] * vel[1] + vel[2] * vel[2])
    estar = ((sk - un) * energy + pstar * s - p * un) * inv
    e_face = jnp.where(beyond, energy, estar)
    flux = [mass]
    for i in range(3):
        flux.append(push if i == normal else mass * vel[i])
    flux.append(u_face * (e_face + p_face))
    for i in range(5, COMPS):
        flux.append(mass * pick(left[i], right[i]))
    return flux


def gelu(x):
    k = math.sqrt(2.0 / math.pi)
    y = x * (x * x * (0.044715 * k) + k)
    h = 0.5 * x
    return h * jnp.tanh(y) + h


def dot_nt(a, b):
    return lax.dot_general(a, b, (((1,), (1,)), ((), ())), preferred_element_type=F32)


def dot_tn(a, b):
    return lax.dot_general(a, b, (((0,), (0,)), ((), ())), preferred_element_type=F32)


def iota(shape, dim):
    return lax.broadcasted_iota(jnp.int32, shape, dim)


def one_where(mask):
    return jnp.where(mask, 1.0, 0.0)


def kernel(
    sizes,
    fields_hbm,
    react_hbm,
    pmap_hbm,
    w1_hbm,
    w2_hbm,
    w3_hbm,
    w4_hbm,
    out_ref,
    imp_ref,
    fields,
    react,
    pmap,
    w1,
    w2,
    w3,
    w4,
    rec,
    ybuf,
    zbuf,
    xlo,
    xhi,
    ylo,
    yhi,
    zlo,
    zhi,
    st_l,
    st_r,
    flux_x,
    flux_y,
    flux_z,
    turn_y,
    turn_z,
    hid1,
    hid2,
    source,
    contrib,
    rows2,
    parts,
    own,
    load_sem,
    send_sem,
    recv_sem,
    s1_send,
    s1_recv,
    s2_send,
    s2_recv,
    ready,
    late,
):
    nx, ny, nz = sizes
    gx = lax.axis_index("gx")
    gy = lax.axis_index("gy")
    gz = lax.axis_index("gz")
    is_wall = (gy == 0) | (gy == ny - 1)
    group = ny * nz
    me = gy * nz + gz
    walls = 2 * nz
    mine = 2 * nx * nz * (CZ // PATCH) // (nx * ny * nz)

    loads = []
    for i, (src, dst) in enumerate(
        (
            (fields_hbm, fields),
            (react_hbm, react),
            (pmap_hbm, pmap),
            (w1_hbm, w1),
            (w2_hbm, w2),
            (w3_hbm, w3),
            (w4_hbm, w4),
        )
    ):
        copy = pltpu.make_async_copy(src, dst, load_sem.at[i])
        copy.start()
        loads.append(copy)

    barrier = pltpu.get_barrier_semaphore()
    around = {
        "xlo": {"gx": lax.rem(gx + nx - 1, nx)},
        "xhi": {"gx": lax.rem(gx + 1, nx)},
        "ylo": {"gy": lax.rem(gy + ny - 1, ny)},
        "yhi": {"gy": lax.rem(gy + 1, ny)},
        "zlo": {"gz": lax.rem(gz + nz - 1, nz)},
        "zhi": {"gz": lax.rem(gz + 1, nz)},
    }
    half = nx // 2
    rank = lax.rem(gx, half)
    side = gx // half
    has_low = gx > 0
    has_high = gx < nx - 1
    late_low = gx == half
    late_high = gx == half - 1

    def greet(where):
        pl.semaphore_signal(barrier, inc=1, device_id=around[where], device_id_type=MESH)

    for where in ("ylo", "yhi", "zlo", "zhi"):
        greet(where)

    @pl.when(has_low)
    def _():
        greet("xlo")

    @pl.when(has_high & jnp.logical_not(late_high))
    def _():
        greet("xhi")

    def greet_wall(w, carry):
        to_side = w // walls
        to_y = lax.rem(w // nz, 2) * (ny - 1)
        to_z = lax.rem(w, nz)

        @pl.when((to_side != side) | (to_y * nz + to_z != me))
        def _():
            pl.semaphore_signal(
                barrier,
                inc=1,
                device_id={"gx": to_side * half + rank, "gy": to_y, "gz": to_z},
                device_id_type=MESH,
            )

        return carry

    lax.fori_loop(0, 2 * walls, greet_wall, 0)

    def ranked(r):
        return side * half + r

    def greet_row(r, carry):
        pl.semaphore_signal(barrier, inc=1, device_id={"gx": ranked(r)}, device_id_type=MESH)
        return carry

    lax.fori_loop(rank + 1, half, greet_row, 0)

    slot_of = side * walls + (gy // jnp.int32(max(ny - 1, 1))) * nz + gz
    loads[0].wait()

    def send_row(r, slot):
        pltpu.make_async_remote_copy(
            src_ref=own,
            dst_ref=rows2.at[slot],
            send_sem=s2_send,
            recv_sem=s2_recv,
            device_id={"gx": ranked(r)},
            device_id_type=MESH,
        ).start()
        return 0

    loads[2].wait()

    @pl.when(is_wall)
    def _():
        low = gy == 0

        near_of = {0: [], 2: [], 4: []}
        for j in range(3):
            rho, *momentum, energy = (
                jnp.where(
                    low,
                    fields[k, pl.ds(j, CX, stride=CY), :],
                    fields[k, pl.ds(CY - 1 - j, CX, stride=CY), :],
                )
                for k in range(5)
            )
            log_rho, vel, log_pressure, _ = primitive(rho, momentum, energy)
            near_of[0].append(log_rho)
            near_of[2].append(vel[1])
            near_of[4].append(log_pressure)

        def line(k, sign):
            near = near_of[k]
            ghost = [sign * x for x in near]
            below = ghost[::-1] + near
            above = near[::-1] + ghost
            return jnp.stack([jnp.where(low, i, j) for i, j in zip(below, above)])

        left, right = {}, {}
        for k in (0, 2, 4):
            left[k], right[k] = weno_pair(line(k, -1.0 if k == 2 else 1.0))
        push = hllc(left, right, 1, only_push=True)[0] * (1.0 / (PATCH * PATCH))
        ids = jnp.where(low, pmap[0], pmap[1])
        total = jnp.zeros((2 * group, LANES), F32)
        for h in range(2):
            value = jnp.sum(push[4 * h : 4 * h + 4], axis=0, keepdims=True)
            panel = ids[4 * h : 4 * h + 1]
            owner = panel // mine
            owner_x = owner // group
            member = owner_x // half * group + owner % group
            place = owner_x % half * mine + panel % mine
            spread = jnp.where(iota((2 * group, LANES), 0) == member, value, 0.0)
            lane = one_where(iota((LANES, LANES), 0) == place).astype(BF16)
            big = spread.astype(BF16)
            small = (spread - big.astype(F32)).astype(BF16)
            total = total + dot_nt(big, lane) + dot_nt(small, lane)
        contrib[...] = total.reshape(2 * group, 1, LANES)
        parts[slot_of] = contrib[side * group + me]

    def recon_step(i, carry):
        span = pl.ds(pl.multiple_of(i * 16, 16), 16)
        rho, *momentum, energy = (fields[k, span, :] for k in range(5))
        log_rho, vel, log_pressure, inv = primitive(rho, momentum, energy)
        rec[0, span, :] = log_rho
        for k in range(3):
            rec[1 + k, span, :] = vel[k]
        rec[4, span, :] = log_pressure
        for k in range(5, COMPS):
            rec[k, span, :] = fields[k, span, :] * inv
        return carry

    waits_long = rank >= half - half // 4

    @pl.when(waits_long)
    def _():
        lax.fori_loop(0, ROWS // 16, recon_step, 0)

    linked = (
        4
        + has_high.astype(jnp.int32)
        + (has_low & jnp.logical_not(late_low)).astype(jnp.int32)
        + rank
        + is_wall.astype(jnp.int32) * (2 * group - 1)
    )
    pl.semaphore_wait(barrier, linked)

    @pl.when(late_high)
    def _():
        pl.semaphore_signal(late, inc=1, device_id=around["xhi"], device_id_type=MESH)

    @pl.when(is_wall)
    def _():
        def send_part(j, carry):
            to = lax.rem(side * group + me + j, 2 * group)
            pltpu.make_async_remote_copy(
                src_ref=contrib.at[to],
                dst_ref=parts.at[slot_of],
                send_sem=s1_send,
                recv_sem=s1_recv,
                device_id={
                    "gx": to // group * half + rank,
                    "gy": lax.rem(to // nz, ny),
                    "gz": lax.rem(to, nz),
                },
                device_id_type=MESH,
            ).start()
            return carry

        lax.fori_loop(1, 2 * group, send_part, 0)

    def signal_row(r, carry):
        pl.semaphore_signal(ready, inc=1, device_id={"gx": ranked(r)}, device_id_type=MESH)
        return carry

    lax.fori_loop(0, rank, signal_row, 0)

    @pl.when(jnp.logical_not(waits_long))
    def _():
        lax.fori_loop(0, ROWS // 16, recon_step, 0)

    sends = []

    def send(i, src, dst, where):
        copy = pltpu.make_async_remote_copy(
            src_ref=src,
            dst_ref=dst,
            send_sem=send_sem.at[i],
            recv_sem=recv_sem.at[i],
            device_id=around[where],
            device_id_type=MESH,
        )
        sends.append(copy)
        return copy

    to_low = send(0, rec.at[:, pl.ds(0, 24), :], xhi, "xlo")
    to_high = send(1, rec.at[:, pl.ds(ROWS - 24, 24), :], xlo, "xhi")

    @pl.when(has_low & jnp.logical_not(late_low))
    def _():
        to_low.start()

    @pl.when(has_high)
    def _():
        to_high.start()


    def turn_to_y(k, carry):
        for y in range(CY):
            ybuf[k, pl.ds(8 * y, 8), :] = rec[k, pl.ds(y, CX, stride=CY), :]
        return carry

    lax.fori_loop(0, COMPS, turn_to_y, 0)
    send(2, ybuf.at[:, pl.ds(0, 24), :], yhi, "ylo").start()
    send(3, ybuf.at[:, pl.ds(ROWS - 24, 24), :], ylo, "yhi").start()

    first_half = iota((HALF, LANES), 1) < HALF

    def turn_to_z(i, carry):
        both = rec[pl.ds(2 * i, 2), :, :].reshape(2 * ROWS, CZ).T
        top = both[:HALF]
        bottom = both[HALF:]
        zbuf[2 * i, pl.ds(8, HALF), :] = jnp.where(first_half, top, pltpu.roll(bottom, HALF, 1))
        zbuf[2 * i + 1, pl.ds(8, HALF), :] = jnp.where(first_half, pltpu.roll(top, HALF, 1), bottom)
        return carry

    lax.fori_loop(0, COMPS // 2, turn_to_z, 0)
    send(4, zbuf.at[:, pl.ds(8, 8), :], zhi, "zlo").start()
    send(5, zbuf.at[:, pl.ds(HALF, 8), :], zlo, "zhi").start()

    loads[1].wait()
    hot = react[...] > 0
    flags = one_where(hot).astype(BF16)
    upto = one_where(iota((CZ, CZ), 0) <= iota((CZ, CZ), 1)).astype(BF16)
    within = jnp.dot(flags, upto, preferred_element_type=F32)
    sums = jnp.dot(flags, jnp.ones((CZ, CAP), BF16), preferred_element_type=F32)
    above = one_where(iota((ROWS, ROWS), 1) < iota((ROWS, ROWS), 0)).astype(BF16)
    start = jnp.dot(above, sums.astype(BF16), preferred_element_type=F32)
    slot = iota((ROWS, CAP), 1).astype(F32)
    row_hot = one_where((start <= slot) & (slot < start + sums))
    order = jnp.where(hot, start[:, :CZ] + within, 0.0).astype(BF16)
    sums_t = dot_nt(jnp.ones((CAP, CZ), BF16), flags)
    before = one_where(iota((ROWS, ROWS), 0) < iota((ROWS, ROWS), 1)).astype(BF16)
    start_t = jnp.dot(sums_t.astype(BF16), before, preferred_element_type=F32)
    slot_t = iota((CAP, ROWS), 0).astype(F32)
    row_hot_t = one_where((start_t <= slot_t) & (slot_t < start_t + sums_t)).astype(BF16)
    line_rank = jnp.dot(row_hot_t, order, preferred_element_type=F32)
    lane_hot = one_where(line_rank == iota((CAP, CZ), 0).astype(F32) + 1.0).astype(BF16)

    @pl.when(is_wall)
    def _():
        few = parts.at[pl.ds(0, 2 * walls - 1)]
        pltpu.make_async_copy(few, few, s1_recv).wait()

    @pl.when(jnp.logical_not(is_wall))
    def _():
        pltpu.make_async_copy(parts, parts, s1_recv).wait()

    own[...] = jnp.sum(parts[...], axis=0)
    rows2[0] = own[...]
    lax.fori_loop(0, rank, lambda r, carry: send_row(r, r - rank + half), 0)

    cells = rec[...].reshape(COMPS * ROWS, CZ).astype(BF16)
    spread_cells = dot_nt(cells, lane_hot).reshape(COMPS, ROWS, CAP)
    features = jnp.sum(spread_cells * row_hot[None], axis=1).astype(BF16)

    loads[3].wait()
    hid1[...] = gelu(dot_tn(w1[...], features)).astype(BF16)
    loads[4].wait()
    hid2[...] = gelu(jnp.dot(w2[...], hid1[...], preferred_element_type=F32)).astype(BF16)
    loads[5].wait()
    loads[6].wait()
    hid3 = gelu(jnp.dot(w3[...], hid2[...], preferred_element_type=F32)).astype(BF16)
    rates = jnp.dot(w4[...], hid3, preferred_element_type=F32).astype(BF16).astype(F32)
    spread_rates = (rates[:, None, :] * row_hot[None]).reshape(COMPS * ROWS, CAP).astype(BF16)
    source[...] = jnp.dot(spread_rates, lane_hot, preferred_element_type=F32).reshape(
        COMPS, ROWS, CZ
    )

    def faces(load, normal, flux):
        def weno_step(k, carry):
            left, right = weno_pair(load(k))
            st_l[k] = left
            st_r[k] = right
            return carry

        lax.fori_loop(0, COMPS, weno_step, 0)

        def flux_step(i, carry):
            span = pl.ds(i * 3, 3)
            left = [st_l[k, span] for k in range(COMPS)]
            right = [st_r[k, span] for k in range(COMPS)]
            for k, x in enumerate(hllc(left, right, normal)):
                flux[k, span] = x
            return carry

        lax.fori_loop(0, 3, flux_step, 0)

    def sign_of(k, normal):
        return jnp.where(k == 1 + normal, -1.0, 1.0).astype(F32)

    sends[4].wait_recv()
    sends[5].wait_recv()
    first_lanes = iota((8, LANES), 1) < HALF

    def ghosts_z(k, carry):
        zbuf[k, pl.ds(0, 8), :] = pltpu.roll(
            jnp.where(first_lanes, zbuf[k, pl.ds(HALF, 8), :], zlo[k]), HALF, 1
        )
        zbuf[k, pl.ds(HALF + 8, 8), :] = pltpu.roll(
            jnp.where(first_lanes, zhi[k], zbuf[k, pl.ds(8, 8), :]), HALF, 1
        )
        return carry

    lax.fori_loop(0, COMPS, ghosts_z, 0)
    lane_low = iota((1, LANES), 1) < HALF

    @pl.when(gz == 0)
    def _():
        def mirror(k, carry):
            for j in range(3):
                here = zbuf[k, pl.ds(7 - j, 1), :]
                inside = zbuf[k, pl.ds(8 + j, 1), :] * sign_of(k, 2)
                zbuf[k, pl.ds(7 - j, 1), :] = jnp.where(lane_low, inside, here)
            return carry

        lax.fori_loop(0, COMPS, mirror, 0)

    @pl.when(gz == nz - 1)
    def _():
        def mirror(k, carry):
            for j in range(3):
                here = zbuf[k, pl.ds(HALF + 8 + j, 1), :]
                inside = zbuf[k, pl.ds(HALF + 7 - j, 1), :] * sign_of(k, 2)
                zbuf[k, pl.ds(HALF + 8 + j, 1), :] = jnp.where(lane_low, here, inside)
            return carry

        lax.fori_loop(0, COMPS, mirror, 0)

    faces(
        lambda k: jnp.stack([zbuf[k, pl.ds(5 + j, 8, stride=8), :] for j in range(14)]), 2, flux_z
    )

    def send_up():
        pl.semaphore_wait(ready, half - 1 - rank)
        lax.fori_loop(rank + 1, half, lambda r, carry: send_row(r, r - rank), 0)

    goes_up = rank < half - 1
    goes_early = rank >= half // 2

    @pl.when(goes_up & goes_early)
    def _():
        send_up()

    def mirror_planes(inner, low, high, normal, place, count):
        @pl.when(place == 0)
        def _():
            def mirror(k, carry):
                for j in range(3):
                    low[k, pl.ds(16 - 8 * j, 8), :] = inner[k, pl.ds(8 * j, 8), :] * sign_of(k, normal)
                return carry

            lax.fori_loop(0, COMPS, mirror, 0)

        @pl.when(place == count - 1)
        def _():
            def mirror(k, carry):
                for j in range(3):
                    high[k, pl.ds(8 * j, 8), :] = inner[k, pl.ds(ROWS - 8 - 8 * j, 8), :] * sign_of(
                        k, normal
                    )
                return carry

            lax.fori_loop(0, COMPS, mirror, 0)

    def planes(low, inner, high):
        def load(k):
            return jnp.concatenate(
                [low[k].reshape(3, 8, CZ), inner[k].reshape(8, 8, CZ), high[k].reshape(3, 8, CZ)]
            )

        return load

    sends[2].wait_recv()
    sends[3].wait_recv()
    mirror_planes(ybuf, ylo, yhi, 1, gy, ny)
    faces(planes(ylo, ybuf, yhi), 1, flux_y)
    @pl.when(late_low)
    def _():
        pl.semaphore_wait(late, 1)
        to_low.start()

    @pl.when(has_high)
    def _():
        to_low.wait_recv()

    @pl.when(has_low)
    def _():
        to_high.wait_recv()

    mirror_planes(rec, xlo, xhi, 0, gx, nx)
    faces(planes(xlo, rec, xhi), 0, flux_x)

    def finish(i, carry):
        change = []
        for h in range(2):
            k = 2 * i + h
            along_z = flux_z[k, pl.ds(1, 8)] - flux_z[k, pl.ds(0, 8)]
            along_y = flux_y[k, pl.ds(1, 8)] - flux_y[k, pl.ds(0, 8)]
            for j in range(8):
                turn_z[h, pl.ds(j, 8, stride=8), :] = along_z[j]
                turn_y[h, pl.ds(j, 8, stride=8), :] = along_y[j]
            change.append((flux_x[k, pl.ds(1, 8)] - flux_x[k, pl.ds(0, 8)]).reshape(ROWS, CZ))
        one = turn_z[0]
        two = turn_z[1]
        top = jnp.where(first_half, one, pltpu.roll(two, HALF, 1))
        bottom = jnp.where(first_half, pltpu.roll(one, HALF, 1), two)
        back = jnp.concatenate([top, bottom], axis=0).T
        for h in range(2):
            k = 2 * i + h
            whole = change[h] + turn_y[h] + back[ROWS * h : ROWS * h + ROWS]
            out_ref[k] = fields[k] - TIME_STEP * whole + CHEM_STEP * source[k]
        return carry

    lax.fori_loop(0, COMPS // 2, finish, 0)

    @pl.when(goes_up & jnp.logical_not(goes_early))
    def _():
        send_up()

    many = pl.ds(1, half - 1)
    if half > 1:
        pltpu.make_async_copy(rows2.at[many], rows2.at[many], s2_recv).wait()
    total = jnp.sum(rows2[...], axis=0)
    wide = jnp.broadcast_to(total, (8, LANES))
    imp_ref[...] = pltpu.roll(wide, lax.rem(LANES - rank * mine, LANES), 1)
    if half > 1:
        pltpu.make_async_copy(rows2.at[many], rows2.at[many], s2_send).wait()

    @pl.when(is_wall)
    def _():
        most = pl.ds(1, 2 * group - 1)
        pltpu.make_async_copy(contrib.at[most], contrib.at[most], s1_send).wait()

    for copy in sends[2:]:
        copy.wait_send()

    @pl.when(has_low)
    def _():
        to_low.wait_send()

    @pl.when(has_high)
    def _():
        to_high.wait_send()


def body(fields, reacting, panel_map, layer_one, layer_two, layer_three, layer_four):
    sizes = (lax.axis_size("gx"), lax.axis_size("gy"), lax.axis_size("gz"))
    nx, ny, nz = sizes
    any_spec = pl.BlockSpec(memory_space=pltpu.HBM)
    vmem_spec = pl.BlockSpec(memory_space=pltpu.VMEM)
    plane = (COMPS, ROWS, CZ)
    ghost = (COMPS, 24, CZ)
    state = (COMPS, 9, 8, CZ)
    dma = pltpu.SemaphoreType.DMA
    held = pltpu.with_memory_space_constraint
    new_fields, impulse = pl.pallas_call(
        functools.partial(kernel, sizes),
        out_shape=(
            pltpu.VMEM(plane, F32),
            pltpu.VMEM((8, LANES), F32),
        ),
        in_specs=[any_spec] * 7,
        out_specs=(vmem_spec, vmem_spec),
        scratch_shapes=[
            pltpu.VMEM(plane, F32),
            pltpu.VMEM((ROWS, CZ), jnp.int32),
            pltpu.VMEM((2, CX, CZ), jnp.int32),
            pltpu.VMEM((COMPS, H1), BF16),
            pltpu.VMEM((H2, H1), BF16),
            pltpu.VMEM((H3, H2), BF16),
            pltpu.VMEM((COMPS, H3), BF16),
            pltpu.VMEM(plane, F32),
            pltpu.VMEM(plane, F32),
            pltpu.VMEM((COMPS, HALF + 16, LANES), F32),
            pltpu.VMEM(ghost, F32),
            pltpu.VMEM(ghost, F32),
            pltpu.VMEM(ghost, F32),
            pltpu.VMEM(ghost, F32),
            pltpu.VMEM((COMPS, 8, LANES), F32),
            pltpu.VMEM((COMPS, 8, LANES), F32),
            pltpu.VMEM(state, F32),
            pltpu.VMEM(state, F32),
            pltpu.VMEM(state, F32),
            pltpu.VMEM(state, F32),
            pltpu.VMEM(state, F32),
            pltpu.VMEM((2, ROWS, CZ), F32),
            pltpu.VMEM((2, ROWS, CZ), F32),
            pltpu.VMEM((H1, CAP), BF16),
            pltpu.VMEM((H2, CAP), BF16),
            pltpu.VMEM(plane, F32),
            pltpu.VMEM((2 * ny * nz, 1, LANES), F32),
            pltpu.VMEM((nx // 2, 1, LANES), F32),
            pltpu.VMEM((4 * nz, 1, LANES), F32),
            pltpu.VMEM((1, LANES), F32),
            dma((7,)),
            dma((6,)),
            dma((6,)),
            dma(()),
            dma(()),
            dma(()),
            dma(()),
            pltpu.SemaphoreType.REGULAR,
            pltpu.SemaphoreType.REGULAR,
        ],
        compiler_params=pltpu.CompilerParams(
            collective_id=0, has_side_effects=True, vmem_limit_bytes=48 * 2**20
        ),
    )(
        held(fields.reshape(plane), pltpu.HBM),
        held(reacting.reshape(ROWS, CZ), pltpu.HBM),
        held(panel_map, pltpu.HBM),
        held(layer_one.T, pltpu.HBM),
        held(layer_two, pltpu.HBM),
        held(layer_three, pltpu.HBM),
        held(layer_four, pltpu.HBM),
    )
    own_panels = 2 * nx * nz * (CZ // PATCH) // (nx * ny * nz)
    return new_fields.reshape(fields.shape), impulse[0, :own_panels]


def solution(mesh):
    return jax.shard_map(
        body,
        mesh=mesh,
        in_specs=(
            P(None, "gx", "gy", "gz"),
            P("gx", "gy", "gz"),
            P(None, "gx", "gz"),
            P(),
            P(),
            P(),
            P(),
        ),
        out_specs=(P(None, "gx", "gy", "gz"), P(("gx", "gy", "gz"))),
        check_vma=False,
    )
```

```python
import functools
import math

import jax
import jax.numpy as jnp
from jax import lax
from jax.experimental import pallas as pl
from jax.experimental.pallas import tpu as pltpu
from jax.sharding import PartitionSpec as P

COMPS = 12
CX = 8
CY = 8
CZ = 128
ROWS = CX * CY
HALF = CZ // 2
CAP = 256
H1 = 1600
H2 = 800
H3 = 400
PATCH = 8
LANES = 128

TIME_STEP = 0.1
CHEM_STEP = 0.25
WENO_EPS = 1e-06
ALPHA = math.sqrt(12.0 / 13.0)
EPS_SCALED = WENO_EPS * 12.0 / 13.0
LOG_HEAT_HALF = 0.5 * math.log(1.4)

MESH = pl.DeviceIdType.MESH
F32 = jnp.float32
BF16 = jnp.bfloat16


def recip(x):
    r = pl.reciprocal(x, approx=True)
    return r * (2.0 - x * r)


def primitive(rho, momentum, energy):
    inv = recip(rho)
    inv = inv * (2.0 - rho * inv)
    vel = [x * inv for x in momentum]
    speed = vel[0] * vel[0] + vel[1] * vel[1] + vel[2] * vel[2]
    return jnp.log(rho), vel, jnp.log(0.4 * (energy - 0.5 * rho * speed)), inv


def weno_pair(v):
    count = v.shape[0]
    d = v[1:] - v[:-1]
    q = d[1:] - d[:-1]
    g = (q[1:] - q[:-1]) * (1.0 / 3.0)
    da = d * ALPHA
    ha = q * (0.5 * ALPHA)
    qq = q * q + EPS_SCALED
    m = count - 4
    f0 = da[1 : 1 + m] + ha[0:m]
    f1 = da[1 : 1 + m] + ha[1 : 1 + m]
    f2 = da[2 : 2 + m] - ha[2 : 2 + m]
    t0 = f0 * f0 + qq[0:m]
    t1 = f1 * f1 + qq[1 : 1 + m]
    t2 = f2 * f2 + qq[2 : 2 + m]
    a = t1 * t2
    b = t0 * t2
    c = t0 * t1
    a = a * a
    b = b * b * 6.0
    c = c * c
    u = a + c + b
    x = a * g[0:m]
    y = c * g[1 : 1 + m]
    center = v[2 : 2 + m] + q[1 : 1 + m] * (1.0 / 3.0)
    hd = d * 0.5
    n = m - 1
    low = slice(0, n)
    high = slice(1, m)
    left = (
        center[low]
        + hd[1 : 1 + n]
        - (x[low] + 1.5 * y[low]) * pl.reciprocal(u[low] + 2.0 * c[low], approx=True)
    )
    right = (
        center[high]
        - hd[3 : 3 + n]
        + (y[high] + 1.5 * x[high]) * pl.reciprocal(u[high] + 2.0 * a[high], approx=True)
    )
    return left, right


def hllc(left, right, normal, only_push=False):
    rl = jnp.exp(left[0])
    rr = jnp.exp(right[0])
    p_l = jnp.exp(left[4])
    p_r = jnp.exp(right[4])
    cl = jnp.exp(0.5 * (left[4] - left[0]) + LOG_HEAT_HALF)
    cr = jnp.exp(0.5 * (right[4] - right[0]) + LOG_HEAT_HALF)
    ul = left[1 + normal]
    ur = right[1 + normal]
    sl = jnp.minimum(ul - cl, ur - cr)
    sr = jnp.maximum(ul + cl, ur + cr)
    al = rl * (sl - ul)
    ar = rr * (sr - ur)
    s = (p_r - p_l + al * ul - ar * ur) * recip(al - ar)
    take_left = jnp.maximum(s, sl) >= 0.0

    def pick(i, j):
        return jnp.where(take_left, i, j)

    rho = pick(rl, rr)
    p = pick(p_l, p_r)
    sk = pick(sl, sr)
    a = pick(al, ar)
    beyond = pick(sl, -sr) >= 0.0
    un = pick(ul, ur)
    inv = recip(sk - s)
    pstar = p + a * (s - un)
    u_face = jnp.where(beyond, un, s)
    p_face = jnp.where(beyond, p, pstar)
    mass = jnp.where(beyond, rho, a * inv) * u_face
    push = mass * u_face + p_face
    if only_push:
        return push
    vel = [un if i == normal else pick(left[1 + i], right[1 + i]) for i in range(3)]
    energy = 2.5 * p + 0.5 * rho * (vel[0] * vel[0] + vel[1] * vel[1] + vel[2] * vel[2])
    estar = ((sk - un) * energy + pstar * s - p * un) * inv
    e_face = jnp.where(beyond, energy, estar)
    flux = [mass]
    for i in range(3):
        flux.append(push if i == normal else mass * vel[i])
    flux.append(u_face * (e_face + p_face))
    for i in range(5, COMPS):
        flux.append(mass * pick(left[i], right[i]))
    return flux


def gelu(x):
    k = math.sqrt(2.0 / math.pi)
    y = x * (x * x * (0.044715 * k) + k)
    h = 0.5 * x
    return h * jnp.tanh(y) + h


def dot_nt(a, b):
    return lax.dot_general(a, b, (((1,), (1,)), ((), ())), preferred_element_type=F32)


def dot_tn(a, b):
    return lax.dot_general(a, b, (((0,), (0,)), ((), ())), preferred_element_type=F32)


def iota(shape, dim):
    return lax.broadcasted_iota(jnp.int32, shape, dim)


def one_where(mask):
    return jnp.where(mask, 1.0, 0.0)


def kernel(
    sizes,
    fields_hbm,
    react_hbm,
    pmap_hbm,
    w1_hbm,
    w2_hbm,
    w3_hbm,
    w4_hbm,
    out_ref,
    imp_ref,
    fields,
    react,
    pmap,
    w1,
    w2,
    w3,
    w4,
    rec,
    ybuf,
    zbuf,
    xlo,
    xhi,
    ylo,
    yhi,
    zlo,
    zhi,
    st_l,
    st_r,
    flux_x,
    flux_y,
    flux_z,
    turn_y,
    turn_z,
    hid1,
    hid2,
    source,
    contrib,
    rows2,
    parts,
    own,
    load_sem,
    send_sem,
    recv_sem,
    s1_send,
    s1_recv,
    s2_send,
    s2_recv,
    ready,
    late,
):
    nx, ny, nz = sizes
    gx = lax.axis_index("gx")
    gy = lax.axis_index("gy")
    gz = lax.axis_index("gz")
    is_wall = (gy == 0) | (gy == ny - 1)
    group = ny * nz
    me = gy * nz + gz
    walls = 2 * nz
    mine = 2 * nx * nz * (CZ // PATCH) // (nx * ny * nz)

    loads = []
    for i, (src, dst) in enumerate(
        (
            (fields_hbm, fields),
            (react_hbm, react),
            (pmap_hbm, pmap),
            (w1_hbm, w1),
            (w2_hbm, w2),
            (w3_hbm, w3),
            (w4_hbm, w4),
        )
    ):
        copy = pltpu.make_async_copy(src, dst, load_sem.at[i])
        if i < 3:
            copy.start()
        loads.append(copy)

    barrier = pltpu.get_barrier_semaphore()
    around = {
        "xlo": {"gx": lax.rem(gx + nx - 1, nx)},
        "xhi": {"gx": lax.rem(gx + 1, nx)},
        "ylo": {"gy": lax.rem(gy + ny - 1, ny)},
        "yhi": {"gy": lax.rem(gy + 1, ny)},
        "zlo": {"gz": lax.rem(gz + nz - 1, nz)},
        "zhi": {"gz": lax.rem(gz + 1, nz)},
    }
    half = nx // 2
    rank = lax.rem(gx, half)
    side = gx // half
    has_low = gx > 0
    has_high = gx < nx - 1
    late_low = gx == half
    late_high = gx == half - 1

    xs = [side * half + rank, (1 - side) * half + rank]
    sides = [side, 1 - side]
    ys = [gy] + [lax.rem(gy + i, ny) for i in range(1, ny)]
    zs = [gz] + [lax.rem(gz + i, nz) for i in range(1, nz)]

    def far_first(count):
        return sorted(range(count), key=lambda i: -min(i, count - i))

    for ds in (1, 0):
        for dz in far_first(nz):
            for to_y in (0, ny - 1):

                def greet_wall(ds=ds, dz=dz, to_y=to_y):
                    pl.semaphore_signal(
                        barrier,
                        inc=1,
                        device_id={"gx": xs[ds], "gy": jnp.int32(to_y), "gz": zs[dz]},
                        device_id_type=MESH,
                    )

                if ds == 0 and dz == 0:
                    pl.when(gy != to_y)(greet_wall)
                else:
                    greet_wall()

    def greet(where):
        pl.semaphore_signal(barrier, inc=1, device_id=around[where], device_id_type=MESH)

    for where in ("ylo", "yhi", "zlo", "zhi"):
        greet(where)

    @pl.when(has_low)
    def _():
        greet("xlo")

    @pl.when(has_high & jnp.logical_not(late_high))
    def _():
        greet("xhi")

    def ranked(r):
        return side * half + r

    def greet_row(r, carry):
        pl.semaphore_signal(barrier, inc=1, device_id={"gx": ranked(r)}, device_id_type=MESH)
        return carry

    lax.fori_loop(rank + 1, half, greet_row, 0)

    slot_of = side * walls + (gy // jnp.int32(max(ny - 1, 1))) * nz + gz
    loads[0].wait()

    def send_row(r, slot):
        pltpu.make_async_remote_copy(
            src_ref=own,
            dst_ref=rows2.at[slot],
            send_sem=s2_send,
            recv_sem=s2_recv,
            device_id={"gx": ranked(r)},
            device_id_type=MESH,
        ).start()
        return 0

    loads[2].wait()

    @pl.when(is_wall)
    def _():
        low = gy == 0

        near_of = {0: [], 2: [], 4: []}
        for j in range(3):
            rho, *momentum, energy = (
                jnp.where(
                    low,
                    fields[k, pl.ds(j, CX, stride=CY), :],
                    fields[k, pl.ds(CY - 1 - j, CX, stride=CY), :],
                )
                for k in range(5)
            )
            log_rho, vel, log_pressure, _ = primitive(rho, momentum, energy)
            near_of[0].append(log_rho)
            near_of[2].append(vel[1])
            near_of[4].append(log_pressure)

        def line(k, sign):
            near = near_of[k]
            ghost = [sign * x for x in near]
            below = ghost[::-1] + near
            above = near[::-1] + ghost
            return jnp.stack([jnp.where(low, i, j) for i, j in zip(below, above)])

        left, right = {}, {}
        for k in (0, 2, 4):
            left[k], right[k] = weno_pair(line(k, -1.0 if k == 2 else 1.0))
        push = hllc(left, right, 1, only_push=True)[0] * (1.0 / (PATCH * PATCH))
        ids = jnp.where(low, pmap[0], pmap[1])
        total = jnp.zeros((2 * group, LANES), F32)
        for h in range(2):
            value = jnp.sum(push[4 * h : 4 * h + 4], axis=0, keepdims=True)
            panel = ids[4 * h : 4 * h + 1]
            owner = panel // mine
            owner_x = owner // group
            member = owner_x // half * group + owner % group
            place = owner_x % half * mine + panel % mine
            spread = jnp.where(iota((2 * group, LANES), 0) == member, value, 0.0)
            lane = one_where(iota((LANES, LANES), 0) == place).astype(BF16)
            big = spread.astype(BF16)
            small = (spread - big.astype(F32)).astype(BF16)
            total = total + dot_nt(big, lane) + dot_nt(small, lane)
        contrib[...] = total.reshape(2 * group, 1, LANES)
        parts[slot_of] = contrib[side * group + me]

    def recon_step(i, carry):
        span = pl.ds(pl.multiple_of(i * 16, 16), 16)
        rho, *momentum, energy = (fields[k, span, :] for k in range(5))
        log_rho, vel, log_pressure, inv = primitive(rho, momentum, energy)
        rec[0, span, :] = log_rho
        for k in range(3):
            rec[1 + k, span, :] = vel[k]
        rec[4, span, :] = log_pressure
        for k in range(5, COMPS):
            rec[k, span, :] = fields[k, span, :] * inv
        return carry

    waits_long = rank >= half - half // 4

    @pl.when(waits_long)
    def _():
        lax.fori_loop(0, ROWS // 16, recon_step, 0)

    linked = (
        4
        + has_high.astype(jnp.int32)
        + (has_low & jnp.logical_not(late_low)).astype(jnp.int32)
        + rank
        + is_wall.astype(jnp.int32) * (2 * group - 1)
    )
    pl.semaphore_wait(barrier, linked)
    for copy in loads[3:]:
        copy.start()

    @pl.when(late_high)
    def _():
        pl.semaphore_signal(late, inc=1, device_id=around["xhi"], device_id_type=MESH)

    @pl.when(is_wall)
    def _():
        for ds in (1, 0):
            for dy in far_first(ny):
                for dz in far_first(nz):
                    if ds or dy or dz:
                        pltpu.make_async_remote_copy(
                            src_ref=contrib.at[sides[ds] * group + ys[dy] * nz + zs[dz]],
                            dst_ref=parts.at[slot_of],
                            send_sem=s1_send,
                            recv_sem=s1_recv,
                            device_id={"gx": xs[ds], "gy": ys[dy], "gz": zs[dz]},
                            device_id_type=MESH,
                        ).start()

    def signal_row(r, carry):
        pl.semaphore_signal(ready, inc=1, device_id={"gx": ranked(r)}, device_id_type=MESH)
        return carry

    lax.fori_loop(0, rank, signal_row, 0)

    def pass_on():
        @pl.when(is_wall)
        def _():
            few = parts.at[pl.ds(0, 2 * walls - 1)]
            pltpu.make_async_copy(few, few, s1_recv).wait()

        @pl.when(jnp.logical_not(is_wall))
        def _():
            pltpu.make_async_copy(parts, parts, s1_recv).wait()

        own[...] = jnp.sum(parts[...], axis=0)
        rows2[0] = own[...]
        lax.fori_loop(0, rank, lambda r, carry: send_row(r, r - rank + half), 0)

    in_last = (rank >= half // 2) & (rank < half - half // 4)

    @pl.when(in_last)
    def _():
        pass_on()

    @pl.when(jnp.logical_not(waits_long))
    def _():
        lax.fori_loop(0, ROWS // 16, recon_step, 0)

    sends = []

    def send(i, src, dst, where):
        copy = pltpu.make_async_remote_copy(
            src_ref=src,
            dst_ref=dst,
            send_sem=send_sem.at[i],
            recv_sem=recv_sem.at[i],
            device_id=around[where],
            device_id_type=MESH,
        )
        sends.append(copy)
        return copy

    to_low = send(0, rec.at[:, pl.ds(0, 24), :], xhi, "xlo")
    to_high = send(1, rec.at[:, pl.ds(ROWS - 24, 24), :], xlo, "xhi")

    @pl.when(has_low & jnp.logical_not(late_low))
    def _():
        to_low.start()

    @pl.when(has_high)
    def _():
        to_high.start()


    def turn_to_y(k, carry):
        for y in range(CY):
            ybuf[k, pl.ds(8 * y, 8), :] = rec[k, pl.ds(y, CX, stride=CY), :]
        return carry

    lax.fori_loop(0, COMPS, turn_to_y, 0)
    send(2, ybuf.at[:, pl.ds(0, 24), :], yhi, "ylo").start()
    send(3, ybuf.at[:, pl.ds(ROWS - 24, 24), :], ylo, "yhi").start()

    first_half = iota((HALF, LANES), 1) < HALF

    def turn_to_z(i, carry):
        both = rec[pl.ds(2 * i, 2), :, :].reshape(2 * ROWS, CZ).T
        top = both[:HALF]
        bottom = both[HALF:]
        zbuf[2 * i, pl.ds(8, HALF), :] = jnp.where(first_half, top, pltpu.roll(bottom, HALF, 1))
        zbuf[2 * i + 1, pl.ds(8, HALF), :] = jnp.where(first_half, pltpu.roll(top, HALF, 1), bottom)
        return carry

    lax.fori_loop(0, COMPS // 2, turn_to_z, 0)
    send(4, zbuf.at[:, pl.ds(8, 8), :], zhi, "zlo").start()
    send(5, zbuf.at[:, pl.ds(HALF, 8), :], zlo, "zhi").start()

    loads[1].wait()
    hot = react[...] > 0
    flags = one_where(hot).astype(BF16)
    upto = one_where(iota((CZ, CZ), 0) <= iota((CZ, CZ), 1)).astype(BF16)
    within = jnp.dot(flags, upto, preferred_element_type=F32)
    sums = jnp.dot(flags, jnp.ones((CZ, CAP), BF16), preferred_element_type=F32)
    above = one_where(iota((ROWS, ROWS), 1) < iota((ROWS, ROWS), 0)).astype(BF16)
    start = jnp.dot(above, sums.astype(BF16), preferred_element_type=F32)
    slot = iota((ROWS, CAP), 1).astype(F32)
    row_hot = one_where((start <= slot) & (slot < start + sums))
    order = jnp.where(hot, start[:, :CZ] + within, 0.0).astype(BF16)
    sums_t = dot_nt(jnp.ones((CAP, CZ), BF16), flags)
    before = one_where(iota((ROWS, ROWS), 0) < iota((ROWS, ROWS), 1)).astype(BF16)
    start_t = jnp.dot(sums_t.astype(BF16), before, preferred_element_type=F32)
    slot_t = iota((CAP, ROWS), 0).astype(F32)
    row_hot_t = one_where((start_t <= slot_t) & (slot_t < start_t + sums_t)).astype(BF16)
    line_rank = jnp.dot(row_hot_t, order, preferred_element_type=F32)
    lane_hot = one_where(line_rank == iota((CAP, CZ), 0).astype(F32) + 1.0).astype(BF16)

    @pl.when((rank >= half // 4) & jnp.logical_not(in_last))
    def _():
        pass_on()

    cells = rec[...].reshape(COMPS * ROWS, CZ).astype(BF16)
    spread_cells = dot_nt(cells, lane_hot).reshape(COMPS, ROWS, CAP)
    features = jnp.sum(spread_cells * row_hot[None], axis=1).astype(BF16)

    loads[3].wait()
    hid1[...] = gelu(dot_tn(w1[...], features)).astype(BF16)
    loads[4].wait()
    hid2[...] = gelu(jnp.dot(w2[...], hid1[...], preferred_element_type=F32)).astype(BF16)
    loads[5].wait()
    loads[6].wait()
    hid3 = gelu(jnp.dot(w3[...], hid2[...], preferred_element_type=F32)).astype(BF16)
    rates = jnp.dot(w4[...], hid3, preferred_element_type=F32).astype(BF16).astype(F32)
    spread_rates = (rates[:, None, :] * row_hot[None]).reshape(COMPS * ROWS, CAP).astype(BF16)
    source[...] = jnp.dot(spread_rates, lane_hot, preferred_element_type=F32).reshape(
        COMPS, ROWS, CZ
    )

    @pl.when(rank < half // 4)
    def _():
        pass_on()

    def faces(load, normal, flux):
        def weno_step(k, carry):
            left, right = weno_pair(load(k))
            st_l[k] = left
            st_r[k] = right
            return carry

        lax.fori_loop(0, COMPS, weno_step, 0)

        def flux_step(i, carry):
            span = pl.ds(i * 3, 3)
            left = [st_l[k, span] for k in range(COMPS)]
            right = [st_r[k, span] for k in range(COMPS)]
            for k, x in enumerate(hllc(left, right, normal)):
                flux[k, span] = x
            return carry

        lax.fori_loop(0, 3, flux_step, 0)

    def sign_of(k, normal):
        return jnp.where(k == 1 + normal, -1.0, 1.0).astype(F32)

    sends[4].wait_recv()
    sends[5].wait_recv()
    first_lanes = iota((8, LANES), 1) < HALF

    def ghosts_z(k, carry):
        zbuf[k, pl.ds(0, 8), :] = pltpu.roll(
            jnp.where(first_lanes, zbuf[k, pl.ds(HALF, 8), :], zlo[k]), HALF, 1
        )
        zbuf[k, pl.ds(HALF + 8, 8), :] = pltpu.roll(
            jnp.where(first_lanes, zhi[k], zbuf[k, pl.ds(8, 8), :]), HALF, 1
        )
        return carry

    lax.fori_loop(0, COMPS, ghosts_z, 0)
    lane_low = iota((1, LANES), 1) < HALF

    @pl.when(gz == 0)
    def _():
        def mirror(k, carry):
            for j in range(3):
                here = zbuf[k, pl.ds(7 - j, 1), :]
                inside = zbuf[k, pl.ds(8 + j, 1), :] * sign_of(k, 2)
                zbuf[k, pl.ds(7 - j, 1), :] = jnp.where(lane_low, inside, here)
            return carry

        lax.fori_loop(0, COMPS, mirror, 0)

    @pl.when(gz == nz - 1)
    def _():
        def mirror(k, carry):
            for j in range(3):
                here = zbuf[k, pl.ds(HALF + 8 + j, 1), :]
                inside = zbuf[k, pl.ds(HALF + 7 - j, 1), :] * sign_of(k, 2)
                zbuf[k, pl.ds(HALF + 8 + j, 1), :] = jnp.where(lane_low, here, inside)
            return carry

        lax.fori_loop(0, COMPS, mirror, 0)

    faces(
        lambda k: jnp.stack([zbuf[k, pl.ds(5 + j, 8, stride=8), :] for j in range(14)]), 2, flux_z
    )

    def send_up():
        pl.semaphore_wait(ready, half - 1 - rank)
        lax.fori_loop(rank + 1, half, lambda r, carry: send_row(r, r - rank), 0)

    goes_up = rank < half - 1
    goes_early = rank >= half // 2

    @pl.when(goes_up & goes_early)
    def _():
        send_up()

    def mirror_planes(inner, low, high, normal, place, count):
        @pl.when(place == 0)
        def _():
            def mirror(k, carry):
                for j in range(3):
                    low[k, pl.ds(16 - 8 * j, 8), :] = inner[k, pl.ds(8 * j, 8), :] * sign_of(k, normal)
                return carry

            lax.fori_loop(0, COMPS, mirror, 0)

        @pl.when(place == count - 1)
        def _():
            def mirror(k, carry):
                for j in range(3):
                    high[k, pl.ds(8 * j, 8), :] = inner[k, pl.ds(ROWS - 8 - 8 * j, 8), :] * sign_of(
                        k, normal
                    )
                return carry

            lax.fori_loop(0, COMPS, mirror, 0)

    def planes(low, inner, high):
        def load(k):
            return jnp.concatenate(
                [low[k].reshape(3, 8, CZ), inner[k].reshape(8, 8, CZ), high[k].reshape(3, 8, CZ)]
            )

        return load

    sends[2].wait_recv()
    sends[3].wait_recv()
    mirror_planes(ybuf, ylo, yhi, 1, gy, ny)
    faces(planes(ylo, ybuf, yhi), 1, flux_y)
    @pl.when(late_low)
    def _():
        pl.semaphore_wait(late, 1)
        to_low.start()

    goes_middle = ((rank >= half // 4) & (rank < half // 2)) | (late_low & jnp.logical_not(goes_early))

    @pl.when(goes_up & goes_middle)
    def _():
        send_up()

    @pl.when(has_high)
    def _():
        to_low.wait_recv()

    @pl.when(has_low)
    def _():
        to_high.wait_recv()

    mirror_planes(rec, xlo, xhi, 0, gx, nx)
    faces(planes(xlo, rec, xhi), 0, flux_x)

    def finish(i, carry):
        change = []
        for h in range(2):
            k = 2 * i + h
            along_z = flux_z[k, pl.ds(1, 8)] - flux_z[k, pl.ds(0, 8)]
            along_y = flux_y[k, pl.ds(1, 8)] - flux_y[k, pl.ds(0, 8)]
            for j in range(8):
                turn_z[h, pl.ds(j, 8, stride=8), :] = along_z[j]
                turn_y[h, pl.ds(j, 8, stride=8), :] = along_y[j]
            change.append((flux_x[k, pl.ds(1, 8)] - flux_x[k, pl.ds(0, 8)]).reshape(ROWS, CZ))
        one = turn_z[0]
        two = turn_z[1]
        top = jnp.where(first_half, one, pltpu.roll(two, HALF, 1))
        bottom = jnp.where(first_half, pltpu.roll(one, HALF, 1), two)
        back = jnp.concatenate([top, bottom], axis=0).T
        for h in range(2):
            k = 2 * i + h
            whole = change[h] + turn_y[h] + back[ROWS * h : ROWS * h + ROWS]
            out_ref[k] = fields[k] - TIME_STEP * whole + CHEM_STEP * source[k]
        return carry

    lax.fori_loop(0, COMPS // 2, finish, 0)

    @pl.when(goes_up & jnp.logical_not(goes_early | goes_middle))
    def _():
        send_up()

    many = pl.ds(1, half - 1)
    if half > 1:
        pltpu.make_async_copy(rows2.at[many], rows2.at[many], s2_recv).wait()
    total = jnp.sum(rows2[...], axis=0)
    wide = jnp.broadcast_to(total, (8, LANES))
    imp_ref[...] = pltpu.roll(wide, lax.rem(LANES - rank * mine, LANES), 1)
    if half > 1:
        pltpu.make_async_copy(rows2.at[many], rows2.at[many], s2_send).wait()

    @pl.when(is_wall)
    def _():
        most = pl.ds(1, 2 * group - 1)
        pltpu.make_async_copy(contrib.at[most], contrib.at[most], s1_send).wait()

    for copy in sends[2:]:
        copy.wait_send()

    @pl.when(has_low)
    def _():
        to_low.wait_send()

    @pl.when(has_high)
    def _():
        to_high.wait_send()


def body(fields, reacting, panel_map, layer_one, layer_two, layer_three, layer_four):
    sizes = (lax.axis_size("gx"), lax.axis_size("gy"), lax.axis_size("gz"))
    nx, ny, nz = sizes
    any_spec = pl.BlockSpec(memory_space=pltpu.HBM)
    vmem_spec = pl.BlockSpec(memory_space=pltpu.VMEM)
    plane = (COMPS, ROWS, CZ)
    ghost = (COMPS, 24, CZ)
    state = (COMPS, 9, 8, CZ)
    dma = pltpu.SemaphoreType.DMA
    held = pltpu.with_memory_space_constraint
    new_fields, impulse = pl.pallas_call(
        functools.partial(kernel, sizes),
        out_shape=(
            pltpu.VMEM(plane, F32),
            pltpu.VMEM((8, LANES), F32),
        ),
        in_specs=[any_spec] * 7,
        out_specs=(vmem_spec, vmem_spec),
        scratch_shapes=[
            pltpu.VMEM(plane, F32),
            pltpu.VMEM((ROWS, CZ), jnp.int32),
            pltpu.VMEM((2, CX, CZ), jnp.int32),
            pltpu.VMEM((COMPS, H1), BF16),
            pltpu.VMEM((H2, H1), BF16),
            pltpu.VMEM((H3, H2), BF16),
            pltpu.VMEM((COMPS, H3), BF16),
            pltpu.VMEM(plane, F32),
            pltpu.VMEM(plane, F32),
            pltpu.VMEM((COMPS, HALF + 16, LANES), F32),
            pltpu.VMEM(ghost, F32),
            pltpu.VMEM(ghost, F32),
            pltpu.VMEM(ghost, F32),
            pltpu.VMEM(ghost, F32),
            pltpu.VMEM((COMPS, 8, LANES), F32),
            pltpu.VMEM((COMPS, 8, LANES), F32),
            pltpu.VMEM(state, F32),
            pltpu.VMEM(state, F32),
            pltpu.VMEM(state, F32),
            pltpu.VMEM(state, F32),
            pltpu.VMEM(state, F32),
            pltpu.VMEM((2, ROWS, CZ), F32),
            pltpu.VMEM((2, ROWS, CZ), F32),
            pltpu.VMEM((H1, CAP), BF16),
            pltpu.VMEM((H2, CAP), BF16),
            pltpu.VMEM(plane, F32),
            pltpu.VMEM((2 * ny * nz, 1, LANES), F32),
            pltpu.VMEM((nx // 2, 1, LANES), F32),
            pltpu.VMEM((4 * nz, 1, LANES), F32),
            pltpu.VMEM((1, LANES), F32),
            dma((7,)),
            dma((6,)),
            dma((6,)),
            dma(()),
            dma(()),
            dma(()),
            dma(()),
            pltpu.SemaphoreType.REGULAR,
            pltpu.SemaphoreType.REGULAR,
        ],
        compiler_params=pltpu.CompilerParams(
            collective_id=0, has_side_effects=True, vmem_limit_bytes=48 * 2**20
        ),
    )(
        held(fields.reshape(plane), pltpu.HBM),
        held(reacting.reshape(ROWS, CZ), pltpu.HBM),
        held(panel_map, pltpu.HBM),
        held(layer_one.T, pltpu.HBM),
        held(layer_two, pltpu.HBM),
        held(layer_three, pltpu.HBM),
        held(layer_four, pltpu.HBM),
    )
    own_panels = 2 * nx * nz * (CZ // PATCH) // (nx * ny * nz)
    return new_fields.reshape(fields.shape), impulse[0, :own_panels]


def solution(mesh):
    return jax.shard_map(
        body,
        mesh=mesh,
        in_specs=(
            P(None, "gx", "gy", "gz"),
            P("gx", "gy", "gz"),
            P(None, "gx", "gz"),
            P(),
            P(),
            P(),
            P(),
        ),
        out_specs=(P(None, "gx", "gy", "gz"), P(("gx", "gy", "gz"))),
        check_vma=False,
    )
```

```python
import functools
import math

import jax
import jax.numpy as jnp
from jax import lax
from jax.experimental import pallas as pl
from jax.experimental.pallas import tpu as pltpu
from jax.sharding import PartitionSpec as P

COMPS = 12
CX = 8
CY = 8
CZ = 128
ROWS = CX * CY
HALF = CZ // 2
CAP = 256
H1 = 1600
H2 = 800
H3 = 400
PATCH = 8
LANES = 128

TIME_STEP = 0.1
CHEM_STEP = 0.25
WENO_EPS = 1e-06
ALPHA = math.sqrt(12.0 / 13.0)
EPS_SCALED = WENO_EPS * 12.0 / 13.0
LOG_HEAT_HALF = 0.5 * math.log(1.4)

MESH = pl.DeviceIdType.MESH
F32 = jnp.float32
BF16 = jnp.bfloat16


def recip(x):
    r = pl.reciprocal(x, approx=True)
    return r * (2.0 - x * r)


def primitive(rho, momentum, energy):
    inv = recip(rho)
    inv = inv * (2.0 - rho * inv)
    vel = [x * inv for x in momentum]
    speed = vel[0] * vel[0] + vel[1] * vel[1] + vel[2] * vel[2]
    return jnp.log(rho), vel, jnp.log(0.4 * (energy - 0.5 * rho * speed)), inv


def weno_pair(v):
    count = v.shape[0]
    d = v[1:] - v[:-1]
    q = d[1:] - d[:-1]
    g = (q[1:] - q[:-1]) * (1.0 / 3.0)
    da = d * ALPHA
    ha = q * (0.5 * ALPHA)
    qq = q * q + EPS_SCALED
    m = count - 4
    f0 = da[1 : 1 + m] + ha[0:m]
    f1 = da[1 : 1 + m] + ha[1 : 1 + m]
    f2 = da[2 : 2 + m] - ha[2 : 2 + m]
    t0 = f0 * f0 + qq[0:m]
    t1 = f1 * f1 + qq[1 : 1 + m]
    t2 = f2 * f2 + qq[2 : 2 + m]
    a = t1 * t2
    b = t0 * t2
    c = t0 * t1
    a = a * a
    b = b * b * 6.0
    c = c * c
    u = a + c + b
    x = a * g[0:m]
    y = c * g[1 : 1 + m]
    center = v[2 : 2 + m] + q[1 : 1 + m] * (1.0 / 3.0)
    hd = d * 0.5
    n = m - 1
    low = slice(0, n)
    high = slice(1, m)
    left = (
        center[low]
        + hd[1 : 1 + n]
        - (x[low] + 1.5 * y[low]) * pl.reciprocal(u[low] + 2.0 * c[low], approx=True)
    )
    right = (
        center[high]
        - hd[3 : 3 + n]
        + (y[high] + 1.5 * x[high]) * pl.reciprocal(u[high] + 2.0 * a[high], approx=True)
    )
    return left, right


def hllc(left, right, normal, only_push=False):
    rl = jnp.exp(left[0])
    rr = jnp.exp(right[0])
    p_l = jnp.exp(left[4])
    p_r = jnp.exp(right[4])
    cl = jnp.exp(0.5 * (left[4] - left[0]) + LOG_HEAT_HALF)
    cr = jnp.exp(0.5 * (right[4] - right[0]) + LOG_HEAT_HALF)
    ul = left[1 + normal]
    ur = right[1 + normal]
    sl = jnp.minimum(ul - cl, ur - cr)
    sr = jnp.maximum(ul + cl, ur + cr)
    al = rl * (sl - ul)
    ar = rr * (sr - ur)
    s = (p_r - p_l + al * ul - ar * ur) * recip(al - ar)
    take_left = jnp.maximum(s, sl) >= 0.0

    def pick(i, j):
        return jnp.where(take_left, i, j)

    rho = pick(rl, rr)
    p = pick(p_l, p_r)
    sk = pick(sl, sr)
    a = pick(al, ar)
    beyond = pick(sl, -sr) >= 0.0
    un = pick(ul, ur)
    inv = recip(sk - s)
    pstar = p + a * (s - un)
    u_face = jnp.where(beyond, un, s)
    p_face = jnp.where(beyond, p, pstar)
    mass = jnp.where(beyond, rho, a * inv) * u_face
    push = mass * u_face + p_face
    if only_push:
        return push
    vel = [un if i == normal else pick(left[1 + i], right[1 + i]) for i in range(3)]
    energy = 2.5 * p + 0.5 * rho * (vel[0] * vel[0] + vel[1] * vel[1] + vel[2] * vel[2])
    estar = ((sk - un) * energy + pstar * s - p * un) * inv
    e_face = jnp.where(beyond, energy, estar)
    flux = [mass]
    for i in range(3):
        flux.append(push if i == normal else mass * vel[i])
    flux.append(u_face * (e_face + p_face))
    for i in range(5, COMPS):
        flux.append(mass * pick(left[i], right[i]))
    return flux


def gelu(x):
    k = math.sqrt(2.0 / math.pi)
    y = x * (x * x * (0.044715 * k) + k)
    h = 0.5 * x
    return h * jnp.tanh(y) + h


def dot_nt(a, b):
    return lax.dot_general(a, b, (((1,), (1,)), ((), ())), preferred_element_type=F32)


def dot_tn(a, b):
    return lax.dot_general(a, b, (((0,), (0,)), ((), ())), preferred_element_type=F32)


def iota(shape, dim):
    return lax.broadcasted_iota(jnp.int32, shape, dim)


def one_where(mask):
    return jnp.where(mask, 1.0, 0.0)


def kernel(
    sizes,
    fields_hbm,
    react_hbm,
    pmap_hbm,
    w1_hbm,
    w2_hbm,
    w3_hbm,
    w4_hbm,
    out_ref,
    imp_ref,
    fields,
    react,
    pmap,
    w1,
    w2,
    w3,
    w4,
    rec,
    ybuf,
    zbuf,
    xlo,
    xhi,
    ylo,
    yhi,
    zlo,
    zhi,
    st_l,
    st_r,
    flux_x,
    flux_y,
    flux_z,
    turn_y,
    turn_z,
    hid1,
    hid2,
    source,
    contrib,
    rows2,
    parts,
    direct,
    own,
    load_sem,
    send_sem,
    recv_sem,
    s1_send,
    s1_recv,
    s2_send,
    s2_recv,
    ready,
    late,
    d_send,
    d_recv,
):
    nx, ny, nz = sizes
    gx = lax.axis_index("gx")
    gy = lax.axis_index("gy")
    gz = lax.axis_index("gz")
    is_wall = (gy == 0) | (gy == ny - 1)
    group = ny * nz
    me = gy * nz + gz
    walls = 2 * nz
    mine = 2 * nx * nz * (CZ // PATCH) // (nx * ny * nz)

    loads = []
    for i, (src, dst) in enumerate(
        (
            (fields_hbm, fields),
            (react_hbm, react),
            (pmap_hbm, pmap),
            (w1_hbm, w1),
            (w2_hbm, w2),
            (w3_hbm, w3),
            (w4_hbm, w4),
        )
    ):
        copy = pltpu.make_async_copy(src, dst, load_sem.at[i])
        if i < 3:
            copy.start()
        loads.append(copy)

    barrier = pltpu.get_barrier_semaphore()
    around = {
        "xlo": {"gx": lax.rem(gx + nx - 1, nx)},
        "xhi": {"gx": lax.rem(gx + 1, nx)},
        "ylo": {"gy": lax.rem(gy + ny - 1, ny)},
        "yhi": {"gy": lax.rem(gy + 1, ny)},
        "zlo": {"gz": lax.rem(gz + nz - 1, nz)},
        "zhi": {"gz": lax.rem(gz + 1, nz)},
    }
    half = nx // 2
    rank = lax.rem(gx, half)
    side = gx // half
    has_low = gx > 0
    has_high = gx < nx - 1
    late_low = gx == half
    late_high = gx == half - 1

    xs = [side * half + rank, (1 - side) * half + rank]
    sides = [side, 1 - side]
    ys = [gy] + [lax.rem(gy + i, ny) for i in range(1, ny)]
    zs = [gz] + [lax.rem(gz + i, nz) for i in range(1, nz)]

    def far_first(count):
        return sorted(range(count), key=lambda i: -min(i, count - i))

    for ds in (1, 0):
        for dz in far_first(nz):
            for to_y in (0, ny - 1):

                def greet_wall(ds=ds, dz=dz, to_y=to_y):
                    pl.semaphore_signal(
                        barrier,
                        inc=1,
                        device_id={"gx": xs[ds], "gy": jnp.int32(to_y), "gz": zs[dz]},
                        device_id_type=MESH,
                    )

                if ds == 0 and dz == 0:
                    pl.when(gy != to_y)(greet_wall)
                else:
                    greet_wall()

    def greet(where):
        pl.semaphore_signal(barrier, inc=1, device_id=around[where], device_id_type=MESH)

    for where in ("ylo", "yhi", "zlo", "zhi"):
        greet(where)

    @pl.when(has_low)
    def _():
        greet("xlo")

    @pl.when(has_high & jnp.logical_not(late_high))
    def _():
        greet("xhi")

    firsts = half // 8
    last_at = half // 2
    lasts = half // 4 if firsts else 0
    is_first = rank < firsts
    in_last = (rank >= last_at) & (rank < half - half // 4)

    if firsts:

        @pl.when(is_first)
        def _():
            def greet_last(i, carry):
                to_x = (i % 2) * half + last_at + i // 4
                to_y = (i // 2 % 2) * (ny - 1)
                for to_z in range(nz):
                    pl.semaphore_signal(
                        barrier,
                        inc=1,
                        device_id={"gx": to_x, "gy": to_y, "gz": jnp.int32(to_z)},
                        device_id_type=MESH,
                    )
                return carry

            lax.fori_loop(0, lasts * 4, greet_last, 0)

    def ranked(r):
        return side * half + r

    def greet_row(r, carry):
        pl.semaphore_signal(barrier, inc=1, device_id={"gx": ranked(r)}, device_id_type=MESH)
        return carry

    lax.fori_loop(rank + 1, half, greet_row, 0)

    slot_of = side * walls + (gy // jnp.int32(max(ny - 1, 1))) * nz + gz
    loads[0].wait()

    def send_row(r, slot):
        pltpu.make_async_remote_copy(
            src_ref=own,
            dst_ref=rows2.at[slot],
            send_sem=s2_send,
            recv_sem=s2_recv,
            device_id={"gx": ranked(r)},
            device_id_type=MESH,
        ).start()
        return 0

    loads[2].wait()

    @pl.when(is_wall)
    def _():
        low = gy == 0

        near_of = {0: [], 2: [], 4: []}
        for j in range(3):
            rho, *momentum, energy = (
                jnp.where(
                    low,
                    fields[k, pl.ds(j, CX, stride=CY), :],
                    fields[k, pl.ds(CY - 1 - j, CX, stride=CY), :],
                )
                for k in range(5)
            )
            log_rho, vel, log_pressure, _ = primitive(rho, momentum, energy)
            near_of[0].append(log_rho)
            near_of[2].append(vel[1])
            near_of[4].append(log_pressure)

        def line(k, sign):
            near = near_of[k]
            ghost = [sign * x for x in near]
            below = ghost[::-1] + near
            above = near[::-1] + ghost
            return jnp.stack([jnp.where(low, i, j) for i, j in zip(below, above)])

        left, right = {}, {}
        for k in (0, 2, 4):
            left[k], right[k] = weno_pair(line(k, -1.0 if k == 2 else 1.0))
        push = hllc(left, right, 1, only_push=True)[0] * (1.0 / (PATCH * PATCH))
        ids = jnp.where(low, pmap[0], pmap[1])
        total = jnp.zeros((2 * group, LANES), F32)
        for h in range(2):
            value = jnp.sum(push[4 * h : 4 * h + 4], axis=0, keepdims=True)
            panel = ids[4 * h : 4 * h + 1]
            owner = panel // mine
            owner_x = owner // group
            member = owner_x // half * group + owner % group
            place = owner_x % half * mine + panel % mine
            spread = jnp.where(iota((2 * group, LANES), 0) == member, value, 0.0)
            lane = one_where(iota((LANES, LANES), 0) == place).astype(BF16)
            big = spread.astype(BF16)
            small = (spread - big.astype(F32)).astype(BF16)
            total = total + dot_nt(big, lane) + dot_nt(small, lane)
        contrib[...] = total.reshape(2 * group, 1, LANES)
        parts[slot_of] = contrib[side * group + me]

    def recon_step(i, carry):
        span = pl.ds(pl.multiple_of(i * 16, 16), 16)
        rho, *momentum, energy = (fields[k, span, :] for k in range(5))
        log_rho, vel, log_pressure, inv = primitive(rho, momentum, energy)
        rec[0, span, :] = log_rho
        for k in range(3):
            rec[1 + k, span, :] = vel[k]
        rec[4, span, :] = log_pressure
        for k in range(5, COMPS):
            rec[k, span, :] = fields[k, span, :] * inv
        return carry

    waits_long = rank >= half - half // 4

    @pl.when(waits_long)
    def _():
        lax.fori_loop(0, ROWS // 16, recon_step, 0)

    linked = (
        4
        + has_high.astype(jnp.int32)
        + (has_low & jnp.logical_not(late_low)).astype(jnp.int32)
        + rank
        + is_wall.astype(jnp.int32) * (2 * group - 1)
        + (is_wall & in_last).astype(jnp.int32) * (firsts * 2 * group)
    )
    pl.semaphore_wait(barrier, linked)
    for copy in loads[3:]:
        copy.start()

    @pl.when(late_high)
    def _():
        pl.semaphore_signal(late, inc=1, device_id=around["xhi"], device_id_type=MESH)

    @pl.when(is_wall)
    def _():
        for ds in (1, 0):
            for dy in far_first(ny):
                for dz in far_first(nz):
                    if ds or dy or dz:
                        pltpu.make_async_remote_copy(
                            src_ref=contrib.at[sides[ds] * group + ys[dy] * nz + zs[dz]],
                            dst_ref=parts.at[slot_of],
                            send_sem=s1_send,
                            recv_sem=s1_recv,
                            device_id={"gx": xs[ds], "gy": ys[dy], "gz": zs[dz]},
                            device_id_type=MESH,
                        ).start()

    if firsts:

        @pl.when(is_wall & in_last)
        def _():
            def send_direct(i, carry):
                to_side = i // ny % 2
                to_y = i % ny
                for to_z in range(nz):
                    pltpu.make_async_remote_copy(
                        src_ref=contrib.at[to_side * group + to_y * nz + to_z],
                        dst_ref=direct.at[(rank - last_at) * 2 * walls + slot_of],
                        send_sem=d_send,
                        recv_sem=d_recv,
                        device_id={
                            "gx": to_side * half + i // (2 * ny),
                            "gy": to_y,
                            "gz": jnp.int32(to_z),
                        },
                        device_id_type=MESH,
                    ).start()
                return carry

            lax.fori_loop(0, firsts * 2 * ny, send_direct, 0)

    def signal_row(r, carry):
        pl.semaphore_signal(ready, inc=1, device_id={"gx": ranked(r)}, device_id_type=MESH)
        return carry

    lax.fori_loop(0, rank, signal_row, 0)

    def pass_on():
        @pl.when(is_wall)
        def _():
            few = parts.at[pl.ds(0, 2 * walls - 1)]
            pltpu.make_async_copy(few, few, s1_recv).wait()

        @pl.when(jnp.logical_not(is_wall))
        def _():
            pltpu.make_async_copy(parts, parts, s1_recv).wait()

        own[...] = jnp.sum(parts[...], axis=0)
        rows2[0] = own[...]
        first = jnp.where(in_last, firsts, 0)
        lax.fori_loop(first, rank, lambda r, carry: send_row(r, r - rank + half), 0)

    @pl.when(in_last)
    def _():
        pass_on()

    @pl.when(jnp.logical_not(waits_long))
    def _():
        lax.fori_loop(0, ROWS // 16, recon_step, 0)

    sends = []

    def send(i, src, dst, where):
        copy = pltpu.make_async_remote_copy(
            src_ref=src,
            dst_ref=dst,
            send_sem=send_sem.at[i],
            recv_sem=recv_sem.at[i],
            device_id=around[where],
            device_id_type=MESH,
        )
        sends.append(copy)
        return copy

    to_low = send(0, rec.at[:, pl.ds(0, 24), :], xhi, "xlo")
    to_high = send(1, rec.at[:, pl.ds(ROWS - 24, 24), :], xlo, "xhi")

    @pl.when(has_low & jnp.logical_not(late_low))
    def _():
        to_low.start()

    @pl.when(has_high)
    def _():
        to_high.start()


    def turn_to_y(k, carry):
        for y in range(CY):
            ybuf[k, pl.ds(8 * y, 8), :] = rec[k, pl.ds(y, CX, stride=CY), :]
        return carry

    lax.fori_loop(0, COMPS, turn_to_y, 0)
    send(2, ybuf.at[:, pl.ds(0, 24), :], yhi, "ylo").start()
    send(3, ybuf.at[:, pl.ds(ROWS - 24, 24), :], ylo, "yhi").start()

    first_half = iota((HALF, LANES), 1) < HALF

    def turn_to_z(i, carry):
        both = rec[pl.ds(2 * i, 2), :, :].reshape(2 * ROWS, CZ).T
        top = both[:HALF]
        bottom = both[HALF:]
        zbuf[2 * i, pl.ds(8, HALF), :] = jnp.where(first_half, top, pltpu.roll(bottom, HALF, 1))
        zbuf[2 * i + 1, pl.ds(8, HALF), :] = jnp.where(first_half, pltpu.roll(top, HALF, 1), bottom)
        return carry

    lax.fori_loop(0, COMPS // 2, turn_to_z, 0)
    send(4, zbuf.at[:, pl.ds(8, 8), :], zhi, "zlo").start()
    send(5, zbuf.at[:, pl.ds(HALF, 8), :], zlo, "zhi").start()

    loads[1].wait()
    hot = react[...] > 0
    flags = one_where(hot).astype(BF16)
    upto = one_where(iota((CZ, CZ), 0) <= iota((CZ, CZ), 1)).astype(BF16)
    within = jnp.dot(flags, upto, preferred_element_type=F32)
    sums = jnp.dot(flags, jnp.ones((CZ, CAP), BF16), preferred_element_type=F32)
    above = one_where(iota((ROWS, ROWS), 1) < iota((ROWS, ROWS), 0)).astype(BF16)
    start = jnp.dot(above, sums.astype(BF16), preferred_element_type=F32)
    slot = iota((ROWS, CAP), 1).astype(F32)
    row_hot = one_where((start <= slot) & (slot < start + sums))
    order = jnp.where(hot, start[:, :CZ] + within, 0.0).astype(BF16)
    sums_t = dot_nt(jnp.ones((CAP, CZ), BF16), flags)
    before = one_where(iota((ROWS, ROWS), 0) < iota((ROWS, ROWS), 1)).astype(BF16)
    start_t = jnp.dot(sums_t.astype(BF16), before, preferred_element_type=F32)
    slot_t = iota((CAP, ROWS), 0).astype(F32)
    row_hot_t = one_where((start_t <= slot_t) & (slot_t < start_t + sums_t)).astype(BF16)
    line_rank = jnp.dot(row_hot_t, order, preferred_element_type=F32)
    lane_hot = one_where(line_rank == iota((CAP, CZ), 0).astype(F32) + 1.0).astype(BF16)

    @pl.when((rank >= half // 4) & jnp.logical_not(in_last))
    def _():
        pass_on()

    cells = rec[...].reshape(COMPS * ROWS, CZ).astype(BF16)
    spread_cells = dot_nt(cells, lane_hot).reshape(COMPS, ROWS, CAP)
    features = jnp.sum(spread_cells * row_hot[None], axis=1).astype(BF16)

    loads[3].wait()
    hid1[...] = gelu(dot_tn(w1[...], features)).astype(BF16)
    loads[4].wait()
    hid2[...] = gelu(jnp.dot(w2[...], hid1[...], preferred_element_type=F32)).astype(BF16)
    loads[5].wait()
    loads[6].wait()
    hid3 = gelu(jnp.dot(w3[...], hid2[...], preferred_element_type=F32)).astype(BF16)
    rates = jnp.dot(w4[...], hid3, preferred_element_type=F32).astype(BF16).astype(F32)
    spread_rates = (rates[:, None, :] * row_hot[None]).reshape(COMPS * ROWS, CAP).astype(BF16)
    source[...] = jnp.dot(spread_rates, lane_hot, preferred_element_type=F32).reshape(
        COMPS, ROWS, CZ
    )

    @pl.when(rank < half // 4)
    def _():
        pass_on()

    def faces(load, normal, flux):
        def weno_step(k, carry):
            left, right = weno_pair(load(k))
            st_l[k] = left
            st_r[k] = right
            return carry

        lax.fori_loop(0, COMPS, weno_step, 0)

        def flux_step(i, carry):
            span = pl.ds(i * 3, 3)
            left = [st_l[k, span] for k in range(COMPS)]
            right = [st_r[k, span] for k in range(COMPS)]
            for k, x in enumerate(hllc(left, right, normal)):
                flux[k, span] = x
            return carry

        lax.fori_loop(0, 3, flux_step, 0)

    def sign_of(k, normal):
        return jnp.where(k == 1 + normal, -1.0, 1.0).astype(F32)

    sends[4].wait_recv()
    sends[5].wait_recv()
    first_lanes = iota((8, LANES), 1) < HALF

    def ghosts_z(k, carry):
        zbuf[k, pl.ds(0, 8), :] = pltpu.roll(
            jnp.where(first_lanes, zbuf[k, pl.ds(HALF, 8), :], zlo[k]), HALF, 1
        )
        zbuf[k, pl.ds(HALF + 8, 8), :] = pltpu.roll(
            jnp.where(first_lanes, zhi[k], zbuf[k, pl.ds(8, 8), :]), HALF, 1
        )
        return carry

    lax.fori_loop(0, COMPS, ghosts_z, 0)
    lane_low = iota((1, LANES), 1) < HALF

    @pl.when(gz == 0)
    def _():
        def mirror(k, carry):
            for j in range(3):
                here = zbuf[k, pl.ds(7 - j, 1), :]
                inside = zbuf[k, pl.ds(8 + j, 1), :] * sign_of(k, 2)
                zbuf[k, pl.ds(7 - j, 1), :] = jnp.where(lane_low, inside, here)
            return carry

        lax.fori_loop(0, COMPS, mirror, 0)

    @pl.when(gz == nz - 1)
    def _():
        def mirror(k, carry):
            for j in range(3):
                here = zbuf[k, pl.ds(HALF + 8 + j, 1), :]
                inside = zbuf[k, pl.ds(HALF + 7 - j, 1), :] * sign_of(k, 2)
                zbuf[k, pl.ds(HALF + 8 + j, 1), :] = jnp.where(lane_low, here, inside)
            return carry

        lax.fori_loop(0, COMPS, mirror, 0)

    faces(
        lambda k: jnp.stack([zbuf[k, pl.ds(5 + j, 8, stride=8), :] for j in range(14)]), 2, flux_z
    )

    def send_up():
        pl.semaphore_wait(ready, half - 1 - rank)
        lax.fori_loop(rank + 1, half, lambda r, carry: send_row(r, r - rank), 0)

    goes_up = rank < half - 1
    goes_early = rank >= half // 2

    @pl.when(goes_up & goes_early)
    def _():
        send_up()

    def mirror_planes(inner, low, high, normal, place, count):
        @pl.when(place == 0)
        def _():
            def mirror(k, carry):
                for j in range(3):
                    low[k, pl.ds(16 - 8 * j, 8), :] = inner[k, pl.ds(8 * j, 8), :] * sign_of(k, normal)
                return carry

            lax.fori_loop(0, COMPS, mirror, 0)

        @pl.when(place == count - 1)
        def _():
            def mirror(k, carry):
                for j in range(3):
                    high[k, pl.ds(8 * j, 8), :] = inner[k, pl.ds(ROWS - 8 - 8 * j, 8), :] * sign_of(
                        k, normal
                    )
                return carry

            lax.fori_loop(0, COMPS, mirror, 0)

    def planes(low, inner, high):
        def load(k):
            return jnp.concatenate(
                [low[k].reshape(3, 8, CZ), inner[k].reshape(8, 8, CZ), high[k].reshape(3, 8, CZ)]
            )

        return load

    sends[2].wait_recv()
    sends[3].wait_recv()
    mirror_planes(ybuf, ylo, yhi, 1, gy, ny)
    faces(planes(ylo, ybuf, yhi), 1, flux_y)
    @pl.when(late_low)
    def _():
        pl.semaphore_wait(late, 1)
        to_low.start()

    goes_middle = ((rank >= half // 4) & (rank < half // 2)) | (late_low & jnp.logical_not(goes_early))

    @pl.when(goes_up & goes_middle)
    def _():
        send_up()

    @pl.when(has_high)
    def _():
        to_low.wait_recv()

    @pl.when(has_low)
    def _():
        to_high.wait_recv()

    mirror_planes(rec, xlo, xhi, 0, gx, nx)
    faces(planes(xlo, rec, xhi), 0, flux_x)

    def finish(i, carry):
        change = []
        for h in range(2):
            k = 2 * i + h
            along_z = flux_z[k, pl.ds(1, 8)] - flux_z[k, pl.ds(0, 8)]
            along_y = flux_y[k, pl.ds(1, 8)] - flux_y[k, pl.ds(0, 8)]
            for j in range(8):
                turn_z[h, pl.ds(j, 8, stride=8), :] = along_z[j]
                turn_y[h, pl.ds(j, 8, stride=8), :] = along_y[j]
            change.append((flux_x[k, pl.ds(1, 8)] - flux_x[k, pl.ds(0, 8)]).reshape(ROWS, CZ))
        one = turn_z[0]
        two = turn_z[1]
        top = jnp.where(first_half, one, pltpu.roll(two, HALF, 1))
        bottom = jnp.where(first_half, pltpu.roll(one, HALF, 1), two)
        back = jnp.concatenate([top, bottom], axis=0).T
        for h in range(2):
            k = 2 * i + h
            whole = change[h] + turn_y[h] + back[ROWS * h : ROWS * h + ROWS]
            out_ref[k] = fields[k] - TIME_STEP * whole + CHEM_STEP * source[k]
        return carry

    lax.fori_loop(0, COMPS // 2, finish, 0)

    @pl.when(goes_up & jnp.logical_not(goes_early | goes_middle))
    def _():
        send_up()

    many = pl.ds(1, half - 1)
    if firsts:

        @pl.when(is_first)
        def _():
            for i in range(lasts):
                rows2[rank + half - last_at - i] = jnp.zeros((1, LANES), F32)
            some = pl.ds(1, half - 1 - lasts)
            pltpu.make_async_copy(rows2.at[some], rows2.at[some], s2_recv).wait()
            pltpu.make_async_copy(direct, direct, d_recv).wait()
            rows2[0] += jnp.sum(direct[...], axis=0)

        @pl.when(jnp.logical_not(is_first))
        def _():
            pltpu.make_async_copy(rows2.at[many], rows2.at[many], s2_recv).wait()

    elif half > 1:
        pltpu.make_async_copy(rows2.at[many], rows2.at[many], s2_recv).wait()
    total = jnp.sum(rows2[...], axis=0)
    wide = jnp.broadcast_to(total, (8, LANES))
    imp_ref[...] = pltpu.roll(wide, lax.rem(LANES - rank * mine, LANES), 1)
    if firsts:

        @pl.when(in_last)
        def _():
            some = pl.ds(1, half - 1 - firsts)
            pltpu.make_async_copy(rows2.at[some], rows2.at[some], s2_send).wait()

        @pl.when(jnp.logical_not(in_last))
        def _():
            pltpu.make_async_copy(rows2.at[many], rows2.at[many], s2_send).wait()

        @pl.when(is_wall & in_last)
        def _():
            every = pl.ds(0, 2 * group)

            def sent(i, carry):
                pltpu.make_async_copy(contrib.at[every], contrib.at[every], d_send).wait()
                return carry

            lax.fori_loop(0, firsts, sent, 0)

    elif half > 1:
        pltpu.make_async_copy(rows2.at[many], rows2.at[many], s2_send).wait()

    @pl.when(is_wall)
    def _():
        most = pl.ds(1, 2 * group - 1)
        pltpu.make_async_copy(contrib.at[most], contrib.at[most], s1_send).wait()

    for copy in sends[2:]:
        copy.wait_send()

    @pl.when(has_low)
    def _():
        to_low.wait_send()

    @pl.when(has_high)
    def _():
        to_high.wait_send()


def body(fields, reacting, panel_map, layer_one, layer_two, layer_three, layer_four):
    sizes = (lax.axis_size("gx"), lax.axis_size("gy"), lax.axis_size("gz"))
    nx, ny, nz = sizes
    any_spec = pl.BlockSpec(memory_space=pltpu.HBM)
    vmem_spec = pl.BlockSpec(memory_space=pltpu.VMEM)
    plane = (COMPS, ROWS, CZ)
    ghost = (COMPS, 24, CZ)
    state = (COMPS, 9, 8, CZ)
    dma = pltpu.SemaphoreType.DMA
    held = pltpu.with_memory_space_constraint
    new_fields, impulse = pl.pallas_call(
        functools.partial(kernel, sizes),
        out_shape=(
            pltpu.VMEM(plane, F32),
            pltpu.VMEM((8, LANES), F32),
        ),
        in_specs=[any_spec] * 7,
        out_specs=(vmem_spec, vmem_spec),
        scratch_shapes=[
            pltpu.VMEM(plane, F32),
            pltpu.VMEM((ROWS, CZ), jnp.int32),
            pltpu.VMEM((2, CX, CZ), jnp.int32),
            pltpu.VMEM((COMPS, H1), BF16),
            pltpu.VMEM((H2, H1), BF16),
            pltpu.VMEM((H3, H2), BF16),
            pltpu.VMEM((COMPS, H3), BF16),
            pltpu.VMEM(plane, F32),
            pltpu.VMEM(plane, F32),
            pltpu.VMEM((COMPS, HALF + 16, LANES), F32),
            pltpu.VMEM(ghost, F32),
            pltpu.VMEM(ghost, F32),
            pltpu.VMEM(ghost, F32),
            pltpu.VMEM(ghost, F32),
            pltpu.VMEM((COMPS, 8, LANES), F32),
            pltpu.VMEM((COMPS, 8, LANES), F32),
            pltpu.VMEM(state, F32),
            pltpu.VMEM(state, F32),
            pltpu.VMEM(state, F32),
            pltpu.VMEM(state, F32),
            pltpu.VMEM(state, F32),
            pltpu.VMEM((2, ROWS, CZ), F32),
            pltpu.VMEM((2, ROWS, CZ), F32),
            pltpu.VMEM((H1, CAP), BF16),
            pltpu.VMEM((H2, CAP), BF16),
            pltpu.VMEM(plane, F32),
            pltpu.VMEM((2 * ny * nz, 1, LANES), F32),
            pltpu.VMEM((nx // 2, 1, LANES), F32),
            pltpu.VMEM((4 * nz, 1, LANES), F32),
            pltpu.VMEM((max(nx // 8, 1) * 4 * nz, 1, LANES), F32),
            pltpu.VMEM((1, LANES), F32),
            dma((7,)),
            dma((6,)),
            dma((6,)),
            dma(()),
            dma(()),
            dma(()),
            dma(()),
            pltpu.SemaphoreType.REGULAR,
            pltpu.SemaphoreType.REGULAR,
            dma(()),
            dma(()),
        ],
        compiler_params=pltpu.CompilerParams(
            collective_id=0, has_side_effects=True, vmem_limit_bytes=48 * 2**20
        ),
    )(
        held(fields.reshape(plane), pltpu.HBM),
        held(reacting.reshape(ROWS, CZ), pltpu.HBM),
        held(panel_map, pltpu.HBM),
        held(layer_one.T, pltpu.HBM),
        held(layer_two, pltpu.HBM),
        held(layer_three, pltpu.HBM),
        held(layer_four, pltpu.HBM),
    )
    own_panels = 2 * nx * nz * (CZ // PATCH) // (nx * ny * nz)
    return new_fields.reshape(fields.shape), impulse[0, :own_panels]


def solution(mesh):
    return jax.shard_map(
        body,
        mesh=mesh,
        in_specs=(
            P(None, "gx", "gy", "gz"),
            P("gx", "gy", "gz"),
            P(None, "gx", "gz"),
            P(),
            P(),
            P(),
            P(),
        ),
        out_specs=(P(None, "gx", "gy", "gz"), P(("gx", "gy", "gz"))),
        check_vma=False,
    )
```

```python
import functools
import math

import jax
import jax.numpy as jnp
from jax import lax
from jax.experimental import pallas as pl
from jax.experimental.pallas import tpu as pltpu
from jax.sharding import PartitionSpec as P

COMPS = 12
CX = 8
CY = 8
CZ = 128
ROWS = CX * CY
HALF = CZ // 2
CAP = 256
H1 = 1600
H2 = 800
H3 = 400
PATCH = 8
LANES = 128

TIME_STEP = 0.1
CHEM_STEP = 0.25
WENO_EPS = 1e-06
ALPHA = math.sqrt(12.0 / 13.0)
EPS_SCALED = WENO_EPS * 12.0 / 13.0
LOG_HEAT_HALF = 0.5 * math.log(1.4)

MESH = pl.DeviceIdType.MESH
F32 = jnp.float32
BF16 = jnp.bfloat16


def recip(x):
    r = pl.reciprocal(x, approx=True)
    return r * (2.0 - x * r)


def primitive(rho, momentum, energy):
    inv = recip(rho)
    inv = inv * (2.0 - rho * inv)
    vel = [x * inv for x in momentum]
    speed = vel[0] * vel[0] + vel[1] * vel[1] + vel[2] * vel[2]
    return jnp.log(rho), vel, jnp.log(0.4 * (energy - 0.5 * rho * speed)), inv


def weno_pair(v):
    count = v.shape[0]
    d = v[1:] - v[:-1]
    q = d[1:] - d[:-1]
    g = (q[1:] - q[:-1]) * (1.0 / 3.0)
    da = d * ALPHA
    ha = q * (0.5 * ALPHA)
    qq = q * q + EPS_SCALED
    m = count - 4
    f0 = da[1 : 1 + m] + ha[0:m]
    f1 = da[1 : 1 + m] + ha[1 : 1 + m]
    f2 = da[2 : 2 + m] - ha[2 : 2 + m]
    t0 = f0 * f0 + qq[0:m]
    t1 = f1 * f1 + qq[1 : 1 + m]
    t2 = f2 * f2 + qq[2 : 2 + m]
    a = t1 * t2
    b = t0 * t2
    c = t0 * t1
    a = a * a
    b = b * b * 6.0
    c = c * c
    u = a + c + b
    x = a * g[0:m]
    y = c * g[1 : 1 + m]
    center = v[2 : 2 + m] + q[1 : 1 + m] * (1.0 / 3.0)
    hd = d * 0.5
    n = m - 1
    low = slice(0, n)
    high = slice(1, m)
    left = (
        center[low]
        + hd[1 : 1 + n]
        - (x[low] + 1.5 * y[low]) * pl.reciprocal(u[low] + 2.0 * c[low], approx=True)
    )
    right = (
        center[high]
        - hd[3 : 3 + n]
        + (y[high] + 1.5 * x[high]) * pl.reciprocal(u[high] + 2.0 * a[high], approx=True)
    )
    return left, right


def hllc(left, right, normal, only_push=False):
    rl = jnp.exp(left[0])
    rr = jnp.exp(right[0])
    p_l = jnp.exp(left[4])
    p_r = jnp.exp(right[4])
    cl = jnp.exp(0.5 * (left[4] - left[0]) + LOG_HEAT_HALF)
    cr = jnp.exp(0.5 * (right[4] - right[0]) + LOG_HEAT_HALF)
    ul = left[1 + normal]
    ur = right[1 + normal]
    sl = jnp.minimum(ul - cl, ur - cr)
    sr = jnp.maximum(ul + cl, ur + cr)
    al = rl * (sl - ul)
    ar = rr * (sr - ur)
    s = (p_r - p_l + al * ul - ar * ur) * recip(al - ar)
    take_left = jnp.maximum(s, sl) >= 0.0

    def pick(i, j):
        return jnp.where(take_left, i, j)

    rho = pick(rl, rr)
    p = pick(p_l, p_r)
    sk = pick(sl, sr)
    a = pick(al, ar)
    beyond = pick(sl, -sr) >= 0.0
    un = pick(ul, ur)
    inv = recip(sk - s)
    pstar = p + a * (s - un)
    u_face = jnp.where(beyond, un, s)
    p_face = jnp.where(beyond, p, pstar)
    mass = jnp.where(beyond, rho, a * inv) * u_face
    push = mass * u_face + p_face
    if only_push:
        return push
    vel = [un if i == normal else pick(left[1 + i], right[1 + i]) for i in range(3)]
    energy = 2.5 * p + 0.5 * rho * (vel[0] * vel[0] + vel[1] * vel[1] + vel[2] * vel[2])
    estar = ((sk - un) * energy + pstar * s - p * un) * inv
    e_face = jnp.where(beyond, energy, estar)
    flux = [mass]
    for i in range(3):
        flux.append(push if i == normal else mass * vel[i])
    flux.append(u_face * (e_face + p_face))
    for i in range(5, COMPS):
        flux.append(mass * pick(left[i], right[i]))
    return flux


def gelu(x):
    k = math.sqrt(2.0 / math.pi)
    y = x * (x * x * (0.044715 * k) + k)
    h = 0.5 * x
    return h * jnp.tanh(y) + h


def dot_nt(a, b):
    return lax.dot_general(a, b, (((1,), (1,)), ((), ())), preferred_element_type=F32)


def dot_tn(a, b):
    return lax.dot_general(a, b, (((0,), (0,)), ((), ())), preferred_element_type=F32)


def iota(shape, dim):
    return lax.broadcasted_iota(jnp.int32, shape, dim)


def one_where(mask):
    return jnp.where(mask, 1.0, 0.0)


def kernel(
    sizes,
    fields_hbm,
    react_hbm,
    pmap_hbm,
    w1_hbm,
    w2_hbm,
    w3_hbm,
    w4_hbm,
    out_ref,
    imp_ref,
    fields,
    react,
    pmap,
    w1,
    w2,
    w3,
    w4,
    rec,
    ybuf,
    zbuf,
    xlo,
    xhi,
    ylo,
    yhi,
    zlo,
    zhi,
    st_l,
    st_r,
    flux_x,
    flux_y,
    flux_z,
    turn_y,
    turn_z,
    hid1,
    hid2,
    source,
    contrib,
    rows2,
    parts,
    direct,
    own,
    load_sem,
    send_sem,
    recv_sem,
    s1_send,
    s1_recv,
    s2_send,
    s2_recv,
    ready,
    late,
    d_send,
    d_recv,
):
    nx, ny, nz = sizes
    gx = lax.axis_index("gx")
    gy = lax.axis_index("gy")
    gz = lax.axis_index("gz")
    is_wall = (gy == 0) | (gy == ny - 1)
    group = ny * nz
    me = gy * nz + gz
    walls = 2 * nz
    mine = 2 * nx * nz * (CZ // PATCH) // (nx * ny * nz)

    loads = []
    for i, (src, dst) in enumerate(
        (
            (fields_hbm, fields),
            (react_hbm, react),
            (pmap_hbm, pmap),
            (w1_hbm, w1),
            (w2_hbm, w2),
            (w3_hbm, w3),
            (w4_hbm, w4),
        )
    ):
        copy = pltpu.make_async_copy(src, dst, load_sem.at[i])
        if i < 3:
            copy.start()
        loads.append(copy)

    barrier = pltpu.get_barrier_semaphore()
    around = {
        "xlo": {"gx": lax.rem(gx + nx - 1, nx)},
        "xhi": {"gx": lax.rem(gx + 1, nx)},
        "ylo": {"gy": lax.rem(gy + ny - 1, ny)},
        "yhi": {"gy": lax.rem(gy + 1, ny)},
        "zlo": {"gz": lax.rem(gz + nz - 1, nz)},
        "zhi": {"gz": lax.rem(gz + 1, nz)},
    }
    half = nx // 2
    rank = lax.rem(gx, half)
    side = gx // half
    has_low = gx > 0
    has_high = gx < nx - 1
    late_low = gx == half
    late_high = gx == half - 1

    xs = [side * half + rank, (1 - side) * half + rank]
    sides = [side, 1 - side]
    ys = [gy] + [lax.rem(gy + i, ny) for i in range(1, ny)]
    zs = [gz] + [lax.rem(gz + i, nz) for i in range(1, nz)]

    def far_first(count):
        return sorted(range(count), key=lambda i: -min(i, count - i))

    for ds in (1, 0):
        for dz in far_first(nz):
            for to_y in (0, ny - 1):

                def greet_wall(ds=ds, dz=dz, to_y=to_y):
                    pl.semaphore_signal(
                        barrier,
                        inc=1,
                        device_id={"gx": xs[ds], "gy": jnp.int32(to_y), "gz": zs[dz]},
                        device_id_type=MESH,
                    )

                if ds == 0 and dz == 0:
                    pl.when(gy != to_y)(greet_wall)
                else:
                    greet_wall()

    def greet(where):
        pl.semaphore_signal(barrier, inc=1, device_id=around[where], device_id_type=MESH)

    for where in ("ylo", "yhi", "zlo", "zhi"):
        greet(where)

    @pl.when(has_low)
    def _():
        greet("xlo")

    @pl.when(has_high & jnp.logical_not(late_high))
    def _():
        greet("xhi")

    firsts = half // 8
    last_at = half // 2
    lasts = half // 4 if firsts else 0
    is_first = rank < firsts
    in_last = (rank >= last_at) & (rank < half - half // 4)

    if firsts:

        @pl.when(is_first)
        def _():
            def greet_last(i, carry):
                to_x = (i % 2) * half + last_at + i // 4
                to_y = (i // 2 % 2) * (ny - 1)
                for to_z in range(nz):
                    pl.semaphore_signal(
                        barrier,
                        inc=1,
                        device_id={"gx": to_x, "gy": to_y, "gz": jnp.int32(to_z)},
                        device_id_type=MESH,
                    )
                return carry

            lax.fori_loop(0, lasts * 4, greet_last, 0)

    def ranked(r):
        return side * half + r

    def greet_row(r, carry):
        pl.semaphore_signal(barrier, inc=1, device_id={"gx": ranked(r)}, device_id_type=MESH)
        return carry

    lax.fori_loop(rank + 1, half, greet_row, 0)

    slot_of = side * walls + (gy // jnp.int32(max(ny - 1, 1))) * nz + gz
    loads[0].wait()

    def send_row(r, slot):
        pltpu.make_async_remote_copy(
            src_ref=own,
            dst_ref=rows2.at[slot],
            send_sem=s2_send,
            recv_sem=s2_recv,
            device_id={"gx": ranked(r)},
            device_id_type=MESH,
        ).start()
        return 0

    loads[2].wait()

    @pl.when(is_wall)
    def _():
        low = gy == 0

        near_of = {0: [], 2: [], 4: []}
        for j in range(3):
            rho, *momentum, energy = (
                jnp.where(
                    low,
                    fields[k, pl.ds(j, CX, stride=CY), :],
                    fields[k, pl.ds(CY - 1 - j, CX, stride=CY), :],
                )
                for k in range(5)
            )
            log_rho, vel, log_pressure, _ = primitive(rho, momentum, energy)
            near_of[0].append(log_rho)
            near_of[2].append(vel[1])
            near_of[4].append(log_pressure)

        def line(k, sign):
            near = near_of[k]
            ghost = [sign * x for x in near]
            below = ghost[::-1] + near
            above = near[::-1] + ghost
            return jnp.stack([jnp.where(low, i, j) for i, j in zip(below, above)])

        left, right = {}, {}
        for k in (0, 2, 4):
            left[k], right[k] = weno_pair(line(k, -1.0 if k == 2 else 1.0))
        push = hllc(left, right, 1, only_push=True)[0] * (1.0 / (PATCH * PATCH))
        ids = jnp.where(low, pmap[0], pmap[1])
        total = jnp.zeros((2 * group, LANES), F32)
        for h in range(2):
            value = jnp.sum(push[4 * h : 4 * h + 4], axis=0, keepdims=True)
            panel = ids[4 * h : 4 * h + 1]
            owner = panel // mine
            owner_x = owner // group
            member = owner_x // half * group + owner % group
            place = owner_x % half * mine + panel % mine
            spread = jnp.where(iota((2 * group, LANES), 0) == member, value, 0.0)
            lane = one_where(iota((LANES, LANES), 0) == place).astype(BF16)
            big = spread.astype(BF16)
            small = (spread - big.astype(F32)).astype(BF16)
            total = total + dot_nt(big, lane) + dot_nt(small, lane)
        contrib[...] = total.reshape(2 * group, 1, LANES)
        parts[slot_of] = contrib[side * group + me]

    def recon_step(i, carry):
        span = pl.ds(pl.multiple_of(i * 16, 16), 16)
        rho, *momentum, energy = (fields[k, span, :] for k in range(5))
        log_rho, vel, log_pressure, inv = primitive(rho, momentum, energy)
        rec[0, span, :] = log_rho
        for k in range(3):
            rec[1 + k, span, :] = vel[k]
        rec[4, span, :] = log_pressure
        for k in range(5, COMPS):
            rec[k, span, :] = fields[k, span, :] * inv
        return carry

    waits_long = rank >= half - half // 4

    @pl.when(waits_long)
    def _():
        lax.fori_loop(0, ROWS // 16, recon_step, 0)

    sends = []

    def send(i, src, dst, where):
        copy = pltpu.make_async_remote_copy(
            src_ref=src,
            dst_ref=dst,
            send_sem=send_sem.at[i],
            recv_sem=recv_sem.at[i],
            device_id=around[where],
            device_id_type=MESH,
        )
        sends.append(copy)
        return copy

    to_low = send(0, rec.at[:, pl.ds(0, 24), :], xhi, "xlo")
    to_high = send(1, rec.at[:, pl.ds(ROWS - 24, 24), :], xlo, "xhi")

    def send_x():
        @pl.when(has_high)
        def _():
            to_high.start()

        @pl.when(has_low & jnp.logical_not(late_low))
        def _():
            to_low.start()

    linked = (
        4
        + has_high.astype(jnp.int32)
        + (has_low & jnp.logical_not(late_low)).astype(jnp.int32)
        + rank
        + is_wall.astype(jnp.int32) * (2 * group - 1)
        + (is_wall & in_last).astype(jnp.int32) * (firsts * 2 * group)
    )
    pl.semaphore_wait(barrier, linked)

    @pl.when(waits_long)
    def _():
        send_x()

    for copy in loads[3:]:
        copy.start()

    @pl.when(late_high)
    def _():
        pl.semaphore_signal(late, inc=1, device_id=around["xhi"], device_id_type=MESH)

    @pl.when(is_wall)
    def _():
        for ds in (1, 0):
            for dy in far_first(ny):
                for dz in far_first(nz):
                    if ds or dy or dz:
                        pltpu.make_async_remote_copy(
                            src_ref=contrib.at[sides[ds] * group + ys[dy] * nz + zs[dz]],
                            dst_ref=parts.at[slot_of],
                            send_sem=s1_send,
                            recv_sem=s1_recv,
                            device_id={"gx": xs[ds], "gy": ys[dy], "gz": zs[dz]},
                            device_id_type=MESH,
                        ).start()

    if firsts:

        @pl.when(is_wall & in_last)
        def _():
            def send_direct(i, carry):
                to_side = i // ny % 2
                to_y = i % ny
                for to_z in range(nz):
                    pltpu.make_async_remote_copy(
                        src_ref=contrib.at[to_side * group + to_y * nz + to_z],
                        dst_ref=direct.at[(rank - last_at) * 2 * walls + slot_of],
                        send_sem=d_send,
                        recv_sem=d_recv,
                        device_id={
                            "gx": to_side * half + i // (2 * ny),
                            "gy": to_y,
                            "gz": jnp.int32(to_z),
                        },
                        device_id_type=MESH,
                    ).start()
                return carry

            lax.fori_loop(0, firsts * 2 * ny, send_direct, 0)

    def signal_row(r, carry):
        pl.semaphore_signal(ready, inc=1, device_id={"gx": ranked(r)}, device_id_type=MESH)
        return carry

    lax.fori_loop(0, rank, signal_row, 0)

    def pass_on():
        @pl.when(is_wall)
        def _():
            few = parts.at[pl.ds(0, 2 * walls - 1)]
            pltpu.make_async_copy(few, few, s1_recv).wait()

        @pl.when(jnp.logical_not(is_wall))
        def _():
            pltpu.make_async_copy(parts, parts, s1_recv).wait()

        own[...] = jnp.sum(parts[...], axis=0)
        rows2[0] = own[...]
        first = jnp.where(in_last, firsts, 0)
        lax.fori_loop(first, rank, lambda r, carry: send_row(r, r - rank + half), 0)

    @pl.when(in_last)
    def _():
        pass_on()

    @pl.when(jnp.logical_not(waits_long))
    def _():
        lax.fori_loop(0, ROWS // 16, recon_step, 0)

    @pl.when(jnp.logical_not(waits_long))
    def _():
        send_x()


    def turn_to_y(k, carry):
        for y in range(CY):
            ybuf[k, pl.ds(8 * y, 8), :] = rec[k, pl.ds(y, CX, stride=CY), :]
        return carry

    lax.fori_loop(0, COMPS, turn_to_y, 0)
    send(2, ybuf.at[:, pl.ds(0, 24), :], yhi, "ylo").start()
    send(3, ybuf.at[:, pl.ds(ROWS - 24, 24), :], ylo, "yhi").start()

    first_half = iota((HALF, LANES), 1) < HALF

    def turn_to_z(i, carry):
        both = rec[pl.ds(2 * i, 2), :, :].reshape(2 * ROWS, CZ).T
        top = both[:HALF]
        bottom = both[HALF:]
        zbuf[2 * i, pl.ds(8, HALF), :] = jnp.where(first_half, top, pltpu.roll(bottom, HALF, 1))
        zbuf[2 * i + 1, pl.ds(8, HALF), :] = jnp.where(first_half, pltpu.roll(top, HALF, 1), bottom)
        return carry

    lax.fori_loop(0, COMPS // 2, turn_to_z, 0)
    send(4, zbuf.at[:, pl.ds(8, 8), :], zhi, "zlo").start()
    send(5, zbuf.at[:, pl.ds(HALF, 8), :], zlo, "zhi").start()

    loads[1].wait()
    hot = react[...] > 0
    flags = one_where(hot).astype(BF16)
    upto = one_where(iota((CZ, CZ), 0) <= iota((CZ, CZ), 1)).astype(BF16)
    within = jnp.dot(flags, upto, preferred_element_type=F32)
    sums = jnp.dot(flags, jnp.ones((CZ, CAP), BF16), preferred_element_type=F32)
    above = one_where(iota((ROWS, ROWS), 1) < iota((ROWS, ROWS), 0)).astype(BF16)
    start = jnp.dot(above, sums.astype(BF16), preferred_element_type=F32)
    slot = iota((ROWS, CAP), 1).astype(F32)
    row_hot = one_where((start <= slot) & (slot < start + sums))
    order = jnp.where(hot, start[:, :CZ] + within, 0.0).astype(BF16)
    sums_t = dot_nt(jnp.ones((CAP, CZ), BF16), flags)
    before = one_where(iota((ROWS, ROWS), 0) < iota((ROWS, ROWS), 1)).astype(BF16)
    start_t = jnp.dot(sums_t.astype(BF16), before, preferred_element_type=F32)
    slot_t = iota((CAP, ROWS), 0).astype(F32)
    row_hot_t = one_where((start_t <= slot_t) & (slot_t < start_t + sums_t)).astype(BF16)
    line_rank = jnp.dot(row_hot_t, order, preferred_element_type=F32)
    lane_hot = one_where(line_rank == iota((CAP, CZ), 0).astype(F32) + 1.0).astype(BF16)

    @pl.when((rank >= half // 4) & jnp.logical_not(in_last))
    def _():
        pass_on()

    cells = rec[...].reshape(COMPS * ROWS, CZ).astype(BF16)
    spread_cells = dot_nt(cells, lane_hot).reshape(COMPS, ROWS, CAP)
    features = jnp.sum(spread_cells * row_hot[None], axis=1).astype(BF16)

    loads[3].wait()
    hid1[...] = gelu(dot_tn(w1[...], features)).astype(BF16)
    loads[4].wait()
    hid2[...] = gelu(jnp.dot(w2[...], hid1[...], preferred_element_type=F32)).astype(BF16)
    loads[5].wait()
    loads[6].wait()
    hid3 = gelu(jnp.dot(w3[...], hid2[...], preferred_element_type=F32)).astype(BF16)
    rates = jnp.dot(w4[...], hid3, preferred_element_type=F32).astype(BF16).astype(F32)
    spread_rates = (rates[:, None, :] * row_hot[None]).reshape(COMPS * ROWS, CAP).astype(BF16)
    source[...] = jnp.dot(spread_rates, lane_hot, preferred_element_type=F32).reshape(
        COMPS, ROWS, CZ
    )

    @pl.when(rank < half // 4)
    def _():
        pass_on()

    def faces(load, normal, flux):
        def weno_step(k, carry):
            left, right = weno_pair(load(k))
            st_l[k] = left
            st_r[k] = right
            return carry

        lax.fori_loop(0, COMPS, weno_step, 0)

        def flux_step(i, carry):
            span = pl.ds(i * 3, 3)
            left = [st_l[k, span] for k in range(COMPS)]
            right = [st_r[k, span] for k in range(COMPS)]
            for k, x in enumerate(hllc(left, right, normal)):
                flux[k, span] = x
            return carry

        lax.fori_loop(0, 3, flux_step, 0)

    def sign_of(k, normal):
        return jnp.where(k == 1 + normal, -1.0, 1.0).astype(F32)

    sends[4].wait_recv()
    sends[5].wait_recv()
    first_lanes = iota((8, LANES), 1) < HALF

    def ghosts_z(k, carry):
        zbuf[k, pl.ds(0, 8), :] = pltpu.roll(
            jnp.where(first_lanes, zbuf[k, pl.ds(HALF, 8), :], zlo[k]), HALF, 1
        )
        zbuf[k, pl.ds(HALF + 8, 8), :] = pltpu.roll(
            jnp.where(first_lanes, zhi[k], zbuf[k, pl.ds(8, 8), :]), HALF, 1
        )
        return carry

    lax.fori_loop(0, COMPS, ghosts_z, 0)
    lane_low = iota((1, LANES), 1) < HALF

    @pl.when(gz == 0)
    def _():
        def mirror(k, carry):
            for j in range(3):
                here = zbuf[k, pl.ds(7 - j, 1), :]
                inside = zbuf[k, pl.ds(8 + j, 1), :] * sign_of(k, 2)
                zbuf[k, pl.ds(7 - j, 1), :] = jnp.where(lane_low, inside, here)
            return carry

        lax.fori_loop(0, COMPS, mirror, 0)

    @pl.when(gz == nz - 1)
    def _():
        def mirror(k, carry):
            for j in range(3):
                here = zbuf[k, pl.ds(HALF + 8 + j, 1), :]
                inside = zbuf[k, pl.ds(HALF + 7 - j, 1), :] * sign_of(k, 2)
                zbuf[k, pl.ds(HALF + 8 + j, 1), :] = jnp.where(lane_low, here, inside)
            return carry

        lax.fori_loop(0, COMPS, mirror, 0)

    faces(
        lambda k: jnp.stack([zbuf[k, pl.ds(5 + j, 8, stride=8), :] for j in range(14)]), 2, flux_z
    )

    def send_up():
        pl.semaphore_wait(ready, half - 1 - rank)
        lax.fori_loop(rank + 1, half, lambda r, carry: send_row(r, r - rank), 0)

    goes_up = rank < half - 1
    goes_early = rank >= half // 2

    @pl.when(goes_up & goes_early)
    def _():
        send_up()

    def mirror_planes(inner, low, high, normal, place, count):
        @pl.when(place == 0)
        def _():
            def mirror(k, carry):
                for j in range(3):
                    low[k, pl.ds(16 - 8 * j, 8), :] = inner[k, pl.ds(8 * j, 8), :] * sign_of(k, normal)
                return carry

            lax.fori_loop(0, COMPS, mirror, 0)

        @pl.when(place == count - 1)
        def _():
            def mirror(k, carry):
                for j in range(3):
                    high[k, pl.ds(8 * j, 8), :] = inner[k, pl.ds(ROWS - 8 - 8 * j, 8), :] * sign_of(
                        k, normal
                    )
                return carry

            lax.fori_loop(0, COMPS, mirror, 0)

    def planes(low, inner, high):
        def load(k):
            return jnp.concatenate(
                [low[k].reshape(3, 8, CZ), inner[k].reshape(8, 8, CZ), high[k].reshape(3, 8, CZ)]
            )

        return load

    sends[2].wait_recv()
    sends[3].wait_recv()
    mirror_planes(ybuf, ylo, yhi, 1, gy, ny)
    faces(planes(ylo, ybuf, yhi), 1, flux_y)
    @pl.when(late_low)
    def _():
        pl.semaphore_wait(late, 1)
        to_low.start()

    goes_middle = ((rank >= half // 4) & (rank < half // 2)) | (late_low & jnp.logical_not(goes_early))

    @pl.when(goes_up & goes_middle)
    def _():
        send_up()

    @pl.when(has_high)
    def _():
        to_low.wait_recv()

    @pl.when(has_low)
    def _():
        to_high.wait_recv()

    mirror_planes(rec, xlo, xhi, 0, gx, nx)
    faces(planes(xlo, rec, xhi), 0, flux_x)

    def finish(i, carry):
        change = []
        for h in range(2):
            k = 2 * i + h
            along_z = flux_z[k, pl.ds(1, 8)] - flux_z[k, pl.ds(0, 8)]
            along_y = flux_y[k, pl.ds(1, 8)] - flux_y[k, pl.ds(0, 8)]
            for j in range(8):
                turn_z[h, pl.ds(j, 8, stride=8), :] = along_z[j]
                turn_y[h, pl.ds(j, 8, stride=8), :] = along_y[j]
            change.append((flux_x[k, pl.ds(1, 8)] - flux_x[k, pl.ds(0, 8)]).reshape(ROWS, CZ))
        one = turn_z[0]
        two = turn_z[1]
        top = jnp.where(first_half, one, pltpu.roll(two, HALF, 1))
        bottom = jnp.where(first_half, pltpu.roll(one, HALF, 1), two)
        back = jnp.concatenate([top, bottom], axis=0).T
        for h in range(2):
            k = 2 * i + h
            whole = change[h] + turn_y[h] + back[ROWS * h : ROWS * h + ROWS]
            out_ref[k] = fields[k] - TIME_STEP * whole + CHEM_STEP * source[k]
        return carry

    lax.fori_loop(0, COMPS // 2, finish, 0)

    @pl.when(goes_up & jnp.logical_not(goes_early | goes_middle))
    def _():
        send_up()

    many = pl.ds(1, half - 1)
    if firsts:

        @pl.when(is_first)
        def _():
            for i in range(lasts):
                rows2[rank + half - last_at - i] = jnp.zeros((1, LANES), F32)
            some = pl.ds(1, half - 1 - lasts)
            pltpu.make_async_copy(rows2.at[some], rows2.at[some], s2_recv).wait()
            pltpu.make_async_copy(direct, direct, d_recv).wait()
            rows2[0] += jnp.sum(direct[...], axis=0)

        @pl.when(jnp.logical_not(is_first))
        def _():
            pltpu.make_async_copy(rows2.at[many], rows2.at[many], s2_recv).wait()

    elif half > 1:
        pltpu.make_async_copy(rows2.at[many], rows2.at[many], s2_recv).wait()
    total = jnp.sum(rows2[...], axis=0)
    wide = jnp.broadcast_to(total, (8, LANES))
    imp_ref[...] = pltpu.roll(wide, lax.rem(LANES - rank * mine, LANES), 1)
    if firsts:

        @pl.when(in_last)
        def _():
            some = pl.ds(1, half - 1 - firsts)
            pltpu.make_async_copy(rows2.at[some], rows2.at[some], s2_send).wait()

        @pl.when(jnp.logical_not(in_last))
        def _():
            pltpu.make_async_copy(rows2.at[many], rows2.at[many], s2_send).wait()

        @pl.when(is_wall & in_last)
        def _():
            every = pl.ds(0, 2 * group)

            def sent(i, carry):
                pltpu.make_async_copy(contrib.at[every], contrib.at[every], d_send).wait()
                return carry

            lax.fori_loop(0, firsts, sent, 0)

    elif half > 1:
        pltpu.make_async_copy(rows2.at[many], rows2.at[many], s2_send).wait()

    @pl.when(is_wall)
    def _():
        most = pl.ds(1, 2 * group - 1)
        pltpu.make_async_copy(contrib.at[most], contrib.at[most], s1_send).wait()

    for copy in sends[2:]:
        copy.wait_send()

    @pl.when(has_low)
    def _():
        to_low.wait_send()

    @pl.when(has_high)
    def _():
        to_high.wait_send()


def body(fields, reacting, panel_map, layer_one, layer_two, layer_three, layer_four):
    sizes = (lax.axis_size("gx"), lax.axis_size("gy"), lax.axis_size("gz"))
    nx, ny, nz = sizes
    any_spec = pl.BlockSpec(memory_space=pltpu.HBM)
    vmem_spec = pl.BlockSpec(memory_space=pltpu.VMEM)
    plane = (COMPS, ROWS, CZ)
    ghost = (COMPS, 24, CZ)
    state = (COMPS, 9, 8, CZ)
    dma = pltpu.SemaphoreType.DMA
    held = pltpu.with_memory_space_constraint
    new_fields, impulse = pl.pallas_call(
        functools.partial(kernel, sizes),
        out_shape=(
            pltpu.VMEM(plane, F32),
            pltpu.VMEM((8, LANES), F32),
        ),
        in_specs=[any_spec] * 7,
        out_specs=(vmem_spec, vmem_spec),
        scratch_shapes=[
            pltpu.VMEM(plane, F32),
            pltpu.VMEM((ROWS, CZ), jnp.int32),
            pltpu.VMEM((2, CX, CZ), jnp.int32),
            pltpu.VMEM((COMPS, H1), BF16),
            pltpu.VMEM((H2, H1), BF16),
            pltpu.VMEM((H3, H2), BF16),
            pltpu.VMEM((COMPS, H3), BF16),
            pltpu.VMEM(plane, F32),
            pltpu.VMEM(plane, F32),
            pltpu.VMEM((COMPS, HALF + 16, LANES), F32),
            pltpu.VMEM(ghost, F32),
            pltpu.VMEM(ghost, F32),
            pltpu.VMEM(ghost, F32),
            pltpu.VMEM(ghost, F32),
            pltpu.VMEM((COMPS, 8, LANES), F32),
            pltpu.VMEM((COMPS, 8, LANES), F32),
            pltpu.VMEM(state, F32),
            pltpu.VMEM(state, F32),
            pltpu.VMEM(state, F32),
            pltpu.VMEM(state, F32),
            pltpu.VMEM(state, F32),
            pltpu.VMEM((2, ROWS, CZ), F32),
            pltpu.VMEM((2, ROWS, CZ), F32),
            pltpu.VMEM((H1, CAP), BF16),
            pltpu.VMEM((H2, CAP), BF16),
            pltpu.VMEM(plane, F32),
            pltpu.VMEM((2 * ny * nz, 1, LANES), F32),
            pltpu.VMEM((nx // 2, 1, LANES), F32),
            pltpu.VMEM((4 * nz, 1, LANES), F32),
            pltpu.VMEM((max(nx // 8, 1) * 4 * nz, 1, LANES), F32),
            pltpu.VMEM((1, LANES), F32),
            dma((7,)),
            dma((6,)),
            dma((6,)),
            dma(()),
            dma(()),
            dma(()),
            dma(()),
            pltpu.SemaphoreType.REGULAR,
            pltpu.SemaphoreType.REGULAR,
            dma(()),
            dma(()),
        ],
        compiler_params=pltpu.CompilerParams(
            collective_id=0, has_side_effects=True, vmem_limit_bytes=48 * 2**20
        ),
    )(
        held(fields.reshape(plane), pltpu.HBM),
        held(reacting.reshape(ROWS, CZ), pltpu.HBM),
        held(panel_map, pltpu.HBM),
        held(layer_one.T, pltpu.HBM),
        held(layer_two, pltpu.HBM),
        held(layer_three, pltpu.HBM),
        held(layer_four, pltpu.HBM),
    )
    own_panels = 2 * nx * nz * (CZ // PATCH) // (nx * ny * nz)
    return new_fields.reshape(fields.shape), impulse[0, :own_panels]


def solution(mesh):
    return jax.shard_map(
        body,
        mesh=mesh,
        in_specs=(
            P(None, "gx", "gy", "gz"),
            P("gx", "gy", "gz"),
            P(None, "gx", "gz"),
            P(),
            P(),
            P(),
            P(),
        ),
        out_specs=(P(None, "gx", "gy", "gz"), P(("gx", "gy", "gz"))),
        check_vma=False,
    )
```

```python
import functools
import math

import jax
import jax.numpy as jnp
from jax import lax
from jax.experimental import pallas as pl
from jax.experimental.pallas import tpu as pltpu
from jax.sharding import PartitionSpec as P

COMPS = 12
CX = 8
CY = 8
CZ = 128
ROWS = CX * CY
HALF = CZ // 2
CAP = 256
H1 = 1600
H2 = 800
H3 = 400
PATCH = 8
LANES = 128

TIME_STEP = 0.1
CHEM_STEP = 0.25
WENO_EPS = 1e-06
ALPHA = math.sqrt(12.0 / 13.0)
EPS_SCALED = WENO_EPS * 12.0 / 13.0
LOG_HEAT_HALF = 0.5 * math.log(1.4)

MESH = pl.DeviceIdType.MESH
F32 = jnp.float32
BF16 = jnp.bfloat16


def recip(x):
    r = pl.reciprocal(x, approx=True)
    return r * (2.0 - x * r)


def primitive(rho, momentum, energy):
    inv = recip(rho)
    inv = inv * (2.0 - rho * inv)
    vel = [x * inv for x in momentum]
    speed = vel[0] * vel[0] + vel[1] * vel[1] + vel[2] * vel[2]
    return jnp.log(rho), vel, jnp.log(0.4 * (energy - 0.5 * rho * speed)), inv


def weno_pair(v):
    count = v.shape[0]
    d = v[1:] - v[:-1]
    q = d[1:] - d[:-1]
    g = (q[1:] - q[:-1]) * (1.0 / 3.0)
    da = d * ALPHA
    ha = q * (0.5 * ALPHA)
    qq = q * q + EPS_SCALED
    m = count - 4
    f0 = da[1 : 1 + m] + ha[0:m]
    f1 = da[1 : 1 + m] + ha[1 : 1 + m]
    f2 = da[2 : 2 + m] - ha[2 : 2 + m]
    t0 = f0 * f0 + qq[0:m]
    t1 = f1 * f1 + qq[1 : 1 + m]
    t2 = f2 * f2 + qq[2 : 2 + m]
    a = t1 * t2
    b = t0 * t2
    c = t0 * t1
    a = a * a
    b = b * b * 6.0
    c = c * c
    u = a + c + b
    x = a * g[0:m]
    y = c * g[1 : 1 + m]
    center = v[2 : 2 + m] + q[1 : 1 + m] * (1.0 / 3.0)
    hd = d * 0.5
    n = m - 1
    low = slice(0, n)
    high = slice(1, m)
    left = (
        center[low]
        + hd[1 : 1 + n]
        - (x[low] + 1.5 * y[low]) * pl.reciprocal(u[low] + 2.0 * c[low], approx=True)
    )
    right = (
        center[high]
        - hd[3 : 3 + n]
        + (y[high] + 1.5 * x[high]) * pl.reciprocal(u[high] + 2.0 * a[high], approx=True)
    )
    return left, right


def hllc(left, right, normal, only_push=False):
    rl = jnp.exp(left[0])
    rr = jnp.exp(right[0])
    p_l = jnp.exp(left[4])
    p_r = jnp.exp(right[4])
    cl = jnp.exp(0.5 * (left[4] - left[0]) + LOG_HEAT_HALF)
    cr = jnp.exp(0.5 * (right[4] - right[0]) + LOG_HEAT_HALF)
    ul = left[1 + normal]
    ur = right[1 + normal]
    sl = jnp.minimum(ul - cl, ur - cr)
    sr = jnp.maximum(ul + cl, ur + cr)
    al = rl * (sl - ul)
    ar = rr * (sr - ur)
    s = (p_r - p_l + al * ul - ar * ur) * recip(al - ar)
    take_left = jnp.maximum(s, sl) >= 0.0

    def pick(i, j):
        return jnp.where(take_left, i, j)

    rho = pick(rl, rr)
    p = pick(p_l, p_r)
    sk = pick(sl, sr)
    a = pick(al, ar)
    beyond = pick(sl, -sr) >= 0.0
    un = pick(ul, ur)
    inv = recip(sk - s)
    pstar = p + a * (s - un)
    u_face = jnp.where(beyond, un, s)
    p_face = jnp.where(beyond, p, pstar)
    mass = jnp.where(beyond, rho, a * inv) * u_face
    push = mass * u_face + p_face
    if only_push:
        return push
    vel = [un if i == normal else pick(left[1 + i], right[1 + i]) for i in range(3)]
    energy = 2.5 * p + 0.5 * rho * (vel[0] * vel[0] + vel[1] * vel[1] + vel[2] * vel[2])
    estar = ((sk - un) * energy + pstar * s - p * un) * inv
    e_face = jnp.where(beyond, energy, estar)
    flux = [mass]
    for i in range(3):
        flux.append(push if i == normal else mass * vel[i])
    flux.append(u_face * (e_face + p_face))
    for i in range(5, COMPS):
        flux.append(mass * pick(left[i], right[i]))
    return flux


def gelu(x):
    k = math.sqrt(2.0 / math.pi)
    y = x * (x * x * (0.044715 * k) + k)
    h = 0.5 * x
    return h * jnp.tanh(y) + h


def dot_nt(a, b):
    return lax.dot_general(a, b, (((1,), (1,)), ((), ())), preferred_element_type=F32)


def dot_tn(a, b):
    return lax.dot_general(a, b, (((0,), (0,)), ((), ())), preferred_element_type=F32)


def iota(shape, dim):
    return lax.broadcasted_iota(jnp.int32, shape, dim)


def one_where(mask):
    return jnp.where(mask, 1.0, 0.0)


def kernel(
    sizes,
    fields_hbm,
    react_hbm,
    pmap_hbm,
    w1_hbm,
    w2_hbm,
    w3_hbm,
    w4_hbm,
    out_ref,
    imp_ref,
    fields,
    react,
    pmap,
    w1,
    w2,
    w3,
    w4,
    rec,
    ybuf,
    zbuf,
    xlo,
    xhi,
    ylo,
    yhi,
    zlo,
    zhi,
    st_l,
    st_r,
    flux_x,
    flux_y,
    flux_z,
    turn_y,
    turn_z,
    hid1,
    hid2,
    source,
    contrib,
    rows2,
    parts,
    direct,
    own,
    load_sem,
    send_sem,
    recv_sem,
    s1_send,
    s1_recv,
    s2_send,
    s2_recv,
    ready,
    late,
    d_send,
    d_recv,
):
    nx, ny, nz = sizes
    gx = lax.axis_index("gx")
    gy = lax.axis_index("gy")
    gz = lax.axis_index("gz")
    is_wall = (gy == 0) | (gy == ny - 1)
    group = ny * nz
    me = gy * nz + gz
    walls = 2 * nz
    mine = 2 * nx * nz * (CZ // PATCH) // (nx * ny * nz)

    loads = []
    for i, (src, dst) in enumerate(
        (
            (fields_hbm, fields),
            (react_hbm, react),
            (pmap_hbm, pmap),
            (w1_hbm, w1),
            (w2_hbm, w2),
            (w3_hbm, w3),
            (w4_hbm, w4),
        )
    ):
        copy = pltpu.make_async_copy(src, dst, load_sem.at[i])
        if i < 3:
            copy.start()
        loads.append(copy)

    barrier = pltpu.get_barrier_semaphore()
    around = {
        "xlo": {"gx": lax.rem(gx + nx - 1, nx)},
        "xhi": {"gx": lax.rem(gx + 1, nx)},
        "ylo": {"gy": lax.rem(gy + ny - 1, ny)},
        "yhi": {"gy": lax.rem(gy + 1, ny)},
        "zlo": {"gz": lax.rem(gz + nz - 1, nz)},
        "zhi": {"gz": lax.rem(gz + 1, nz)},
    }
    half = nx // 2
    rank = lax.rem(gx, half)
    side = gx // half
    has_low = gx > 0
    has_high = gx < nx - 1
    late_low = gx == half
    late_high = gx == half - 1

    xs = [side * half + rank, (1 - side) * half + rank]
    sides = [side, 1 - side]
    ys = [gy] + [lax.rem(gy + i, ny) for i in range(1, ny)]
    zs = [gz] + [lax.rem(gz + i, nz) for i in range(1, nz)]

    def far_first(count):
        return sorted(range(count), key=lambda i: -min(i, count - i))

    for ds in (1, 0):
        for dz in far_first(nz):
            for to_y in (0, ny - 1):

                def greet_wall(ds=ds, dz=dz, to_y=to_y):
                    pl.semaphore_signal(
                        barrier,
                        inc=1,
                        device_id={"gx": xs[ds], "gy": jnp.int32(to_y), "gz": zs[dz]},
                        device_id_type=MESH,
                    )

                if ds == 0 and dz == 0:
                    pl.when(gy != to_y)(greet_wall)
                else:
                    greet_wall()

    def greet(where):
        pl.semaphore_signal(barrier, inc=1, device_id=around[where], device_id_type=MESH)

    for where in ("ylo", "yhi", "zlo", "zhi"):
        greet(where)

    @pl.when(has_low)
    def _():
        greet("xlo")

    @pl.when(has_high & jnp.logical_not(late_high))
    def _():
        greet("xhi")

    firsts = half // 4 if half >= 8 else 0
    last_at = half // 2
    lasts = half // 4 if firsts else 0
    is_first = rank < firsts
    in_last = (rank >= last_at) & (rank < half - half // 4)

    if firsts:

        @pl.when(is_first)
        def _():
            def greet_last(i, carry):
                to_x = (i % 2) * half + last_at + i // 4
                to_y = (i // 2 % 2) * (ny - 1)
                for to_z in range(nz):
                    pl.semaphore_signal(
                        barrier,
                        inc=1,
                        device_id={"gx": to_x, "gy": to_y, "gz": jnp.int32(to_z)},
                        device_id_type=MESH,
                    )
                return carry

            lax.fori_loop(0, lasts * 4, greet_last, 0)

    def ranked(r):
        return side * half + r

    def greet_row(r, carry):
        pl.semaphore_signal(barrier, inc=1, device_id={"gx": ranked(r)}, device_id_type=MESH)
        return carry

    lax.fori_loop(rank + 1, half, greet_row, 0)

    slot_of = side * walls + (gy // jnp.int32(max(ny - 1, 1))) * nz + gz
    loads[0].wait()

    def send_row(r, slot):
        pltpu.make_async_remote_copy(
            src_ref=own,
            dst_ref=rows2.at[slot],
            send_sem=s2_send,
            recv_sem=s2_recv,
            device_id={"gx": ranked(r)},
            device_id_type=MESH,
        ).start()
        return 0

    loads[2].wait()

    @pl.when(is_wall)
    def _():
        low = gy == 0

        near_of = {0: [], 2: [], 4: []}
        for j in range(3):
            rho, *momentum, energy = (
                jnp.where(
                    low,
                    fields[k, pl.ds(j, CX, stride=CY), :],
                    fields[k, pl.ds(CY - 1 - j, CX, stride=CY), :],
                )
                for k in range(5)
            )
            log_rho, vel, log_pressure, _ = primitive(rho, momentum, energy)
            near_of[0].append(log_rho)
            near_of[2].append(vel[1])
            near_of[4].append(log_pressure)

        def line(k, sign):
            near = near_of[k]
            ghost = [sign * x for x in near]
            below = ghost[::-1] + near
            above = near[::-1] + ghost
            return jnp.stack([jnp.where(low, i, j) for i, j in zip(below, above)])

        left, right = {}, {}
        for k in (0, 2, 4):
            left[k], right[k] = weno_pair(line(k, -1.0 if k == 2 else 1.0))
        push = hllc(left, right, 1, only_push=True)[0] * (1.0 / (PATCH * PATCH))
        ids = jnp.where(low, pmap[0], pmap[1])
        total = jnp.zeros((2 * group, LANES), F32)
        for h in range(2):
            value = jnp.sum(push[4 * h : 4 * h + 4], axis=0, keepdims=True)
            panel = ids[4 * h : 4 * h + 1]
            owner = panel // mine
            owner_x = owner // group
            member = owner_x // half * group + owner % group
            place = owner_x % half * mine + panel % mine
            spread = jnp.where(iota((2 * group, LANES), 0) == member, value, 0.0)
            lane = one_where(iota((LANES, LANES), 0) == place).astype(BF16)
            big = spread.astype(BF16)
            small = (spread - big.astype(F32)).astype(BF16)
            total = total + dot_nt(big, lane) + dot_nt(small, lane)
        contrib[...] = total.reshape(2 * group, 1, LANES)
        parts[slot_of] = contrib[side * group + me]

    def recon_step(i, carry):
        span = pl.ds(pl.multiple_of(i * 16, 16), 16)
        rho, *momentum, energy = (fields[k, span, :] for k in range(5))
        log_rho, vel, log_pressure, inv = primitive(rho, momentum, energy)
        rec[0, span, :] = log_rho
        for k in range(3):
            rec[1 + k, span, :] = vel[k]
        rec[4, span, :] = log_pressure
        for k in range(5, COMPS):
            rec[k, span, :] = fields[k, span, :] * inv
        return carry

    waits_long = rank >= half - half // 4

    @pl.when(waits_long)
    def _():
        lax.fori_loop(0, ROWS // 16, recon_step, 0)

    sends = []

    def send(i, src, dst, where):
        copy = pltpu.make_async_remote_copy(
            src_ref=src,
            dst_ref=dst,
            send_sem=send_sem.at[i],
            recv_sem=recv_sem.at[i],
            device_id=around[where],
            device_id_type=MESH,
        )
        sends.append(copy)
        return copy

    to_low = send(0, rec.at[:, pl.ds(0, 24), :], xhi, "xlo")
    to_high = send(1, rec.at[:, pl.ds(ROWS - 24, 24), :], xlo, "xhi")

    def send_x():
        @pl.when(has_high)
        def _():
            to_high.start()

        @pl.when(has_low & jnp.logical_not(late_low))
        def _():
            to_low.start()

    linked = (
        4
        + has_high.astype(jnp.int32)
        + (has_low & jnp.logical_not(late_low)).astype(jnp.int32)
        + rank
        + is_wall.astype(jnp.int32) * (2 * group - 1)
        + (is_wall & in_last).astype(jnp.int32) * (firsts * 2 * group)
    )
    pl.semaphore_wait(barrier, linked)

    @pl.when(waits_long)
    def _():
        send_x()

    for copy in loads[3:]:
        copy.start()

    @pl.when(late_high)
    def _():
        pl.semaphore_signal(late, inc=1, device_id=around["xhi"], device_id_type=MESH)

    @pl.when(is_wall)
    def _():
        for ds in (1, 0):
            for dy in far_first(ny):
                for dz in far_first(nz):
                    if ds or dy or dz:
                        pltpu.make_async_remote_copy(
                            src_ref=contrib.at[sides[ds] * group + ys[dy] * nz + zs[dz]],
                            dst_ref=parts.at[slot_of],
                            send_sem=s1_send,
                            recv_sem=s1_recv,
                            device_id={"gx": xs[ds], "gy": ys[dy], "gz": zs[dz]},
                            device_id_type=MESH,
                        ).start()

    if firsts:

        @pl.when(is_wall & in_last)
        def _():
            def send_direct(i, carry):
                to_side = i // ny % 2
                to_y = i % ny
                for to_z in range(nz):
                    pltpu.make_async_remote_copy(
                        src_ref=contrib.at[to_side * group + to_y * nz + to_z],
                        dst_ref=direct.at[(rank - last_at) * 2 * walls + slot_of],
                        send_sem=d_send,
                        recv_sem=d_recv,
                        device_id={
                            "gx": to_side * half + i // (2 * ny),
                            "gy": to_y,
                            "gz": jnp.int32(to_z),
                        },
                        device_id_type=MESH,
                    ).start()
                return carry

            lax.fori_loop(0, firsts * 2 * ny, send_direct, 0)

    def signal_row(r, carry):
        pl.semaphore_signal(ready, inc=1, device_id={"gx": ranked(r)}, device_id_type=MESH)
        return carry

    lax.fori_loop(0, rank, signal_row, 0)

    def pass_on():
        @pl.when(is_wall)
        def _():
            few = parts.at[pl.ds(0, 2 * walls - 1)]
            pltpu.make_async_copy(few, few, s1_recv).wait()

        @pl.when(jnp.logical_not(is_wall))
        def _():
            pltpu.make_async_copy(parts, parts, s1_recv).wait()

        own[...] = jnp.sum(parts[...], axis=0)
        rows2[0] = own[...]
        first = jnp.where(in_last, firsts, 0)
        lax.fori_loop(first, rank, lambda r, carry: send_row(r, r - rank + half), 0)

    @pl.when(in_last)
    def _():
        pass_on()

    @pl.when(jnp.logical_not(waits_long))
    def _():
        lax.fori_loop(0, ROWS // 16, recon_step, 0)

    @pl.when(jnp.logical_not(waits_long))
    def _():
        send_x()


    def turn_to_y(k, carry):
        for y in range(CY):
            ybuf[k, pl.ds(8 * y, 8), :] = rec[k, pl.ds(y, CX, stride=CY), :]
        return carry

    lax.fori_loop(0, COMPS, turn_to_y, 0)
    send(2, ybuf.at[:, pl.ds(0, 24), :], yhi, "ylo").start()
    send(3, ybuf.at[:, pl.ds(ROWS - 24, 24), :], ylo, "yhi").start()

    first_half = iota((HALF, LANES), 1) < HALF

    def turn_to_z(i, carry):
        both = rec[pl.ds(2 * i, 2), :, :].reshape(2 * ROWS, CZ).T
        top = both[:HALF]
        bottom = both[HALF:]
        zbuf[2 * i, pl.ds(8, HALF), :] = jnp.where(first_half, top, pltpu.roll(bottom, HALF, 1))
        zbuf[2 * i + 1, pl.ds(8, HALF), :] = jnp.where(first_half, pltpu.roll(top, HALF, 1), bottom)
        return carry

    lax.fori_loop(0, COMPS // 2, turn_to_z, 0)
    send(4, zbuf.at[:, pl.ds(8, 8), :], zhi, "zlo").start()
    send(5, zbuf.at[:, pl.ds(HALF, 8), :], zlo, "zhi").start()

    loads[1].wait()
    hot = react[...] > 0
    flags = one_where(hot).astype(BF16)
    upto = one_where(iota((CZ, CZ), 0) <= iota((CZ, CZ), 1)).astype(BF16)
    within = jnp.dot(flags, upto, preferred_element_type=F32)
    sums = jnp.dot(flags, jnp.ones((CZ, CAP), BF16), preferred_element_type=F32)
    above = one_where(iota((ROWS, ROWS), 1) < iota((ROWS, ROWS), 0)).astype(BF16)
    start = jnp.dot(above, sums.astype(BF16), preferred_element_type=F32)
    slot = iota((ROWS, CAP), 1).astype(F32)
    row_hot = one_where((start <= slot) & (slot < start + sums))
    order = jnp.where(hot, start[:, :CZ] + within, 0.0).astype(BF16)
    sums_t = dot_nt(jnp.ones((CAP, CZ), BF16), flags)
    before = one_where(iota((ROWS, ROWS), 0) < iota((ROWS, ROWS), 1)).astype(BF16)
    start_t = jnp.dot(sums_t.astype(BF16), before, preferred_element_type=F32)
    slot_t = iota((CAP, ROWS), 0).astype(F32)
    row_hot_t = one_where((start_t <= slot_t) & (slot_t < start_t + sums_t)).astype(BF16)
    line_rank = jnp.dot(row_hot_t, order, preferred_element_type=F32)
    lane_hot = one_where(line_rank == iota((CAP, CZ), 0).astype(F32) + 1.0).astype(BF16)

    @pl.when((rank >= half // 4) & jnp.logical_not(in_last))
    def _():
        pass_on()

    cells = rec[...].reshape(COMPS * ROWS, CZ).astype(BF16)
    spread_cells = dot_nt(cells, lane_hot).reshape(COMPS, ROWS, CAP)
    features = jnp.sum(spread_cells * row_hot[None], axis=1).astype(BF16)

    loads[3].wait()
    hid1[...] = gelu(dot_tn(w1[...], features)).astype(BF16)
    loads[4].wait()
    hid2[...] = gelu(jnp.dot(w2[...], hid1[...], preferred_element_type=F32)).astype(BF16)
    loads[5].wait()
    loads[6].wait()
    hid3 = gelu(jnp.dot(w3[...], hid2[...], preferred_element_type=F32)).astype(BF16)
    rates = jnp.dot(w4[...], hid3, preferred_element_type=F32).astype(BF16).astype(F32)
    spread_rates = (rates[:, None, :] * row_hot[None]).reshape(COMPS * ROWS, CAP).astype(BF16)
    source[...] = jnp.dot(spread_rates, lane_hot, preferred_element_type=F32).reshape(
        COMPS, ROWS, CZ
    )

    @pl.when(rank < half // 4)
    def _():
        pass_on()

    def faces(load, normal, flux):
        def weno_step(k, carry):
            left, right = weno_pair(load(k))
            st_l[k] = left
            st_r[k] = right
            return carry

        lax.fori_loop(0, COMPS, weno_step, 0)

        def flux_step(i, carry):
            span = pl.ds(i * 3, 3)
            left = [st_l[k, span] for k in range(COMPS)]
            right = [st_r[k, span] for k in range(COMPS)]
            for k, x in enumerate(hllc(left, right, normal)):
                flux[k, span] = x
            return carry

        lax.fori_loop(0, 3, flux_step, 0)

    def sign_of(k, normal):
        return jnp.where(k == 1 + normal, -1.0, 1.0).astype(F32)

    sends[4].wait_recv()
    sends[5].wait_recv()
    first_lanes = iota((8, LANES), 1) < HALF

    def ghosts_z(k, carry):
        zbuf[k, pl.ds(0, 8), :] = pltpu.roll(
            jnp.where(first_lanes, zbuf[k, pl.ds(HALF, 8), :], zlo[k]), HALF, 1
        )
        zbuf[k, pl.ds(HALF + 8, 8), :] = pltpu.roll(
            jnp.where(first_lanes, zhi[k], zbuf[k, pl.ds(8, 8), :]), HALF, 1
        )
        return carry

    lax.fori_loop(0, COMPS, ghosts_z, 0)
    lane_low = iota((1, LANES), 1) < HALF

    @pl.when(gz == 0)
    def _():
        def mirror(k, carry):
            for j in range(3):
                here = zbuf[k, pl.ds(7 - j, 1), :]
                inside = zbuf[k, pl.ds(8 + j, 1), :] * sign_of(k, 2)
                zbuf[k, pl.ds(7 - j, 1), :] = jnp.where(lane_low, inside, here)
            return carry

        lax.fori_loop(0, COMPS, mirror, 0)

    @pl.when(gz == nz - 1)
    def _():
        def mirror(k, carry):
            for j in range(3):
                here = zbuf[k, pl.ds(HALF + 8 + j, 1), :]
                inside = zbuf[k, pl.ds(HALF + 7 - j, 1), :] * sign_of(k, 2)
                zbuf[k, pl.ds(HALF + 8 + j, 1), :] = jnp.where(lane_low, here, inside)
            return carry

        lax.fori_loop(0, COMPS, mirror, 0)

    faces(
        lambda k: jnp.stack([zbuf[k, pl.ds(5 + j, 8, stride=8), :] for j in range(14)]), 2, flux_z
    )

    def send_up():
        pl.semaphore_wait(ready, half - 1 - rank)
        lax.fori_loop(rank + 1, half, lambda r, carry: send_row(r, r - rank), 0)

    goes_up = rank < half - 1
    goes_early = rank >= half // 2

    @pl.when(goes_up & goes_early)
    def _():
        send_up()

    def mirror_planes(inner, low, high, normal, place, count):
        @pl.when(place == 0)
        def _():
            def mirror(k, carry):
                for j in range(3):
                    low[k, pl.ds(16 - 8 * j, 8), :] = inner[k, pl.ds(8 * j, 8), :] * sign_of(k, normal)
                return carry

            lax.fori_loop(0, COMPS, mirror, 0)

        @pl.when(place == count - 1)
        def _():
            def mirror(k, carry):
                for j in range(3):
                    high[k, pl.ds(8 * j, 8), :] = inner[k, pl.ds(ROWS - 8 - 8 * j, 8), :] * sign_of(
                        k, normal
                    )
                return carry

            lax.fori_loop(0, COMPS, mirror, 0)

    def planes(low, inner, high):
        def load(k):
            return jnp.concatenate(
                [low[k].reshape(3, 8, CZ), inner[k].reshape(8, 8, CZ), high[k].reshape(3, 8, CZ)]
            )

        return load

    sends[2].wait_recv()
    sends[3].wait_recv()
    mirror_planes(ybuf, ylo, yhi, 1, gy, ny)
    faces(planes(ylo, ybuf, yhi), 1, flux_y)
    @pl.when(late_low)
    def _():
        pl.semaphore_wait(late, 1)
        to_low.start()

    goes_middle = ((rank >= half // 4) & (rank < half // 2)) | (late_low & jnp.logical_not(goes_early))

    @pl.when(goes_up & goes_middle)
    def _():
        send_up()

    @pl.when(has_high)
    def _():
        to_low.wait_recv()

    @pl.when(has_low)
    def _():
        to_high.wait_recv()

    mirror_planes(rec, xlo, xhi, 0, gx, nx)
    faces(planes(xlo, rec, xhi), 0, flux_x)

    def finish(i, carry):
        change = []
        for h in range(2):
            k = 2 * i + h
            along_z = flux_z[k, pl.ds(1, 8)] - flux_z[k, pl.ds(0, 8)]
            along_y = flux_y[k, pl.ds(1, 8)] - flux_y[k, pl.ds(0, 8)]
            for j in range(8):
                turn_z[h, pl.ds(j, 8, stride=8), :] = along_z[j]
                turn_y[h, pl.ds(j, 8, stride=8), :] = along_y[j]
            change.append((flux_x[k, pl.ds(1, 8)] - flux_x[k, pl.ds(0, 8)]).reshape(ROWS, CZ))
        one = turn_z[0]
        two = turn_z[1]
        top = jnp.where(first_half, one, pltpu.roll(two, HALF, 1))
        bottom = jnp.where(first_half, pltpu.roll(one, HALF, 1), two)
        back = jnp.concatenate([top, bottom], axis=0).T
        for h in range(2):
            k = 2 * i + h
            whole = change[h] + turn_y[h] + back[ROWS * h : ROWS * h + ROWS]
            out_ref[k] = fields[k] - TIME_STEP * whole + CHEM_STEP * source[k]
        return carry

    lax.fori_loop(0, COMPS // 2, finish, 0)

    @pl.when(goes_up & jnp.logical_not(goes_early | goes_middle))
    def _():
        send_up()

    many = pl.ds(1, half - 1)
    if firsts:

        @pl.when(is_first)
        def _():
            for i in range(lasts):
                rows2[rank + half - last_at - i] = jnp.zeros((1, LANES), F32)
            some = pl.ds(1, half - 1 - lasts)
            pltpu.make_async_copy(rows2.at[some], rows2.at[some], s2_recv).wait()
            pltpu.make_async_copy(direct, direct, d_recv).wait()
            rows2[0] += jnp.sum(direct[...], axis=0)

        @pl.when(jnp.logical_not(is_first))
        def _():
            pltpu.make_async_copy(rows2.at[many], rows2.at[many], s2_recv).wait()

    elif half > 1:
        pltpu.make_async_copy(rows2.at[many], rows2.at[many], s2_recv).wait()
    total = jnp.sum(rows2[...], axis=0)
    wide = jnp.broadcast_to(total, (8, LANES))
    imp_ref[...] = pltpu.roll(wide, lax.rem(LANES - rank * mine, LANES), 1)
    if firsts:

        @pl.when(in_last)
        def _():
            some = pl.ds(1, half - 1 - firsts)
            pltpu.make_async_copy(rows2.at[some], rows2.at[some], s2_send).wait()

        @pl.when(jnp.logical_not(in_last))
        def _():
            pltpu.make_async_copy(rows2.at[many], rows2.at[many], s2_send).wait()

        @pl.when(is_wall & in_last)
        def _():
            every = pl.ds(0, 2 * group)

            def sent(i, carry):
                pltpu.make_async_copy(contrib.at[every], contrib.at[every], d_send).wait()
                return carry

            lax.fori_loop(0, firsts, sent, 0)

    elif half > 1:
        pltpu.make_async_copy(rows2.at[many], rows2.at[many], s2_send).wait()

    @pl.when(is_wall)
    def _():
        most = pl.ds(1, 2 * group - 1)
        pltpu.make_async_copy(contrib.at[most], contrib.at[most], s1_send).wait()

    for copy in sends[2:]:
        copy.wait_send()

    @pl.when(has_low)
    def _():
        to_low.wait_send()

    @pl.when(has_high)
    def _():
        to_high.wait_send()


def body(fields, reacting, panel_map, layer_one, layer_two, layer_three, layer_four):
    sizes = (lax.axis_size("gx"), lax.axis_size("gy"), lax.axis_size("gz"))
    nx, ny, nz = sizes
    any_spec = pl.BlockSpec(memory_space=pltpu.HBM)
    vmem_spec = pl.BlockSpec(memory_space=pltpu.VMEM)
    plane = (COMPS, ROWS, CZ)
    ghost = (COMPS, 24, CZ)
    state = (COMPS, 9, 8, CZ)
    dma = pltpu.SemaphoreType.DMA
    held = pltpu.with_memory_space_constraint
    new_fields, impulse = pl.pallas_call(
        functools.partial(kernel, sizes),
        out_shape=(
            pltpu.VMEM(plane, F32),
            pltpu.VMEM((8, LANES), F32),
        ),
        in_specs=[any_spec] * 7,
        out_specs=(vmem_spec, vmem_spec),
        scratch_shapes=[
            pltpu.VMEM(plane, F32),
            pltpu.VMEM((ROWS, CZ), jnp.int32),
            pltpu.VMEM((2, CX, CZ), jnp.int32),
            pltpu.VMEM((COMPS, H1), BF16),
            pltpu.VMEM((H2, H1), BF16),
            pltpu.VMEM((H3, H2), BF16),
            pltpu.VMEM((COMPS, H3), BF16),
            pltpu.VMEM(plane, F32),
            pltpu.VMEM(plane, F32),
            pltpu.VMEM((COMPS, HALF + 16, LANES), F32),
            pltpu.VMEM(ghost, F32),
            pltpu.VMEM(ghost, F32),
            pltpu.VMEM(ghost, F32),
            pltpu.VMEM(ghost, F32),
            pltpu.VMEM((COMPS, 8, LANES), F32),
            pltpu.VMEM((COMPS, 8, LANES), F32),
            pltpu.VMEM(state, F32),
            pltpu.VMEM(state, F32),
            pltpu.VMEM(state, F32),
            pltpu.VMEM(state, F32),
            pltpu.VMEM(state, F32),
            pltpu.VMEM((2, ROWS, CZ), F32),
            pltpu.VMEM((2, ROWS, CZ), F32),
            pltpu.VMEM((H1, CAP), BF16),
            pltpu.VMEM((H2, CAP), BF16),
            pltpu.VMEM(plane, F32),
            pltpu.VMEM((2 * ny * nz, 1, LANES), F32),
            pltpu.VMEM((nx // 2, 1, LANES), F32),
            pltpu.VMEM((4 * nz, 1, LANES), F32),
            pltpu.VMEM((max(nx // 8, 1) * 4 * nz, 1, LANES), F32),
            pltpu.VMEM((1, LANES), F32),
            dma((7,)),
            dma((6,)),
            dma((6,)),
            dma(()),
            dma(()),
            dma(()),
            dma(()),
            pltpu.SemaphoreType.REGULAR,
            pltpu.SemaphoreType.REGULAR,
            dma(()),
            dma(()),
        ],
        compiler_params=pltpu.CompilerParams(
            collective_id=0, has_side_effects=True, vmem_limit_bytes=48 * 2**20
        ),
    )(
        held(fields.reshape(plane), pltpu.HBM),
        held(reacting.reshape(ROWS, CZ), pltpu.HBM),
        held(panel_map, pltpu.HBM),
        held(layer_one.T, pltpu.HBM),
        held(layer_two, pltpu.HBM),
        held(layer_three, pltpu.HBM),
        held(layer_four, pltpu.HBM),
    )
    own_panels = 2 * nx * nz * (CZ // PATCH) // (nx * ny * nz)
    return new_fields.reshape(fields.shape), impulse[0, :own_panels]


def solution(mesh):
    return jax.shard_map(
        body,
        mesh=mesh,
        in_specs=(
            P(None, "gx", "gy", "gz"),
            P("gx", "gy", "gz"),
            P(None, "gx", "gz"),
            P(),
            P(),
            P(),
            P(),
        ),
        out_specs=(P(None, "gx", "gy", "gz"), P(("gx", "gy", "gz"))),
        check_vma=False,
    )
```
